32 devices in a mesh: grp: 4 (over x, core), tile: 8 (over z, y).
Axes of the slice: x: 2, y: 2, z: 4, core: 2. Of those that a mesh axis runs over, the one named last changes fastest.
Arguments:
- raw: bfloat16 [16, 256, 3840], P('grp', 'tile'), may hold values from 0.25 to 4
- scales: bfloat16 [16, 64, 120], P('grp', 'tile'), may hold values from 0.29882812 to 1.1953125
- flat: float32 [256, 3840], P(None, 'tile'), may hold values from 0.25 to 1.75
- spectrum: float32 [8, 2, 256, 512], P('tile'), may hold values from -5 to 5
- pupil: float32 [2, 64, 128], replicated, may hold values from -5 to 5
- patterns: int32 [16, 4], replicated, may hold values from 0 to 31, all different within a row
- led_row: int32 [32], replicated, may hold values from 0 to 192
- led_col: int32 [32], replicated, may hold values from 0 to 384
Outputs:
- new_spectrum: float32 [8, 2, 256, 512], P('tile')
- stitched: float32 [2, 256, 3840], P(None, None, 'tile')
The draws below stay inside these ranges and needn't reach their ends.
Inputs may be any that keep to these rules, and one draw needn't show every extreme that they name: `patterns`: each frame lights 4 different LEDs, and every LED is lit in some frame.
All inputs are finite; a program needn't handle non-finite values.
Results may differ from the reference program's by a relative error of at most 0.0003.
Values may be sent and summed in bfloat16 or wider, within the bound.
No kernel may reach another device: no remote copies, remote signals or barrier semaphores. Data moves between devices by JAX's collectives and lax.ppermute only.
A program may use at most 128 MiB of HBM per device.

```python
import math
import jax
import jax.numpy as jnp
from jax import lax

TH = 256
TW = 512
OV = 32
BR = 4
BC = 32
PR = 64
PC = 128
LEDS = 4
NLED = 32
TILES = 8
W = 3840
FRAMES = 16


def plant(entries, rng, least, high):
    extent = entries.shape
    spot = [jax.random.randint(jax.random.fold_in(rng, axis), (), 0, extent[axis]) for axis in range(len(extent))]
    entries = entries.at[tuple(spot)].set(least)
    longest = extent.index(max(extent))
    spot[longest] = (spot[longest] + 1) % extent[longest]
    return entries.at[tuple(spot)].set(high)


def shard_levels(rng, dims, split, least, top_value):
    def one(axis_at, shards_of):
        draws = jax.random.uniform(jax.random.fold_in(jax.random.fold_in(rng, 6), axis_at), (shards_of,), jnp.float32, least / len(split), top_value / len(split))
        return jnp.repeat(jnp.exp(draws), dims[axis_at] // shards_of).reshape((-1,) + (1,) * (len(dims) - axis_at - 1))

    loudness = one(*split[0])
    for cut in split[1:]:
        loudness = loudness * one(*cut)
    return loudness


def picks_of(own_key, rows, amount, top, lift):
    order = jax.random.permutation(jax.random.fold_in(own_key, 1), amount)
    pull = order
    for power in range(3):
        pull = pull * pull // amount
    pull = pull * lift // amount
    chance = jax.random.randint(jax.random.fold_in(own_key, 2), (rows, amount), 0, 4096) + pull
    holders = jax.random.permutation(jax.random.fold_in(own_key, 3), rows)[jnp.arange(amount) % rows]
    chance = jnp.where(jnp.arange(rows)[:, None] == holders[None, :], 1 << 14, chance)
    priority = chance * amount + jnp.arange(amount)
    return lax.top_k(priority.astype(jnp.int32), top)[1].astype(jnp.int32)


def gaussian(own_key, extent, scale, bound, shards=(), kind=jnp.bfloat16):
    drawn = scale * jax.random.normal(own_key, extent, jnp.float32)
    if shards:
        drawn = drawn * shard_levels(own_key, extent, shards, -0.22, 0.18)
    return jnp.clip(drawn, -bound, bound).astype(kind)


def setup_inputs(seed: int = 0) -> dict:
    key_of = jax.random.split(jax.random.key(seed), 9)
    return {
        "raw": jnp.clip(0.25 + 3.75 * jax.random.uniform(key_of[0], (FRAMES, TH, W), jnp.float32) ** shard_levels(key_of[0], (FRAMES, TH, W), ((0, 4), (1, 8)), -0.2, 0.2), 0.25, 4.0).astype(jnp.bfloat16),
        "scales": jnp.clip(jnp.exp(math.log(1.1953125) - 1.3862944 * jax.random.uniform(key_of[1], (FRAMES, TH // BR, W // BC), jnp.float32) ** shard_levels(key_of[1], (FRAMES, TH // BR, W // BC), ((0, 4), (1, 8)), -0.2, 0.2)), 0.29882812, 1.1953125).astype(jnp.bfloat16),
        "flat": jnp.clip(1.0 + 0.15 * jax.random.normal(key_of[2], (TH, W), jnp.float32), 0.25, 1.75),
        "spectrum": gaussian(key_of[3], (TILES, 2, TH, TW), 0.7, 5.0, ((0, 8),), jnp.float32),
        "pupil": gaussian(key_of[4], (2, PR, PC), 0.7, 5.0, (), jnp.float32),
        "patterns": picks_of(key_of[5], FRAMES, NLED, LEDS, 0),
        "led_row": plant(jax.random.randint(key_of[6], (NLED,), 0, TH - PR + 1), jax.random.fold_in(key_of[6], 1), 0, TH - PR).astype(jnp.int32),
        "led_col": plant(jax.random.randint(key_of[7], (NLED,), 0, TW - PC + 1), jax.random.fold_in(key_of[7], 1), 0, TW - PC).astype(jnp.int32),
    }


step_size = 0.02
highest = lax.Precision.HIGHEST

def wave_table(length, band):
    places = jnp.arange(length, dtype=jnp.int32)[:, None]
    freqs = jnp.arange(band, dtype=jnp.int32)[None, :] - band // 2
    turns = places * freqs % length
    angle = turns.astype(jnp.float32) * (2.0 * math.pi / length)
    factor = 1.0 / math.sqrt(band)
    return (jnp.cos(angle) * factor, jnp.sin(angle) * factor)

def complex_product(form, left_pair, right_pair):
    left_re, left_im = left_pair
    right_re, right_im = right_pair

    def einsum_pair(first, second):
        return jnp.einsum(form, first, second, precision=highest)
    return (einsum_pair(left_re, right_re) - einsum_pair(left_im, right_im), einsum_pair(left_re, right_im) + einsum_pair(left_im, right_re))

def remove_tilt(flattened):
    rows_n = flattened.shape[1]
    cols_n = flattened.shape[2]
    ycentre = jnp.arange(rows_n, dtype=jnp.float32) - (rows_n - 1) / 2.0
    xcentre = jnp.arange(cols_n, dtype=jnp.float32) - (cols_n - 1) / 2.0
    slope_y = lax.optimization_barrier(jnp.sum(flattened * ycentre[None, :, None], axis=(1, 2))) / (jnp.sum(ycentre * ycentre) * cols_n)
    slope_x = lax.optimization_barrier(jnp.sum(flattened * xcentre[None, None, :], axis=(1, 2))) / (jnp.sum(xcentre * xcentre) * rows_n)
    return flattened - slope_y[:, None, None] * ycentre[None, :, None] - slope_x[:, None, None] * xcentre[None, None, :]

def box_gradients(spectrum_tile, window, pupil, row_starts, col_starts, lit_count):
    band_rows = pupil.shape[1]
    band_cols = pupil.shape[2]
    height = window.shape[1]
    width = window.shape[2]
    frames_n = window.shape[0]
    anchor = jnp.zeros((), jnp.int32)

    def cut_box(row_top, col_left):
        return lax.dynamic_slice(spectrum_tile, (anchor, row_top, col_left), (2, band_rows, band_cols))
    boxes = jax.vmap(cut_box)(row_starts, col_starts)
    pupil_re = pupil[0]
    pupil_im = pupil[1]
    lit_re = pupil_re * boxes[:, 0] - pupil_im * boxes[:, 1]
    lit_im = pupil_re * boxes[:, 1] + pupil_im * boxes[:, 0]
    rows_re, rows_im = wave_table(height, band_rows)
    cols_re, cols_im = wave_table(width, band_cols)
    spread = complex_product('bup,xp->bux', (lit_re, lit_im), (cols_re, cols_im))
    field_re, field_im = complex_product('yu,bux->byx', (rows_re, rows_im), spread)
    field_re = field_re.reshape(frames_n, lit_count, height, width)
    field_im = field_im.reshape(frames_n, lit_count, height, width)
    estimate = lax.optimization_barrier(jnp.sum(field_re * field_re + field_im * field_im, axis=1))
    misfit = estimate - window
    weighted_re = (misfit[:, None] * field_re).reshape(frames_n * lit_count, height, width)
    weighted_im = (misfit[:, None] * field_im).reshape(frames_n * lit_count, height, width)
    back = complex_product('yu,byx->bux', (rows_re, -rows_im), (weighted_re, weighted_im))
    tile_re, tile_im = complex_product('bux,xp->bup', back, (cols_re, -cols_im))
    grad_re = pupil_re * tile_re + pupil_im * tile_im
    grad_im = pupil_re * tile_im - pupil_im * tile_re
    return jnp.stack([grad_re, grad_im], axis=1)

def place_boxes(grads, row_starts, col_starts, height, width):
    anchor = jnp.zeros((), jnp.int32)

    def add_box(number, total):
        corner = (anchor, row_starts[number], col_starts[number])
        current = lax.dynamic_slice(total, corner, grads.shape[1:])
        return lax.dynamic_update_slice(total, current + grads[number], corner)
    return lax.fori_loop(0, grads.shape[0], add_box, jnp.zeros((2, height, width), jnp.float32))

def object_tile(spectrum_tile):
    height = spectrum_tile.shape[1]
    width = spectrum_tile.shape[2]
    rows_re, rows_im = wave_table(height, height)
    cols_re, cols_im = wave_table(width, width)
    partial_field = complex_product('yu,uv->yv', (rows_re, rows_im), (spectrum_tile[0], spectrum_tile[1]))
    return jnp.stack(complex_product('yv,xv->yx', partial_field, (cols_re, cols_im)))

def blend_core(own, left_part, right_part, has_left, has_right, core):
    margin = left_part.shape[-1]
    correlation = 2 * margin
    positions = jnp.arange(margin, dtype=jnp.float32)
    left_own = (positions + margin + 0.5) / correlation
    left_other = (margin - positions - 0.5) / correlation
    right_own = (correlation - positions - 0.5) / correlation
    right_other = (positions + 0.5) / correlation
    middle = own[..., margin:margin + core]
    head = middle[..., :margin] * (left_own * has_left + (1.0 - has_left)) + left_part * (left_other * has_left)
    tail = middle[..., core - margin:] * (right_own * has_right + (1.0 - has_right)) + right_part * (right_other * has_right)
    return jnp.concatenate([head, middle[..., margin:core - margin], tail], axis=-1)

def reference(raw, scales, flat, spectrum, pupil, patterns, led_row, led_col):
    tiles_n = spectrum.shape[0]
    core = TW - OV
    margin = OV // 2
    anchor = jnp.zeros((), jnp.int32)

    def measure(tile_number):
        start = tile_number * core
        codes = lax.dynamic_slice(raw, (anchor, anchor, start), (FRAMES, TH, core)).astype(jnp.float32)
        factors = lax.dynamic_slice(scales, (anchor, anchor, tile_number * (core // BC)), (FRAMES, TH // BR, core // BC)).astype(jnp.float32)
        factors = jnp.repeat(jnp.repeat(factors, BR, axis=1), BC, axis=2)
        gains = lax.dynamic_slice(flat, (anchor, start), (TH, core))
        return remove_tilt(codes * factors * gains[None])
    measured = lax.map(measure, jnp.arange(tiles_n, dtype=jnp.int32))
    blank = jnp.zeros_like(measured[:1, :, :, :margin])
    from_left = jnp.concatenate([blank, measured[:-1, :, :, core - margin:]], axis=0)
    from_right = jnp.concatenate([measured[1:, :, :, :margin], blank], axis=0)
    windows = jnp.concatenate([from_left, measured, from_right], axis=-1)
    lit_ids = patterns.reshape(-1)
    row_starts = led_row[lit_ids].astype(jnp.int32)
    col_starts = led_col[lit_ids].astype(jnp.int32)

    def update(pieces):
        spectrum_tile, window = pieces
        grads = box_gradients(spectrum_tile, window, pupil, row_starts, col_starts, LEDS)
        total = place_boxes(grads, row_starts, col_starts, TH, TW)
        fresh = spectrum_tile - step_size * total
        return (fresh, object_tile(fresh))
    new_spectrum, objects = lax.map(update, (spectrum, windows))
    flags = jnp.arange(tiles_n, dtype=jnp.int32)
    has_left = (flags > 0).astype(jnp.float32)[:, None, None, None]
    has_right = (flags < tiles_n - 1).astype(jnp.float32)[:, None, None, None]
    empty_part = jnp.zeros_like(objects[:1, :, :, :margin])
    left_parts = jnp.concatenate([empty_part, objects[:-1, :, :, TW - margin:]], axis=0)
    right_parts = jnp.concatenate([objects[1:, :, :, :margin], empty_part], axis=0)
    cores = blend_core(objects, left_parts, right_parts, has_left, has_right, core)
    stitched = jnp.transpose(cores, (1, 2, 0, 3)).reshape(2, TH, tiles_n * core)
    return (new_spectrum, stitched)
```

```python
import functools
import math

import jax
import jax.numpy as jnp
import ml_dtypes
import numpy as np
from jax import lax
from jax.experimental import pallas as pl
from jax.experimental.pallas import tpu as pltpu
from jax.sharding import PartitionSpec as P

OV = 32
BC = 32
STEP = 0.02
F32 = jnp.float32
BF16 = jnp.bfloat16
VMEM = pltpu.VMEM
SMEM = pltpu.SMEM
MIB = 1 << 20


def two_parts(table):
    table = np.asarray(table, np.float64)
    high = table.astype(ml_dtypes.bfloat16)
    low = (table - high.astype(np.float64)).astype(ml_dtypes.bfloat16)
    return high, low


def wave(places, freqs, length, norm):
    turns = np.outer(places, freqs) % length
    angle = turns * (2.0 * math.pi / length)
    return np.cos(angle) / math.sqrt(norm), np.sin(angle) / math.sqrt(norm)


def low_pass(length, band):
    places = 2 * np.arange(length // 2)[:, None] - np.arange(length)[None, :]
    total = np.ones(places.shape)
    for freq in range(1, band):
        total += 2.0 * np.cos(2.0 * math.pi * ((freq * places) % length) / length)
    return total / length


def stacked_tables(height, width, band_rows, band_cols):
    row_re, row_im = wave(
        2 * np.arange(height // 2), np.arange(band_rows) - band_rows // 2, height, band_rows
    )
    rows = np.block([[row_re, -row_im], [row_im, row_re]])
    col_re, col_im = wave(
        np.arange(band_cols) - band_cols // 2, 2 * np.arange(width // 2), width, band_cols
    )
    cols = np.block([[col_re, col_im], [-col_im, col_re]])
    return rows, cols


def split(values):
    high = values.astype(BF16)
    return high, (values - high.astype(F32)).astype(BF16)


def mm(left, right):
    return jnp.dot(left, right, preferred_element_type=F32)


def vmem_spec(count):
    return [pl.BlockSpec(memory_space=VMEM)] * count


def dequant_kernel(raw_ref, scales_ref, out_ref, *, rows_here, core, margin):
    lines, strip = raw_ref.shape
    coarse_rows, coarse_cols = scales_ref.shape
    tiles, _, width = out_ref.shape
    ratio = lines // coarse_rows
    row = lax.broadcasted_iota(jnp.int32, (lines, coarse_rows), 0)
    pick = lax.broadcasted_iota(jnp.int32, (lines, coarse_rows), 1)
    spread_rows = (row // ratio == pick).astype(F32).astype(BF16)
    factors = mm(spread_rows, scales_ref[...]).astype(BF16)
    block = lax.broadcasted_iota(jnp.int32, (coarse_cols, width), 0)
    place = lax.broadcasted_iota(jnp.int32, (coarse_cols, width), 1)
    for tile in range(tiles):
        start = tile * core - margin
        column = place + start
        inside = (column >= block * BC) & (column < (block + 1) * BC)
        scale = mm(factors, inside.astype(F32).astype(BF16))
        base = max(start, 0) // 128 * 128
        span = min(width + 128, strip - base)
        codes = raw_ref[:, base : base + span].astype(F32)
        turn = (base - start) % span
        if turn:
            codes = pltpu.roll(codes, turn, 1)
        out_ref[tile] = (codes[:, :width] * scale).astype(BF16)


def dequantize(raw, scales, tiles, core, margin, width):
    frames, rows_here, strip = raw.shape
    return pl.pallas_call(
        functools.partial(dequant_kernel, rows_here=rows_here, core=core, margin=margin),
        out_shape=jax.ShapeDtypeStruct((tiles, frames * rows_here, width), BF16),
        in_specs=vmem_spec(2),
        out_specs=pl.BlockSpec(memory_space=VMEM),
        compiler_params=pltpu.CompilerParams(vmem_limit_bytes=40 * MIB),
        name="dequantize",
    )(raw.reshape(frames * rows_here, strip), scales.reshape(-1, scales.shape[-1]))


def box_area(top, left, band_rows, band_cols):
    row = top // 8 * 8
    col = left // 128 * 128
    area = (
        pl.ds(pl.multiple_of(row, 8), band_rows + 8),
        pl.ds(pl.multiple_of(col, 128), band_cols + 128),
    )
    return area, top - row, left - col


def field_kernel(
    led_row, led_col, patterns, spec_ref, pupil_ref, cols_hi, cols_lo, rows_hi, rows_lo,
    field_ref, estimate_ref, wide, bright,
):
    step = pl.program_id(0)
    group = field_ref.shape[0]
    band_rows, band_cols = pupil_ref.shape[1:]
    width = spec_ref.shape[2]
    half_h = field_ref.shape[1] // 2
    half_w = field_ref.shape[2]

    @pl.when(step == 0)
    def _():
        wide[...] = jnp.zeros_like(wide)
        wide[:, : spec_ref.shape[1], :width] = spec_ref[...]

    boxes = []
    for place in range(group):
        led = step * group + place
        top = led_row[led]
        left = led_col[led]
        area, down, right = box_area(top, left, band_rows, band_cols)
        parts = []
        for part in range(2):
            strip = pltpu.roll(wide[(part, *area)], lax.rem(2 * band_cols - right, 2 * band_cols), 1)
            strip = pltpu.roll(strip[:, :band_cols], lax.rem(band_rows + 8 - down, band_rows + 8), 0)
            parts.append(strip[:band_rows])
        lit_re = pupil_ref[0] * parts[0] - pupil_ref[1] * parts[1]
        lit_im = pupil_ref[0] * parts[1] + pupil_ref[1] * parts[0]
        boxes.append(jnp.concatenate([lit_re, lit_im], axis=1))
    high, low = split(jnp.concatenate(boxes, axis=0))
    spread = mm(high, cols_hi[...]) + mm(high, cols_lo[...]) + mm(low, cols_hi[...])
    left_rows = jnp.concatenate([rows_hi[...], rows_hi[...], rows_lo[...]], axis=1)
    for place in range(group):
        one = spread[place * band_rows : (place + 1) * band_rows]
        high, low = split(jnp.concatenate([one[:, :half_w], one[:, half_w:]], axis=0))
        field = mm(left_rows, jnp.concatenate([high, low, high], axis=0))
        field_ref[place] = field
        bright[step * group + place] = field[:half_h] ** 2 + field[half_h:] ** 2

    @pl.when(step == pl.num_programs(0) - 1)
    def _():
        def one_frame(frame, carry):
            total = bright[patterns[frame, 0]]
            for lit in range(1, patterns.shape[1]):
                total += bright[patterns[frame, lit]]
            estimate_ref[frame] = total
            return carry

        lax.fori_loop(0, patterns.shape[0], one_frame, 0)


def all_fields(spectrum, pupil, patterns, led_row, led_col, tables, group=4):
    rows, cols = tables
    leds = led_row.shape[0]
    _, height, width = spectrum.shape
    half_h, half_w = height // 2, width // 2
    whole = lambda shape: pl.BlockSpec(shape, lambda i: (0,) * len(shape))
    scalar = pl.BlockSpec(memory_space=SMEM)
    constants = [*two_parts(cols), *two_parts(rows)]
    return pl.pallas_call(
        field_kernel,
        grid=(leds // group,),
        out_shape=(
            jax.ShapeDtypeStruct((leds, 2 * half_h, half_w), F32),
            jax.ShapeDtypeStruct((patterns.shape[0], half_h, half_w), F32),
        ),
        in_specs=[scalar] * 3
        + [whole(spectrum.shape), whole(pupil.shape)]
        + [whole(c.shape) for c in constants],
        out_specs=(
            pl.BlockSpec((group, 2 * half_h, half_w), lambda i: (i, 0, 0)),
            whole((patterns.shape[0], half_h, half_w)),
        ),
        scratch_shapes=[
            pltpu.VMEM((2, height + 8, width + 128), F32),
            pltpu.VMEM((leds, half_h, half_w), F32),
        ],
        compiler_params=pltpu.CompilerParams(vmem_limit_bytes=40 * MIB),
        cost_estimate=pl.CostEstimate(
            flops=8_000_000_000, bytes_accessed=16_000_000, transcendentals=0
        ),
        name="fields",
    )(led_row, led_col, patterns, spectrum, pupil, *constants)


def window_kernel(
    dq_ref, flat_ref, part_a, part_b, odd, lc_hi, lc_lo, lr_hi, lr_lo, shapes_ref,
    window_ref, slopes_ref, *, margin, core,
):
    slabs, lines, width = dq_ref.shape
    frames, half_h, half_w = window_ref.shape
    rows_here = lines // frames
    height = slabs * rows_here
    is_odd = odd[0] == 1
    first, second = part_a[...], part_b[...]
    from_left = jnp.where(is_odd, first, second)
    from_right = jnp.where(is_odd, second, first)
    gains = jnp.concatenate([from_left, flat_ref[...], from_right], axis=1)
    yc = lax.broadcasted_iota(jnp.int32, (height, 1), 0).astype(F32) - (height - 1) / 2.0
    place = lax.broadcasted_iota(jnp.int32, (1, width), 1)
    in_core = ((place >= margin) & (place < margin + core)).astype(F32)
    xc = (place.astype(F32) - margin - (core - 1) / 2.0) * in_core
    over_y = 1.0 / (core * (height * (height * height - 1) / 12.0))
    over_x = 1.0 / (height * (core * (core * core - 1) / 12.0))
    values = [dq_ref[slab].astype(F32) for slab in range(slabs)]
    lane = lax.broadcasted_iota(jnp.int32, (1, 128), 1)
    flats = []
    for frame in range(frames):
        cut = slice(frame * rows_here, (frame + 1) * rows_here)
        flats.append(jnp.concatenate([v[cut] for v in values], axis=0) * gains)
    flattened = jnp.concatenate(flats, axis=0)
    high, low = split(flattened)
    narrow = mm(high, lc_hi[...]) + mm(high, lc_lo[...]) + mm(low, lc_hi[...])
    left_rows = jnp.concatenate([lr_hi[...], lr_hi[...], lr_lo[...]], axis=1)
    slopes_ref[...] = jnp.zeros_like(slopes_ref)
    for frame in range(frames):
        cut = slice(frame * height, (frame + 1) * height)
        slope_y = jnp.sum(jnp.sum(flats[frame] * yc, axis=0, keepdims=True) * in_core) * over_y
        slope_x = jnp.sum(jnp.sum(flats[frame], axis=0, keepdims=True) * xc) * over_x
        high, low = split(narrow[cut])
        window = mm(left_rows, jnp.concatenate([high, low, high], axis=0))
        window = window - shapes_ref[0] * slope_y - shapes_ref[1] * slope_x
        mean = jnp.sum(window) * (1.0 / (half_h * half_w))
        window_ref[frame] = (window - mean).astype(BF16)
        slopes_ref[frame : frame + 1] = jnp.where(
            lane == 0, slope_y, jnp.where(lane == 1, slope_x, jnp.where(lane == 2, mean, 0.0))
        )


def tilt_shapes(height, width, margin, core, lr, lc):
    rows_y = lr @ (np.arange(height) - (height - 1) / 2.0)
    local = np.arange(width) - margin
    shapes = []
    for begin, end, shift in ((0, core, 0), (-margin, 0, core), (core, core + margin, -core)):
        on = (local >= begin) & (local < end)
        xc = (local + shift - (core - 1) / 2.0) * on
        flat_line = on.astype(np.float64) @ lc
        xc_line = xc @ lc
        shapes.append(np.outer(rows_y, flat_line))
        shapes.append(np.outer(np.ones(len(rows_y)), xc_line))
    return np.stack(shapes).astype(np.float32)


def windows(arrived, flat, part_a, part_b, odd, frames, passes, shapes, margin, core):
    lr, lc = passes
    constants = [*two_parts(lc), *two_parts(lr)]
    half_h, half_w = lr.shape[0], lc.shape[1]
    return pl.pallas_call(
        functools.partial(window_kernel, margin=margin, core=core),
        out_shape=(
            jax.ShapeDtypeStruct((frames, half_h, half_w), BF16),
            jax.ShapeDtypeStruct((8, 128), F32),
        ),
        in_specs=vmem_spec(4) + [pl.BlockSpec(memory_space=SMEM)] + vmem_spec(5),
        out_specs=tuple(vmem_spec(2)),
        compiler_params=pltpu.CompilerParams(vmem_limit_bytes=40 * MIB),
        name="windows",
    )(arrived, flat, part_a, part_b, odd, *constants, shapes[:2])


def update_kernel(
    led_row, led_col, patterns, where, field_ref, estimate_ref, w0, w1, w2, w3,
    s0, s1, s2, s3, spec_ref, pupil_ref, shapes_ref, rt_hi, rt_lo, ct_hi, ct_lo,
    fr_hi, fr_lo, fc_hi, fc_lo,
    fresh_ref, high_ref, low_ref, first_ref, second_ref, misfit, weight, grads,
):
    step = pl.program_id(0)
    group = field_ref.shape[0]
    band_rows, band_cols = pupil_ref.shape[1:]
    height, width = spec_ref.shape[1:]
    half_h, half_w = misfit.shape[1:]
    frames_here = w0.shape[0]
    my_group = where[0]
    is_odd = where[1] == 1

    @pl.when(step == 0)
    def _():
        grads[...] = jnp.zeros_like(grads)
        weight[...] = jnp.zeros_like(weight)
        for slot, (window, slopes) in enumerate(((w0, s0), (w1, s1), (w2, s2), (w3, s3))):
            owner = jnp.bitwise_xor(my_group, slot)
            for place in range(frames_here):
                frame = owner * frames_here + place
                own = slopes[place : place + 1]
                first = slopes[8 + place : 9 + place]
                second = slopes[16 + place : 17 + place]
                left = jnp.where(is_odd, first, second)
                right = jnp.where(is_odd, second, first)
                value = estimate_ref[frame] - window[place].astype(F32) - own[:, 2:3]
                value += shapes_ref[0] * left[:, 0:1] + shapes_ref[1] * left[:, 1:2]
                value += shapes_ref[2] * right[:, 0:1] + shapes_ref[3] * right[:, 1:2]
                for lit in range(patterns.shape[1]):
                    weight[patterns[frame, lit]] += value

    left_rows = jnp.concatenate([rt_hi[...], rt_lo[...]], axis=0)
    backs = []
    for place in range(group):
        q = weight[step * group + place]
        field = field_ref[place]
        high, low = split(jnp.concatenate([field[:half_h] * q, field[half_h:] * q], axis=0))
        both = mm(left_rows, high)
        back = both[: 2 * band_rows] + both[2 * band_rows :] + mm(rt_hi[...], low)
        backs.append(jnp.concatenate([back[:band_rows], back[band_rows:]], axis=1))
    high, low = split(jnp.concatenate(backs, axis=0))
    boxes = mm(high, ct_hi[...]) + mm(high, ct_lo[...]) + mm(low, ct_hi[...])
    for place in range(group):
        led = step * group + place
        one = boxes[place * band_rows : (place + 1) * band_rows]
        back_re, back_im = one[:, :band_cols], one[:, band_cols:]
        parts = (
            pupil_ref[0] * back_re + pupil_ref[1] * back_im,
            pupil_ref[0] * back_im - pupil_ref[1] * back_re,
        )
        top = led_row[led]
        left = led_col[led]
        area, down, right = box_area(top, left, band_rows, band_cols)
        for part in range(2):
            filled = jnp.concatenate([parts[part], jnp.zeros((8, band_cols), F32)], axis=0)
            filled = pltpu.roll(filled, down, 0)
            filled = jnp.concatenate([filled, jnp.zeros((band_rows + 8, 128), F32)], axis=1)
            grads[(part, *area)] += pltpu.roll(filled, right, 1)

    @pl.when(step == pl.num_programs(0) - 1)
    def _():
        fresh_re = spec_ref[0] - (4.0 * STEP) * grads[0, :height, :width]
        fresh_im = spec_ref[1] - (4.0 * STEP) * grads[1, :height, :width]
        fresh_ref[0] = fresh_re
        fresh_ref[1] = fresh_im
        re_hi, re_lo = split(fresh_re)
        im_hi, im_lo = split(fresh_im)
        high = jnp.concatenate([re_hi, im_hi], axis=0)
        low = jnp.concatenate([re_lo, im_lo], axis=0)
        spread = mm(fr_hi[...], high) + mm(fr_lo[...], high) + mm(fr_hi[...], low)
        high, low = split(jnp.concatenate([spread[:height], spread[height:]], axis=1))
        high_ref[...] = high
        low_ref[...] = low
        contract = functools.partial(
            lax.dot_general,
            dimension_numbers=(((1,), (1,)), ((), ())),
            preferred_element_type=F32,
        )
        sides = (
            contract(fc_hi[...], high) + contract(fc_lo[...], high) + contract(fc_hi[...], low)
        )
        half = sides.shape[0] // 2
        to_left, to_right = sides[:half], sides[half:]
        first_ref[...] = jnp.where(is_odd, to_left, to_right)
        second_ref[...] = jnp.where(is_odd, to_right, to_left)


def update(
    field, estimate, window_parts, slope_parts, spectrum, pupil, patterns, led_row, led_col,
    where, tables, shapes, margin, group=4,
):
    rows, cols = tables
    leds = led_row.shape[0]
    _, height, width = spectrum.shape
    half_h, half_w = height // 2, width // 2
    fr_re, fr_im = wave(np.arange(height), np.arange(height) - height // 2, height, height)
    full_rows = np.block([[fr_re, -fr_im], [fr_im, fr_re]])
    side_places = np.concatenate([np.arange(margin), width - margin + np.arange(margin)])
    fc_re, fc_im = wave(side_places, np.arange(width) - width // 2, width, width)
    sides = np.concatenate(
        [
            np.concatenate([fc_re[:margin], -fc_im[:margin]], axis=1),
            np.concatenate([fc_im[:margin], fc_re[:margin]], axis=1),
            np.concatenate([fc_re[margin:], -fc_im[margin:]], axis=1),
            np.concatenate([fc_im[margin:], fc_re[margin:]], axis=1),
        ]
    )
    constants = [
        shapes[2:],
        *two_parts(rows.T),
        *two_parts(cols.T),
        *two_parts(full_rows),
        *two_parts(sides),
    ]
    whole = lambda shape: pl.BlockSpec(shape, lambda i: (0,) * len(shape))
    scalar = pl.BlockSpec(memory_space=SMEM)
    operands = [estimate, *window_parts, *slope_parts, spectrum, pupil, *constants]
    out_shape = (
        jax.ShapeDtypeStruct(spectrum.shape, F32),
        jax.ShapeDtypeStruct((height, 2 * width), BF16),
        jax.ShapeDtypeStruct((height, 2 * width), BF16),
        jax.ShapeDtypeStruct((2 * margin, height), F32),
        jax.ShapeDtypeStruct((2 * margin, height), F32),
    )
    return pl.pallas_call(
        update_kernel,
        grid=(leds // group,),
        out_shape=out_shape,
        in_specs=[scalar] * 4
        + [pl.BlockSpec((group, 2 * half_h, half_w), lambda i: (i, 0, 0))]
        + [whole(o.shape) for o in operands],
        out_specs=tuple(whole(o.shape) for o in out_shape),
        scratch_shapes=[
            pltpu.VMEM((8, half_h, half_w), F32),
            pltpu.VMEM((leds, half_h, half_w), F32),
            pltpu.VMEM((2, height + 8, width + 128), F32),
        ],
        compiler_params=pltpu.CompilerParams(vmem_limit_bytes=48 * MIB),
        name="update",
    )(led_row, led_col, patterns, where, field, *operands)


def object_kernel(high_ref, low_ref, re_hi, re_lo, im_hi, im_lo, out_ref):
    width = re_hi.shape[0]
    core = out_ref.shape[2]
    zre_hi, zim_hi = high_ref[:, :width], high_ref[:, width:]
    zre_lo, zim_lo = low_ref[:, :width], low_ref[:, width:]
    z_re = jnp.concatenate([zre_hi, zre_hi, zre_lo], axis=1)
    z_im = jnp.concatenate([zim_hi, zim_hi, zim_lo], axis=1)
    c_re = jnp.concatenate([re_hi[...], re_lo[...], re_hi[...]], axis=0)
    c_im = jnp.concatenate([im_hi[...], im_lo[...], im_hi[...]], axis=0)
    out_ref[0] = (mm(z_re, c_re) - mm(z_im, c_im))[:, :core]
    out_ref[1] = (mm(z_re, c_im) + mm(z_im, c_re))[:, :core]


def object_core(high, low, margin, core):
    height, width = high.shape[0], high.shape[1] // 2
    places = (margin + np.arange(width)) % width
    col_re, col_im = wave(np.arange(width) - width // 2, places, width, width)
    constants = [*two_parts(col_re), *two_parts(col_im)]
    return pl.pallas_call(
        object_kernel,
        out_shape=jax.ShapeDtypeStruct((2, height, core), F32),
        in_specs=vmem_spec(6),
        out_specs=pl.BlockSpec(memory_space=VMEM),
        compiler_params=pltpu.CompilerParams(vmem_limit_bytes=40 * MIB),
        cost_estimate=pl.CostEstimate(
            flops=3_000_000_000, bytes_accessed=5_000_000, transcendentals=0
        ),
        name="object",
    )(high, low, *constants)


def blend_kernel(where, first_ref, second_ref, in_ref, out_ref, *, margin, last):
    side = pl.program_id(0)
    tile = where[2]
    is_odd = where[1] == 1
    height = out_ref.shape[1]
    lanes = out_ref.shape[2]
    lane = lax.broadcasted_iota(jnp.int32, (1, lanes), 1).astype(F32)
    span = 2.0 * margin

    def other_of(incoming):
        wide = jnp.concatenate([incoming, jnp.zeros((lanes - margin, height), F32)], axis=0)
        return jnp.transpose(wide, (1, 0))

    @pl.when(side == 0)
    def _():
        on = (lane < margin) & (tile > 0)
        own_w = jnp.where(on, (lane + margin + 0.5) / span, 1.0)
        other_w = jnp.where(on, (margin - lane - 0.5) / span, 0.0)
        incoming = jnp.where(is_odd, first_ref[...], second_ref[...])
        for part in range(2):
            other = other_of(incoming[part * margin : (part + 1) * margin])
            out_ref[part] = in_ref[part] * own_w + other * other_w

    @pl.when(side == 1)
    def _():
        q = lane - last
        on = (q >= 0.0) & (q < margin) & (tile < where[3] - 1)
        own_w = jnp.where(on, (span - q - 0.5) / span, 1.0)
        other_w = jnp.where(on, (q + 0.5) / span, 0.0)
        incoming = jnp.where(is_odd, second_ref[...], first_ref[...])
        for part in range(2):
            other = other_of(incoming[part * margin : (part + 1) * margin])
            out_ref[part] = in_ref[part] * own_w + pltpu.roll(other, last, 1) * other_w


def blend(core_part, first, second, where, margin):
    _, height, core = core_part.shape
    lanes = 128
    steps = pl.cdiv(core, lanes) - 1
    last = core - margin - steps * lanes
    block = pl.BlockSpec((2, height, lanes), lambda i: (0, 0, i * steps))
    whole = pl.BlockSpec(first.shape, lambda i: (0, 0))
    return pl.pallas_call(
        functools.partial(blend_kernel, margin=margin, last=last),
        grid=(2,),
        out_shape=jax.ShapeDtypeStruct(core_part.shape, F32),
        in_specs=[pl.BlockSpec(memory_space=SMEM), whole, whole, block],
        out_specs=block,
        input_output_aliases={3: 0},
        name="blend",
    )(where, first, second, core_part)


def body(raw, scales, flat, spectrum, pupil, patterns, led_row, led_col):
    height, core = flat.shape
    margin = OV // 2
    width = core + OV
    tiles = lax.axis_size("tile")
    tile = lax.axis_index("tile")
    grp = lax.axis_index("grp")
    frames_here = raw.shape[0]
    band_rows, band_cols = pupil.shape[1:]
    spectrum_tile = spectrum[0]
    odd = lax.rem(tile, 2)
    where = jnp.stack([grp, odd, tile, jnp.int32(tiles)]).astype(jnp.int32)

    swap_a = [(i, i ^ 1) for i in range(tiles)]
    swap_b = [(i, ((i + 1) ^ 1) - 1) for i in range(1, tiles - 1)]

    def neighbours(for_a, for_b):
        return lax.ppermute(for_a, "tile", swap_a), lax.ppermute(for_b, "tile", swap_b)

    tables = stacked_tables(height, width, band_rows, band_cols)
    passes = (low_pass(height, band_rows), low_pass(width, band_cols).T)
    shapes = tilt_shapes(height, width, margin, core, *passes)

    codes = dequantize(raw, scales, tiles, core, margin, width)
    arrived = lax.all_to_all(codes, "tile", split_axis=0, concat_axis=0, tiled=True)
    flat_left, flat_right = flat[:, :margin], flat[:, core - margin :]
    is_odd = odd == 1
    flat_a, flat_b = neighbours(
        jnp.where(is_odd, flat_left, flat_right), jnp.where(is_odd, flat_right, flat_left)
    )
    field, estimate = all_fields(spectrum_tile, pupil, patterns, led_row, led_col, tables)
    window, slopes = windows(
        arrived, flat, flat_a, flat_b, where[1:2], frames_here, passes, shapes, margin, core
    )

    swap_core = [(i, i ^ 1) for i in range(4)]
    swap_chip = [(i, i ^ 2) for i in range(4)]
    other = functools.partial(lax.ppermute, axis_name="grp")
    window_2 = other(window, perm=swap_chip)
    window_1 = other(window, perm=swap_core)
    window_3 = other(window_2, perm=swap_core)
    slopes_a, slopes_b = neighbours(slopes, slopes)
    slopes_0 = jnp.concatenate([slopes, slopes_a, slopes_b], axis=0)
    slopes_2 = other(slopes_0, perm=swap_chip)
    slopes_1 = other(slopes_0, perm=swap_core)
    slopes_3 = other(slopes_2, perm=swap_core)

    fresh, high, low, for_a, for_b = update(
        field, estimate, (window, window_1, window_2, window_3),
        (slopes_0, slopes_1, slopes_2, slopes_3), spectrum_tile, pupil, patterns,
        led_row, led_col, where, tables, shapes, margin,
    )
    side_a, side_b = neighbours(for_a, for_b)
    core_part = object_core(high, low, margin, core)
    stitched = blend(core_part, side_a, side_b, where, margin)
    return fresh[None], stitched


def solution(mesh):
    return jax.shard_map(
        body,
        mesh=mesh,
        in_specs=(
            P("grp", "tile", None),
            P("grp", "tile", None),
            P(None, "tile"),
            P("tile", None, None, None),
            P(),
            P(),
            P(),
            P(),
        ),
        out_specs=(P("tile", None, None, None), P(None, None, "tile")),
        check_vma=False,
    )
```

```python
import functools
import math

import jax
import jax.numpy as jnp
import ml_dtypes
import numpy as np
from jax import lax
from jax.experimental import pallas as pl
from jax.experimental.pallas import tpu as pltpu
from jax.sharding import PartitionSpec as P

OV = 32
BC = 32
STEP = 0.02
F32 = jnp.float32
BF16 = jnp.bfloat16
VMEM = pltpu.VMEM
SMEM = pltpu.SMEM
LIMIT = 58 << 20


def two_parts(table):
    table = np.asarray(table, np.float64)
    high = table.astype(ml_dtypes.bfloat16)
    low = (table - high.astype(np.float64)).astype(ml_dtypes.bfloat16)
    return high, low


def wave(places, freqs, length, norm):
    turns = np.outer(places, freqs) % length
    angle = turns * (2.0 * math.pi / length)
    return np.cos(angle) / math.sqrt(norm), np.sin(angle) / math.sqrt(norm)


def low_pass(length, band):
    places = 2 * np.arange(length // 2)[:, None] - np.arange(length)[None, :]
    total = np.ones(places.shape)
    for freq in range(1, band):
        total += 2.0 * np.cos(2.0 * math.pi * ((freq * places) % length) / length)
    return total / length


def stacked_tables(height, width, band_rows, band_cols):
    row_re, row_im = wave(
        2 * np.arange(height // 2), np.arange(band_rows) - band_rows // 2, height, band_rows
    )
    rows = np.block([[row_re, -row_im], [row_im, row_re]])
    col_re, col_im = wave(
        np.arange(band_cols) - band_cols // 2, 2 * np.arange(width // 2), width, band_cols
    )
    cols = np.block([[col_re, col_im], [-col_im, col_re]])
    return rows, cols


def split(values):
    high = values.astype(BF16)
    return high, (values - high.astype(F32)).astype(BF16)


def mm(left, right):
    return jnp.dot(left, right, preferred_element_type=F32)


def vmem_spec(count):
    return [pl.BlockSpec(memory_space=VMEM)] * count


def parts_rows(values, columns):
    high = values.astype(BF16).astype(F32)
    rest = values - high
    middle = rest.astype(BF16).astype(F32)
    last = rest - middle
    top = jnp.concatenate([high, middle], axis=1)
    bottom = jnp.concatenate([last, jnp.zeros_like(last)], axis=1)
    rows = jnp.concatenate([top, bottom], axis=0)
    if columns > 256:
        rows = jnp.concatenate([rows, jnp.zeros((16, columns - 256), F32)], axis=1)
    return rows.astype(BF16)


def rows_value(rows):
    rows = rows.astype(F32)
    return rows[:8, :128] + rows[:8, 128:256] + rows[8:, :128]


def strips_kernel(
    where, raw_ref, scales_ref, gains_ref, lc_hi, lc_lo, out_ref, *, frames, core, margin
):
    lines, strip = raw_ref.shape
    coarse_rows, coarse_cols = scales_ref.shape
    tiles = out_ref.shape[0]
    width, half_w = lc_hi.shape
    rows_here = lines // frames
    ratio = lines // coarse_rows
    row = lax.broadcasted_iota(jnp.int32, (lines, coarse_rows), 0)
    pick = lax.broadcasted_iota(jnp.int32, (lines, coarse_rows), 1)
    spread_rows = (row // ratio == pick).astype(F32).astype(BF16)
    factors = mm(spread_rows, scales_ref[...]).astype(BF16)
    block = lax.broadcasted_iota(jnp.int32, (coarse_cols, width), 0)
    place = lax.broadcasted_iota(jnp.int32, (coarse_cols, width), 1)
    line = lax.broadcasted_iota(jnp.int32, (1, width), 1)
    in_core = ((line >= margin) & (line < margin + core)).astype(F32)
    xc = (line.astype(F32) - margin - (core - 1) / 2.0) * in_core
    first_row = (where[2] * rows_here).astype(F32)
    height = rows_here * tiles
    yc = lax.broadcasted_iota(jnp.int32, (rows_here, 1), 0).astype(F32)
    yc = yc + (first_row - (height - 1) / 2.0)
    lane = lax.broadcasted_iota(jnp.int32, (8, 128), 1)
    narrow_lane = lax.broadcasted_iota(jnp.int32, (1, 128), 1)
    own, means = [], []
    for tile in range(tiles):
        start = tile * core - margin
        column = place + start
        inside = (column >= block * BC) & (column < (block + 1) * BC)
        scale = mm(factors, inside.astype(F32).astype(BF16))
        base = max(start, 0) // 128 * 128
        span = min(width + 128, strip - base)
        codes = raw_ref[:, base : base + span].astype(F32)
        turn = (base - start) % span
        if turn:
            codes = pltpu.roll(codes, turn, 1)
        gains = pltpu.roll(gains_ref[tile].astype(F32), margin, 1)
        if tile > 0:
            end = gains_ref[tile - 1][:, width - 128 :].astype(F32)
            end = pltpu.roll(end, (2 * margin) + margin, 1)
            end = jnp.where(narrow_lane < margin, end, 0.0)
            gains = jnp.concatenate([gains[:, :128] + end, gains[:, 128:]], axis=1)
        if tile < tiles - 1:
            end = gains_ref[tile + 1][:, :128].astype(F32)
            end = pltpu.roll(end, 128 - margin, 1)
            end = jnp.where(narrow_lane >= 128 - margin, end, 0.0)
            gains = jnp.concatenate(
                [gains[:, : width - 128], gains[:, width - 128 :] + end], axis=1
            )
        gains = jnp.concatenate([gains + 1.0] * frames, axis=0)
        flattened = codes[:, :width] * scale * gains
        high, low = split(flattened)
        narrow = mm(high, lc_hi[...]) + mm(high, lc_lo[...]) + mm(low, lc_hi[...])
        sums, lines_y, flat_means, centred = [], [], [], []
        for frame in range(frames):
            cut = slice(frame * rows_here, (frame + 1) * rows_here)
            sums.append(jnp.sum(flattened[cut], axis=0, keepdims=True))
            lines_y.append(jnp.sum(flattened[cut] * yc, axis=0, keepdims=True))
            mean = jnp.sum(narrow[cut]) * (1.0 / (rows_here * half_w))
            flat_means.append(jnp.full((1, 1), mean, F32))
            centred.append(narrow[cut] - mean)
        out_ref[tile, :lines] = jnp.concatenate(centred, axis=0).astype(BF16)
        blank = [jnp.zeros((8 - frames, width), F32)]
        slope_y = jnp.sum(jnp.concatenate(lines_y + blank, axis=0) * in_core, axis=1, keepdims=True)
        slope_x = jnp.sum(jnp.concatenate(sums + blank, axis=0) * xc, axis=1, keepdims=True)
        own.append(jnp.where(lane == 0, slope_y, jnp.where(lane == 1, slope_x, 0.0)))
        mean = jnp.concatenate(flat_means + [jnp.zeros((8 - frames, 1), F32)], axis=0)
        means.append(jnp.where(lane == 6, mean, 0.0))
    for tile in range(tiles):
        packed = own[tile] + means[tile]
        if tile > 0:
            packed += pltpu.roll(own[tile - 1], 2, 1)
        if tile < tiles - 1:
            packed += pltpu.roll(own[tile + 1], 4, 1)
        out_ref[tile, lines:] = parts_rows(packed, half_w)


def strips(raw, scales, gains, where, lc, tiles, core, margin):
    frames, rows_here, strip = raw.shape
    return pl.pallas_call(
        functools.partial(strips_kernel, frames=frames, core=core, margin=margin),
        out_shape=jax.ShapeDtypeStruct((tiles, frames * rows_here + 16, lc.shape[1]), BF16),
        in_specs=[pl.BlockSpec(memory_space=SMEM)] + vmem_spec(5),
        out_specs=pl.BlockSpec(memory_space=VMEM),
        compiler_params=pltpu.CompilerParams(vmem_limit_bytes=LIMIT),
        name="strips",
    )(
        where, raw.reshape(frames * rows_here, strip), scales.reshape(-1, scales.shape[-1]), gains,
        *two_parts(lc),
    )


def box_area(top, left, band_rows, band_cols):
    row = top // 8 * 8
    col = left // 128 * 128
    area = (
        pl.ds(pl.multiple_of(row, 8), band_rows + 8),
        pl.ds(pl.multiple_of(col, 128), band_cols + 128),
    )
    return area, top - row, left - col


def field_kernel(
    led_row, led_col, patterns, spec_ref, pupil_ref, cols_hi, cols_lo, rows_hi, rows_lo,
    field_ref, estimate_ref, wide, bright,
):
    step = pl.program_id(0)
    group = field_ref.shape[0]
    band_rows, band_cols = pupil_ref.shape[1:]
    width = spec_ref.shape[2]
    half_h = field_ref.shape[1] // 2
    half_w = field_ref.shape[2]

    @pl.when(step == 0)
    def _():
        wide[...] = jnp.zeros_like(wide)
        wide[:, : spec_ref.shape[1], :width] = spec_ref[...]

    boxes = []
    for place in range(group):
        led = step * group + place
        top = led_row[led]
        left = led_col[led]
        area, down, right = box_area(top, left, band_rows, band_cols)
        parts = []
        for part in range(2):
            strip = pltpu.roll(wide[(part, *area)], lax.rem(2 * band_cols - right, 2 * band_cols), 1)
            strip = pltpu.roll(strip[:, :band_cols], lax.rem(band_rows + 8 - down, band_rows + 8), 0)
            parts.append(strip[:band_rows])
        lit_re = pupil_ref[0] * parts[0] - pupil_ref[1] * parts[1]
        lit_im = pupil_ref[0] * parts[1] + pupil_ref[1] * parts[0]
        boxes.append(jnp.concatenate([lit_re, lit_im], axis=1))
    high, low = split(jnp.concatenate(boxes, axis=0))
    spread = mm(high, cols_hi[...]) + mm(high, cols_lo[...]) + mm(low, cols_hi[...])
    left_rows = jnp.concatenate([rows_hi[...], rows_hi[...], rows_lo[...]], axis=1)
    for place in range(group):
        one = spread[place * band_rows : (place + 1) * band_rows]
        high, low = split(jnp.concatenate([one[:, :half_w], one[:, half_w:]], axis=0))
        field = mm(left_rows, jnp.concatenate([high, low, high], axis=0))
        field_ref[place] = field
        bright[step * group + place] = field[:half_h] ** 2 + field[half_h:] ** 2

    @pl.when(step == pl.num_programs(0) - 1)
    def _():
        def one_frame(frame, carry):
            total = bright[patterns[frame, 0]]
            for lit in range(1, patterns.shape[1]):
                total += bright[patterns[frame, lit]]
            estimate_ref[frame] = total
            return carry

        lax.fori_loop(0, patterns.shape[0], one_frame, 0)


def all_fields(spectrum, pupil, patterns, led_row, led_col, tables, group=4):
    rows, cols = tables
    leds = led_row.shape[0]
    _, height, width = spectrum.shape
    half_h, half_w = height // 2, width // 2
    whole = lambda shape: pl.BlockSpec(shape, lambda i: (0,) * len(shape))
    scalar = pl.BlockSpec(memory_space=SMEM)
    constants = [*two_parts(cols), *two_parts(rows)]
    return pl.pallas_call(
        field_kernel,
        grid=(leds // group,),
        out_shape=(
            jax.ShapeDtypeStruct((leds, 2 * half_h, half_w), F32),
            jax.ShapeDtypeStruct((patterns.shape[0], half_h, half_w), F32),
        ),
        in_specs=[scalar] * 3
        + [whole(spectrum.shape), whole(pupil.shape)]
        + [whole(c.shape) for c in constants],
        out_specs=(
            pl.BlockSpec((group, 2 * half_h, half_w), lambda i: (i, 0, 0)),
            whole((patterns.shape[0], half_h, half_w)),
        ),
        scratch_shapes=[
            pltpu.VMEM((2, height + 8, width + 128), F32),
            pltpu.VMEM((leds, half_h, half_w), F32),
        ],
        compiler_params=pltpu.CompilerParams(vmem_limit_bytes=LIMIT),
        cost_estimate=pl.CostEstimate(
            flops=8_000_000_000, bytes_accessed=16_000_000, transcendentals=0
        ),
        name="fields",
    )(led_row, led_col, patterns, spectrum, pupil, *constants)


def window_kernel(dq_ref, after, lr_hi, lr_lo, lr_sum, shapes_ref, window_ref, *, frames, core):
    slabs, lines, half_w = dq_ref.shape
    lines -= 16
    half_h = lr_hi.shape[0]
    rows_here = lines // frames
    height = slabs * rows_here
    over_y = 1.0 / (core * (height * (height * height - 1) / 12.0))
    over_x = 1.0 / (height * (core * (core * core - 1) / 12.0))
    lane = lax.broadcasted_iota(jnp.int32, (8, 128), 1)
    notes = [rows_value(dq_ref[slab, lines:]) for slab in range(slabs)]
    slopes = functools.reduce(jnp.add, notes)
    slopes = slopes * jnp.where(lane % 2 == 0, over_y, over_x)
    slab_means = jnp.zeros((8, 128), F32)
    for slab in range(slabs):
        slab_means = jnp.where(lane == slab, notes[slab][:, 6:7], slab_means)
    left_rows = jnp.concatenate([lr_hi[...], lr_lo[...]], axis=1)
    if rows_here % 16:
        values = [dq_ref[slab, :lines].astype(F32) for slab in range(slabs)]
    else:
        values = [dq_ref[slab, :lines] for slab in range(slabs)]
    means = []
    for frame in range(frames):
        cut = slice(frame * rows_here, (frame + 1) * rows_here)
        whole = jnp.concatenate([v[cut] for v in values], axis=0).astype(BF16)
        window = mm(left_rows, jnp.concatenate([whole, whole], axis=0))
        level = jnp.sum(lr_sum[...] * slab_means[frame : frame + 1], axis=1, keepdims=True)
        window = window + level
        for shape in range(6):
            window = window - shapes_ref[shape] * slopes[frame : frame + 1, shape : shape + 1]
        mean = jnp.sum(window) * (1.0 / (half_h * half_w))
        means.append(jnp.full((1, 128), mean, F32))
        window_ref[frame * half_h : (frame + 1) * half_h] = (window - mean).astype(BF16)
    means = jnp.concatenate(means + [jnp.zeros((8 - frames, 128), F32)], axis=0)
    window_ref[frames * half_h :] = parts_rows(means, half_w)


def tilt_shapes(height, width, margin, core, lr, lc):
    rows_y = lr @ (np.arange(height) - (height - 1) / 2.0)
    local = np.arange(width) - margin
    shapes = []
    for begin, end, shift in ((0, core, 0), (-margin, 0, core), (core, core + margin, -core)):
        on = (local >= begin) & (local < end)
        xc = (local + shift - (core - 1) / 2.0) * on
        flat_line = on.astype(np.float64) @ lc
        xc_line = xc @ lc
        shapes.append(np.outer(rows_y, flat_line))
        shapes.append(np.outer(np.ones(len(rows_y)), xc_line))
    return np.stack(shapes).astype(np.float32)


def windows(arrived, after, frames, lr, shapes, core):
    slabs, _, half_w = arrived.shape
    half_h, height = lr.shape
    sums = np.zeros((half_h, 128), np.float32)
    sums[:, :slabs] = lr.reshape(half_h, slabs, height // slabs).sum(axis=2)
    return pl.pallas_call(
        functools.partial(window_kernel, frames=frames, core=core),
        out_shape=jax.ShapeDtypeStruct((frames * half_h + 16, half_w), BF16),
        in_specs=vmem_spec(1) + [pl.BlockSpec(memory_space=pl.ANY)] + vmem_spec(4),
        out_specs=pl.BlockSpec(memory_space=VMEM),
        compiler_params=pltpu.CompilerParams(vmem_limit_bytes=LIMIT),
        name="windows",
    )(arrived, after, *two_parts(lr), sums, shapes)


def update_kernel(
    led_row, led_col, patterns, where, field_ref, estimate_ref, w0, w1, w2, w3,
    spec_ref, pupil_ref, rt_hi, rt_lo, ct_hi, ct_lo,
    fr_hi, fr_lo, fc_hi, fc_lo,
    fresh_ref, high_ref, low_ref, first_ref, second_ref, misfit, weight, grads,
):
    step = pl.program_id(0)
    group = field_ref.shape[0]
    band_rows, band_cols = pupil_ref.shape[1:]
    height, width = spec_ref.shape[1:]
    half_h, half_w = misfit.shape[1:]
    frames_here = w0.shape[0] // half_h
    my_group = where[0]
    is_odd = where[1] == 1

    @pl.when(step == 0)
    def _():
        grads[...] = jnp.zeros_like(grads)
        weight[...] = jnp.zeros_like(weight)
        for slot, window in enumerate((w0, w1, w2, w3)):
            owner = jnp.bitwise_xor(my_group, slot)
            means = rows_value(window[frames_here * half_h :])
            for place in range(frames_here):
                frame = owner * frames_here + place
                value = estimate_ref[frame] - means[place : place + 1, 0:1]
                value -= window[place * half_h : (place + 1) * half_h].astype(F32)
                for lit in range(patterns.shape[1]):
                    weight[patterns[frame, lit]] += value

    left_rows = jnp.concatenate([rt_hi[...], rt_lo[...]], axis=0)
    backs = []
    for place in range(group):
        q = weight[step * group + place]
        field = field_ref[place]
        high, low = split(jnp.concatenate([field[:half_h] * q, field[half_h:] * q], axis=0))
        both = mm(left_rows, high)
        back = both[: 2 * band_rows] + both[2 * band_rows :] + mm(rt_hi[...], low)
        backs.append(jnp.concatenate([back[:band_rows], back[band_rows:]], axis=1))
    high, low = split(jnp.concatenate(backs, axis=0))
    boxes = mm(high, ct_hi[...]) + mm(high, ct_lo[...]) + mm(low, ct_hi[...])
    for place in range(group):
        led = step * group + place
        one = boxes[place * band_rows : (place + 1) * band_rows]
        back_re, back_im = one[:, :band_cols], one[:, band_cols:]
        parts = (
            pupil_ref[0] * back_re + pupil_ref[1] * back_im,
            pupil_ref[0] * back_im - pupil_ref[1] * back_re,
        )
        top = led_row[led]
        left = led_col[led]
        area, down, right = box_area(top, left, band_rows, band_cols)
        for part in range(2):
            filled = jnp.concatenate([parts[part], jnp.zeros((8, band_cols), F32)], axis=0)
            filled = pltpu.roll(filled, down, 0)
            filled = jnp.concatenate([filled, jnp.zeros((band_rows + 8, 128), F32)], axis=1)
            grads[(part, *area)] += pltpu.roll(filled, right, 1)

    @pl.when(step == pl.num_programs(0) - 1)
    def _():
        fresh_re = spec_ref[0] - (4.0 * STEP) * grads[0, :height, :width]
        fresh_im = spec_ref[1] - (4.0 * STEP) * grads[1, :height, :width]
        fresh_ref[0] = fresh_re
        fresh_ref[1] = fresh_im
        re_hi, re_lo = split(fresh_re)
        im_hi, im_lo = split(fresh_im)
        high = jnp.concatenate([re_hi, im_hi], axis=0)
        low = jnp.concatenate([re_lo, im_lo], axis=0)
        spread = mm(fr_hi[...], high) + mm(fr_lo[...], high) + mm(fr_hi[...], low)
        high, low = split(jnp.concatenate([spread[:height], spread[height:]], axis=1))
        high_ref[...] = high
        low_ref[...] = low
        contract = functools.partial(
            lax.dot_general,
            dimension_numbers=(((1,), (1,)), ((), ())),
            preferred_element_type=F32,
        )
        sides = (
            contract(fc_hi[...], high) + contract(fc_lo[...], high) + contract(fc_hi[...], low)
        )
        half = sides.shape[0] // 2
        to_left, to_right = sides[:half], sides[half:]
        first_ref[...] = jnp.where(is_odd, to_left, to_right)
        second_ref[...] = jnp.where(is_odd, to_right, to_left)


def update(
    field, estimate, window_parts, spectrum, pupil, patterns, led_row, led_col, where, tables,
    margin, group=4,
):
    rows, cols = tables
    leds = led_row.shape[0]
    _, height, width = spectrum.shape
    half_h, half_w = height // 2, width // 2
    fr_re, fr_im = wave(np.arange(height), np.arange(height) - height // 2, height, height)
    full_rows = np.block([[fr_re, -fr_im], [fr_im, fr_re]])
    side_places = np.concatenate([np.arange(margin), width - margin + np.arange(margin)])
    fc_re, fc_im = wave(side_places, np.arange(width) - width // 2, width, width)
    sides = np.concatenate(
        [
            np.concatenate([fc_re[:margin], -fc_im[:margin]], axis=1),
            np.concatenate([fc_im[:margin], fc_re[:margin]], axis=1),
            np.concatenate([fc_re[margin:], -fc_im[margin:]], axis=1),
            np.concatenate([fc_im[margin:], fc_re[margin:]], axis=1),
        ]
    )
    constants = [
        *two_parts(rows.T),
        *two_parts(cols.T),
        *two_parts(full_rows),
        *two_parts(sides),
    ]
    whole = lambda shape: pl.BlockSpec(shape, lambda i: (0,) * len(shape))
    scalar = pl.BlockSpec(memory_space=SMEM)
    operands = [estimate, *window_parts, spectrum, pupil, *constants]
    out_shape = (
        jax.ShapeDtypeStruct(spectrum.shape, F32),
        jax.ShapeDtypeStruct((height, 2 * width), BF16),
        jax.ShapeDtypeStruct((height, 2 * width), BF16),
        jax.ShapeDtypeStruct((2 * margin, height), F32),
        jax.ShapeDtypeStruct((2 * margin, height), F32),
    )
    return pl.pallas_call(
        update_kernel,
        grid=(leds // group,),
        out_shape=out_shape,
        in_specs=[scalar] * 4
        + [pl.BlockSpec((group, 2 * half_h, half_w), lambda i: (i, 0, 0))]
        + [whole(o.shape) for o in operands],
        out_specs=tuple(whole(o.shape) for o in out_shape),
        scratch_shapes=[
            pltpu.VMEM((8, half_h, half_w), F32),
            pltpu.VMEM((leds, half_h, half_w), F32),
            pltpu.VMEM((2, height + 8, width + 128), F32),
        ],
        compiler_params=pltpu.CompilerParams(vmem_limit_bytes=LIMIT),
        name="update",
    )(led_row, led_col, patterns, where, field, *operands)


def object_kernel(high_ref, low_ref, re_hi, re_lo, im_hi, im_lo, out_ref):
    width = re_hi.shape[0]
    core = out_ref.shape[2]
    zre_hi, zim_hi = high_ref[:, :width], high_ref[:, width:]
    zre_lo, zim_lo = low_ref[:, :width], low_ref[:, width:]
    z_re = jnp.concatenate([zre_hi, zre_hi, zre_lo], axis=1)
    z_im = jnp.concatenate([zim_hi, zim_hi, zim_lo], axis=1)
    c_re = jnp.concatenate([re_hi[...], re_lo[...], re_hi[...]], axis=0)
    c_im = jnp.concatenate([im_hi[...], im_lo[...], im_hi[...]], axis=0)
    out_ref[0] = (mm(z_re, c_re) - mm(z_im, c_im))[:, :core]
    out_ref[1] = (mm(z_re, c_im) + mm(z_im, c_re))[:, :core]


def object_core(high, low, margin, core):
    height, width = high.shape[0], high.shape[1] // 2
    places = (margin + np.arange(width)) % width
    col_re, col_im = wave(np.arange(width) - width // 2, places, width, width)
    constants = [*two_parts(col_re), *two_parts(col_im)]
    return pl.pallas_call(
        object_kernel,
        out_shape=jax.ShapeDtypeStruct((2, height, core), F32),
        in_specs=vmem_spec(6),
        out_specs=pl.BlockSpec(memory_space=VMEM),
        compiler_params=pltpu.CompilerParams(vmem_limit_bytes=LIMIT),
        cost_estimate=pl.CostEstimate(
            flops=3_000_000_000, bytes_accessed=5_000_000, transcendentals=0
        ),
        name="object",
    )(high, low, *constants)


def blend_kernel(where, first_ref, second_ref, in_ref, out_ref, *, margin, last):
    side = pl.program_id(0)
    tile = where[2]
    is_odd = where[1] == 1
    height = out_ref.shape[1]
    lanes = out_ref.shape[2]
    lane = lax.broadcasted_iota(jnp.int32, (1, lanes), 1).astype(F32)
    span = 2.0 * margin

    def other_of(incoming):
        wide = jnp.concatenate([incoming, jnp.zeros((lanes - margin, height), F32)], axis=0)
        return jnp.transpose(wide, (1, 0))

    @pl.when(side == 0)
    def _():
        on = (lane < margin) & (tile > 0)
        own_w = jnp.where(on, (lane + margin + 0.5) / span, 1.0)
        other_w = jnp.where(on, (margin - lane - 0.5) / span, 0.0)
        incoming = jnp.where(is_odd, first_ref[...], second_ref[...])
        for part in range(2):
            other = other_of(incoming[part * margin : (part + 1) * margin])
            out_ref[part] = in_ref[part] * own_w + other * other_w

    @pl.when(side == 1)
    def _():
        q = lane - last
        on = (q >= 0.0) & (q < margin) & (tile < where[3] - 1)
        own_w = jnp.where(on, (span - q - 0.5) / span, 1.0)
        other_w = jnp.where(on, (q + 0.5) / span, 0.0)
        incoming = jnp.where(is_odd, second_ref[...], first_ref[...])
        for part in range(2):
            other = other_of(incoming[part * margin : (part + 1) * margin])
            out_ref[part] = in_ref[part] * own_w + pltpu.roll(other, last, 1) * other_w


def blend(core_part, first, second, where, margin):
    _, height, core = core_part.shape
    lanes = 128
    steps = pl.cdiv(core, lanes) - 1
    last = core - margin - steps * lanes
    block = pl.BlockSpec((2, height, lanes), lambda i: (0, 0, i * steps))
    whole = pl.BlockSpec(first.shape, lambda i: (0, 0))
    return pl.pallas_call(
        functools.partial(blend_kernel, margin=margin, last=last),
        grid=(2,),
        out_shape=jax.ShapeDtypeStruct(core_part.shape, F32),
        in_specs=[pl.BlockSpec(memory_space=SMEM), whole, whole, block],
        out_specs=block,
        input_output_aliases={3: 0},
        name="blend",
    )(where, first, second, core_part)


def body(raw, scales, flat, spectrum, pupil, patterns, led_row, led_col):
    height, core = flat.shape
    margin = OV // 2
    width = core + OV
    tiles = lax.axis_size("tile")
    tile = lax.axis_index("tile")
    grp = lax.axis_index("grp")
    frames_here = raw.shape[0]
    band_rows, band_cols = pupil.shape[1:]
    spectrum_tile = spectrum[0]
    odd = lax.rem(tile, 2)
    where = jnp.stack([grp, odd, tile, jnp.int32(tiles)]).astype(jnp.int32)

    swap_a = [(i, i ^ 1) for i in range(tiles)]
    swap_b = [(i, ((i + 1) ^ 1) - 1) for i in range(1, tiles - 1)]

    def neighbours(for_a, for_b):
        return lax.ppermute(for_a, "tile", swap_a), lax.ppermute(for_b, "tile", swap_b)

    tables = stacked_tables(height, width, band_rows, band_cols)
    passes = (low_pass(height, band_rows), low_pass(width, band_cols).T)
    shapes = tilt_shapes(height, width, margin, core, *passes)

    gains = (flat - 1.0).astype(BF16).reshape(tiles, height // tiles, core)
    gains = jnp.pad(gains, ((0, 0), (0, 0), (0, OV)))
    gains = lax.all_to_all(gains, "tile", split_axis=0, concat_axis=0, tiled=True)
    narrow = strips(raw, scales, gains, where, passes[1], tiles, core, margin)
    arrived = lax.all_to_all(narrow, "tile", split_axis=0, concat_axis=0, tiled=True)
    field, estimate = all_fields(spectrum_tile, pupil, patterns, led_row, led_col, tables)
    window = windows(arrived, estimate, frames_here, passes[0], shapes, core)

    swap_core = [(i, i ^ 1) for i in range(4)]
    swap_chip = [(i, i ^ 2) for i in range(4)]
    other = functools.partial(lax.ppermute, axis_name="grp")
    window_2 = other(window, perm=swap_chip)
    window_1 = other(window, perm=swap_core)
    window_3 = other(window_2, perm=swap_core)

    fresh, high, low, for_a, for_b = update(
        field, estimate, (window, window_1, window_2, window_3), spectrum_tile, pupil, patterns,
        led_row, led_col, where, tables, margin,
    )
    side_a, side_b = neighbours(for_a, for_b)
    core_part = object_core(high, low, margin, core)
    stitched = blend(core_part, side_a, side_b, where, margin)
    return fresh[None], stitched


def solution(mesh):
    return jax.shard_map(
        body,
        mesh=mesh,
        in_specs=(
            P("grp", "tile", None),
            P("grp", "tile", None),
            P(None, "tile"),
            P("tile", None, None, None),
            P(),
            P(),
            P(),
            P(),
        ),
        out_specs=(P("tile", None, None, None), P(None, None, "tile")),
        check_vma=False,
    )
```

```python
import functools
import math

import jax
import jax.numpy as jnp
import ml_dtypes
import numpy as np
from jax import lax
from jax.experimental import pallas as pl
from jax.experimental.pallas import tpu as pltpu
from jax.sharding import PartitionSpec as P

OV = 32
BC = 32
STEP = 0.02
F32 = jnp.float32
BF16 = jnp.bfloat16
VMEM = pltpu.VMEM
SMEM = pltpu.SMEM
LIMIT = 30 << 20


def two_parts(table):
    table = np.asarray(table, np.float64)
    high = table.astype(ml_dtypes.bfloat16)
    low = (table - high.astype(np.float64)).astype(ml_dtypes.bfloat16)
    return high, low


def wave(places, freqs, length, norm):
    turns = np.outer(places, freqs) % length
    angle = turns * (2.0 * math.pi / length)
    return np.cos(angle) / math.sqrt(norm), np.sin(angle) / math.sqrt(norm)


def low_pass(length, band):
    places = 2 * np.arange(length // 2)[:, None] - np.arange(length)[None, :]
    total = np.ones(places.shape)
    for freq in range(1, band):
        total += 2.0 * np.cos(2.0 * math.pi * ((freq * places) % length) / length)
    return total / length


def stacked_tables(height, width, band_rows, band_cols):
    row_re, row_im = wave(
        2 * np.arange(height // 2), np.arange(band_rows) - band_rows // 2, height, band_rows
    )
    rows = np.block([[row_re, -row_im], [row_im, row_re]])
    col_re, col_im = wave(
        np.arange(band_cols) - band_cols // 2, 2 * np.arange(width // 2), width, band_cols
    )
    cols = np.block([[col_re, col_im], [-col_im, col_re]])
    return rows, cols


def split(values):
    high = values.astype(BF16)
    return high, (values - high.astype(F32)).astype(BF16)


def mm(left, right):
    return jnp.dot(left, right, preferred_element_type=F32)


def vmem_spec(count):
    return [pl.BlockSpec(memory_space=VMEM)] * count


def parts_rows(values, columns):
    high = values.astype(BF16).astype(F32)
    rest = values - high
    middle = rest.astype(BF16).astype(F32)
    last = rest - middle
    top = jnp.concatenate([high, middle], axis=1)
    bottom = jnp.concatenate([last, jnp.zeros_like(last)], axis=1)
    rows = jnp.concatenate([top, bottom], axis=0)
    if columns > 256:
        rows = jnp.concatenate([rows, jnp.zeros((16, columns - 256), F32)], axis=1)
    return rows.astype(BF16)


def rows_value(rows):
    rows = rows.astype(F32)
    return rows[:8, :128] + rows[:8, 128:256] + rows[8:, :128]


def gains_kernel(flat_hbm, out_ref, flat, sems):
    core, height = flat_hbm.shape
    tiles, rows_here, width = out_ref.shape
    spans = [(begin, min(128, core - begin)) for begin in range(0, core, 128)]
    loads = []
    for number, (begin, length) in enumerate(spans):
        part = pl.ds(begin, length)
        load = pltpu.make_async_copy(flat_hbm.at[part], flat.at[part], sems.at[number])
        load.start()
        loads.append(load)
    for load, (begin, length) in zip(loads, spans):
        load.wait()
        gains = flat[begin : begin + length] - 1.0
        if length < 128:
            gains = jnp.concatenate([gains, jnp.zeros((128 - length, height), F32)], axis=0)
        by_rows = jnp.transpose(gains, (1, 0)).reshape(tiles, rows_here, 128)
        out_ref[:, :, begin : begin + 128] = by_rows.astype(BF16)


def gains_by_rows(flat, tiles, width):
    core, height = flat.shape
    return pl.pallas_call(
        gains_kernel,
        out_shape=jax.ShapeDtypeStruct((tiles, height // tiles, width), BF16),
        in_specs=[pl.BlockSpec(memory_space=pltpu.HBM)],
        out_specs=pl.BlockSpec(memory_space=VMEM),
        scratch_shapes=[pltpu.VMEM((core, height), F32), pltpu.SemaphoreType.DMA((-(-core // 128),))],
        compiler_params=pltpu.CompilerParams(vmem_limit_bytes=LIMIT),
        name="gains",
    )(pltpu.with_memory_space_constraint(flat, pltpu.HBM))


def dequantize_kernel(raw_ref, scales_ref, after, out_ref, *, core, margin):
    lines, strip = raw_ref.shape
    coarse_rows, coarse_cols = scales_ref.shape
    tiles, _, width = out_ref.shape
    ratio = lines // coarse_rows
    row = lax.broadcasted_iota(jnp.int32, (lines, coarse_rows), 0)
    pick = lax.broadcasted_iota(jnp.int32, (lines, coarse_rows), 1)
    spread_rows = (row // ratio == pick).astype(F32).astype(BF16)
    factors = mm(spread_rows, scales_ref[...])
    wide = (coarse_cols // 128 + 1) * 128
    factors = jnp.concatenate([factors, jnp.zeros((lines, wide - coarse_cols), F32)], axis=1)

    blocks = []
    for tile in range(tiles):
        begin = (tile * core - margin) // BC
        blocks.append(pltpu.roll(factors, -begin % wide, 1)[:, :128].astype(BF16))
    block = lax.broadcasted_iota(jnp.int32, (128, width), 0)
    place = lax.broadcasted_iota(jnp.int32, (128, width), 1) + (-margin) % BC
    inside = (place >= block * BC) & (place < (block + 1) * BC)
    scales = mm(jnp.concatenate(blocks, axis=0), inside.astype(F32).astype(BF16))
    for tile in range(tiles):
        start = tile * core - margin
        base = max(start, 0) // 128 * 128
        span = min(width + 128, strip - base)
        codes = raw_ref[:, base : base + span].astype(F32)
        turn = (base - start) % span
        if turn:
            codes = pltpu.roll(codes, turn, 1)
        out_ref[tile] = codes[:, :width] * scales[tile * lines : (tile + 1) * lines]


def dequantize(raw, scales, after, tiles, core, margin):
    frames, rows_here, strip = raw.shape
    return pl.pallas_call(
        functools.partial(dequantize_kernel, core=core, margin=margin),
        out_shape=jax.ShapeDtypeStruct((tiles, frames * rows_here, core + 2 * margin), F32),
        in_specs=vmem_spec(2) + [pl.BlockSpec(memory_space=pl.ANY)],
        out_specs=pl.BlockSpec(memory_space=VMEM),
        compiler_params=pltpu.CompilerParams(vmem_limit_bytes=LIMIT),
        cost_estimate=pl.CostEstimate(
            flops=2_000_000_000, bytes_accessed=4_000_000, transcendentals=0
        ),
        name="dequantize",
    )(raw.reshape(frames * rows_here, strip), scales.reshape(-1, scales.shape[-1]), after)


def strips_kernel(where, dq_ref, gains_ref, lc_ref, out_ref, *, frames, core, margin):
    tiles, lines, width = dq_ref.shape
    half_w = lc_ref.shape[1]
    rows_here = lines // frames
    line = lax.broadcasted_iota(jnp.int32, (1, width), 1)
    in_core = ((line >= margin) & (line < margin + core)).astype(F32)
    xc = (line.astype(F32) - margin - (core - 1) / 2.0) * in_core
    first_row = (where[2] * rows_here).astype(F32)
    height = rows_here * tiles
    yc = lax.broadcasted_iota(jnp.int32, (rows_here, 1), 0).astype(F32)
    yc = yc + (first_row - (height - 1) / 2.0)
    lane = lax.broadcasted_iota(jnp.int32, (8, 128), 1)
    narrow_lane = lax.broadcasted_iota(jnp.int32, (1, 128), 1)

    own, highs, lows = [], [], []
    for tile in range(tiles):
        gains = pltpu.roll(gains_ref[tile].astype(F32), margin, 1)
        if tile > 0:
            end = gains_ref[tile - 1][:, width - 128 :].astype(F32)
            end = pltpu.roll(end, (2 * margin) + margin, 1)
            end = jnp.where(narrow_lane < margin, end, 0.0)
            gains = jnp.concatenate([gains[:, :128] + end, gains[:, 128:]], axis=1)
        if tile < tiles - 1:
            end = gains_ref[tile + 1][:, :128].astype(F32)
            end = pltpu.roll(end, 128 - margin, 1)
            end = jnp.where(narrow_lane >= 128 - margin, end, 0.0)
            gains = jnp.concatenate(
                [gains[:, : width - 128], gains[:, width - 128 :] + end], axis=1
            )
        gains = jnp.concatenate([gains + 1.0] * frames, axis=0)
        flattened = dq_ref[tile] * gains
        high, low = split(flattened)
        highs.append(high)
        lows.append(low)
        sums, lines_y = [], []
        for frame in range(frames):
            cut = slice(frame * rows_here, (frame + 1) * rows_here)
            sums.append(jnp.sum(flattened[cut], axis=0, keepdims=True))
            lines_y.append(jnp.sum(flattened[cut] * yc, axis=0, keepdims=True))
        blank = [jnp.zeros((8 - frames, width), F32)]
        slope_y = jnp.sum(jnp.concatenate(lines_y + blank, axis=0) * in_core, axis=1, keepdims=True)
        slope_x = jnp.sum(jnp.concatenate(sums + blank, axis=0) * xc, axis=1, keepdims=True)
        own.append(jnp.where(lane == 0, slope_y, jnp.where(lane == 1, slope_x, 0.0)))
    high, low = jnp.concatenate(highs, axis=0), jnp.concatenate(lows, axis=0)
    lc_hi, lc_lo = lc_ref[:width], lc_ref[width:]
    narrow = mm(high, lc_hi) + mm(high, lc_lo) + mm(low, lc_hi)
    for tile in range(tiles):
        one = narrow[tile * lines : (tile + 1) * lines]
        means, centred = [], []
        for frame in range(frames):
            cut = slice(frame * rows_here, (frame + 1) * rows_here)
            mean = jnp.sum(one[cut], axis=0, keepdims=True)
            mean = jnp.sum(mean, axis=1, keepdims=True) * (1.0 / (rows_here * half_w))
            means.append(mean)
            centred.append(one[cut] - mean)
        out_ref[tile, :lines] = jnp.concatenate(centred, axis=0).astype(BF16)
        mean = jnp.concatenate(means + [jnp.zeros((8 - frames, 1), F32)], axis=0)
        packed = own[tile] + jnp.where(lane == 6, mean, 0.0)
        if tile > 0:
            packed += pltpu.roll(own[tile - 1], 2, 1)
        if tile < tiles - 1:
            packed += pltpu.roll(own[tile + 1], 4, 1)
        out_ref[tile, lines:] = parts_rows(packed, half_w)


def strips(dequantized, gains, where, lc, frames, core, margin):
    tiles, lines, _ = dequantized.shape
    return pl.pallas_call(
        functools.partial(strips_kernel, frames=frames, core=core, margin=margin),
        out_shape=jax.ShapeDtypeStruct((tiles, lines + 16, lc.shape[1]), BF16),
        in_specs=[pl.BlockSpec(memory_space=SMEM)] + vmem_spec(3),
        out_specs=pl.BlockSpec(memory_space=VMEM),
        compiler_params=pltpu.CompilerParams(vmem_limit_bytes=LIMIT),
        name="strips",
    )(where, dequantized, gains, np.concatenate(two_parts(lc)))


def box_area(top, left, band_rows, band_cols):
    row = top // 8 * 8
    col = left // 128 * 128
    area = (
        pl.ds(pl.multiple_of(row, 8), band_rows + 8),
        pl.ds(pl.multiple_of(col, 128), band_cols + 128),
    )
    return area, top - row, left - col


def field_kernel(
    led_row, led_col, patterns, spec_ref, pupil_ref, cols_ref, rows_ref,
    rows_hbm, small_hbm, field_ref, estimate_ref, rows_out, small_out, wide, bright, sems, *, group,
):
    leds, half_h, half_w = bright.shape
    loads = [
        pltpu.make_async_copy(rows_hbm, rows_out, sems.at[0]),
        pltpu.make_async_copy(small_hbm, small_out, sems.at[1]),
    ]
    for load in loads:
        load.start()
    band_rows, band_cols = pupil_ref.shape[1:]
    width = spec_ref.shape[2]
    depth = 2 * band_cols
    wide[...] = jnp.zeros_like(wide)
    wide[:, : spec_ref.shape[1], :width] = spec_ref[...]

    def some(step, carry):
        boxes = []
        for place in range(group):
            led = step * group + place
            area, down, right = box_area(led_row[led], led_col[led], band_rows, band_cols)
            back = lax.rem(2 * band_cols - right, 2 * band_cols)
            up = lax.rem(band_rows + 8 - down, band_rows + 8)
            parts = []
            for part in range(2):
                strip = pltpu.roll(wide[(part, *area)], back, 1)
                parts.append(pltpu.roll(strip[:, :band_cols], up, 0)[:band_rows])
            lit_re = pupil_ref[0] * parts[0] - pupil_ref[1] * parts[1]
            lit_im = pupil_ref[0] * parts[1] + pupil_ref[1] * parts[0]
            boxes.append(jnp.concatenate([lit_re, lit_im], axis=1))
        high, low = split(jnp.concatenate(boxes, axis=0))
        cols_hi, cols_lo = cols_ref[:depth], cols_ref[depth:]
        spread = mm(high, cols_hi) + mm(high, cols_lo) + mm(low, cols_hi)
        for place in range(group):
            one = spread[place * band_rows : (place + 1) * band_rows]
            high, low = split(jnp.concatenate([one[:, :half_w], one[:, half_w:]], axis=0))
            field = mm(rows_ref[...], jnp.concatenate([high, low, high], axis=0))
            field_ref[step * group + place] = field
            bright[step * group + place] = field[:half_h] ** 2 + field[half_h:] ** 2
        return carry

    lax.fori_loop(0, leds // group, some, 0)

    def one_frame(frame, carry):
        total = bright[patterns[0, frame]]
        for lit in range(1, patterns.shape[0]):
            total += bright[patterns[lit, frame]]
        estimate_ref[frame] = total
        return carry

    lax.fori_loop(0, patterns.shape[1], one_frame, 0)
    for load in loads:
        load.wait()


def all_fields(spectrum, pupil, patterns, led_row, led_col, tables, handed, group=8):
    rows, cols = tables
    leds = led_row.shape[0]
    _, height, width = spectrum.shape
    half_h, half_w = height // 2, width // 2
    high, low = two_parts(rows)
    return pl.pallas_call(
        functools.partial(field_kernel, group=group),
        out_shape=(
            jax.ShapeDtypeStruct((leds, 2 * half_h, half_w), F32),
            jax.ShapeDtypeStruct((patterns.shape[1], half_h, half_w), F32),
            *(jax.ShapeDtypeStruct(table.shape, table.dtype) for table in handed),
        ),
        in_specs=[pl.BlockSpec(memory_space=SMEM)] * 3
        + vmem_spec(4)
        + [pl.BlockSpec(memory_space=pltpu.HBM)] * 2,
        out_specs=tuple(vmem_spec(4)),
        scratch_shapes=[
            pltpu.VMEM((2, height + 8, width + 128), F32),
            pltpu.VMEM((leds, half_h, half_w), F32),
            pltpu.SemaphoreType.DMA((2,)),
        ],
        compiler_params=pltpu.CompilerParams(vmem_limit_bytes=LIMIT),
        cost_estimate=pl.CostEstimate(
            flops=8_000_000_000, bytes_accessed=16_000_000, transcendentals=0
        ),
        name="fields",
    )(
        led_row, led_col, patterns, spectrum, pupil, np.concatenate(two_parts(cols)),
        np.concatenate([high, high, low], axis=1),
        *(pltpu.with_memory_space_constraint(jnp.asarray(t), pltpu.HBM) for t in handed),
    )


def window_kernel(dq_ref, rows_ref, small_ref, window_ref, *, frames, core):
    slabs, lines, half_w = dq_ref.shape
    lines -= 16
    half_h = rows_ref.shape[0]
    lr_sum, line = small_ref[:half_h, :128], small_ref[half_h:]
    rows_here = lines // frames
    height = slabs * rows_here
    over_y = 1.0 / (core * (height * (height * height - 1) / 12.0))
    over_x = 1.0 / (height * (core * (core * core - 1) / 12.0))
    lane = lax.broadcasted_iota(jnp.int32, (8, 128), 1)
    notes = [rows_value(dq_ref[slab, lines:]) for slab in range(slabs)]
    slopes = functools.reduce(jnp.add, notes)
    slopes = slopes * jnp.where(lane % 2 == 0, over_y, over_x)
    slab_means = jnp.zeros((8, 128), F32)
    for slab in range(slabs):
        slab_means = jnp.where(lane == slab, notes[slab][:, 6:7], slab_means)
    if rows_here % 16:
        values = [dq_ref[slab, :lines].astype(F32) for slab in range(slabs)]
    else:
        values = [dq_ref[slab, :lines] for slab in range(slabs)]
    means = []
    for frame in range(frames):
        cut = slice(frame * rows_here, (frame + 1) * rows_here)
        whole = jnp.concatenate([v[cut] for v in values], axis=0).astype(BF16)
        window = mm(rows_ref[...], jnp.concatenate([whole, whole], axis=0))
        level = jnp.sum(lr_sum * slab_means[frame : frame + 1], axis=1, keepdims=True)
        window = window + level
        tilt_y, tilt_x = 0.0, 0.0
        for side in range(3):
            tilt_y += line[2 * side : 2 * side + 1] * slopes[frame : frame + 1, 2 * side : 2 * side + 1]
            tilt_x += line[2 * side + 1 : 2 * side + 2] * slopes[frame : frame + 1, 2 * side + 1 : 2 * side + 2]
        window = window - lr_sum[:, 127:128] * tilt_y - tilt_x
        mean = jnp.sum(window, axis=0, keepdims=True)
        mean = jnp.sum(mean, axis=1, keepdims=True) * (1.0 / (half_h * half_w))
        means.append(jnp.broadcast_to(mean, (1, 128)))
        window_ref[frame * half_h : (frame + 1) * half_h] = (window - mean).astype(BF16)
    means = jnp.concatenate(means + [jnp.zeros((8 - frames, 128), F32)], axis=0)
    window_ref[frames * half_h :] = parts_rows(means, half_w)


def tilt_lines(width, margin, core, lc):
    local = np.arange(width) - margin
    lines = []
    for begin, end, shift in ((0, core, 0), (-margin, 0, core), (core, core + margin, -core)):
        on = (local >= begin) & (local < end)
        lines.append(on.astype(np.float64) @ lc)
        lines.append(((local + shift - (core - 1) / 2.0) * on) @ lc)
    return np.stack(lines + lines[:2])


def window_tables(tiles, passes, margin, core):
    lr, lc = passes
    half_h, height = lr.shape
    sums = np.zeros((half_h, lc.shape[1]))
    sums[:, :tiles] = lr.reshape(half_h, tiles, height // tiles).sum(axis=2)
    sums[:, 127] = lr @ (np.arange(height) - (height - 1) / 2.0)
    small = np.concatenate([sums, tilt_lines(lc.shape[0], margin, core, lc)])
    return np.concatenate(two_parts(lr), axis=1), small.astype(np.float32)


def windows(arrived, rows, small, frames, core):
    half_h, half_w = rows.shape[0], arrived.shape[2]
    return pl.pallas_call(
        functools.partial(window_kernel, frames=frames, core=core),
        out_shape=jax.ShapeDtypeStruct((frames * half_h + 16, half_w), BF16),
        in_specs=vmem_spec(3),
        out_specs=pl.BlockSpec(memory_space=VMEM),
        compiler_params=pltpu.CompilerParams(vmem_limit_bytes=LIMIT),
        name="windows",
    )(arrived, rows, small)


def fetch_kernel(after, field_hbm, field_ref, sem):
    load = pltpu.make_async_copy(field_hbm, field_ref, sem)
    load.start()
    load.wait()


def fetch(field, after):
    return pl.pallas_call(
        fetch_kernel,
        out_shape=jax.ShapeDtypeStruct(field.shape, F32),
        in_specs=[pl.BlockSpec(memory_space=pl.ANY), pl.BlockSpec(memory_space=pltpu.HBM)],
        out_specs=pl.BlockSpec(memory_space=VMEM),
        scratch_shapes=[pltpu.SemaphoreType.DMA],
        compiler_params=pltpu.CompilerParams(vmem_limit_bytes=LIMIT),
        cost_estimate=pl.CostEstimate(flops=0, bytes_accessed=16_000_000, transcendentals=0),
        name="fetch",
    )(after, pltpu.with_memory_space_constraint(field, pltpu.HBM))


def across(left, right):
    dims = (((1,), (1,)), ((), ()))
    return lax.dot_general(left, right, dims, preferred_element_type=F32)


def update_kernel(
    led_row, led_col, patterns, where, field_ref, estimate_ref, w0, w1, w2, w3,
    spec_ref, pupil_ref, small_ref, big_hbm,
    fresh_ref, high_ref, low_ref, first_ref, second_ref,
    weight, grads, big, big_sem, *, group,
):
    leds, half_h, half_w = weight.shape
    band_rows, band_cols = pupil_ref.shape[1:]
    height, width = spec_ref.shape[1:]
    frames_here = w0.shape[0] // half_h
    is_odd = where[1] == 1
    big_load = pltpu.make_async_copy(big_hbm, big, big_sem)
    big_load.start()
    grads[...] = jnp.zeros_like(grads)
    weight[...] = jnp.zeros_like(weight)
    for slot, window in enumerate((w0, w1, w2, w3)):
        owner = jnp.bitwise_xor(where[0], slot)
        means = rows_value(window[frames_here * half_h :])
        for place in range(frames_here):
            frame = owner * frames_here + place
            value = estimate_ref[frame] - means[place : place + 1, 0:1]
            value -= window[place * half_h : (place + 1) * half_h].astype(F32)
            for lit in range(patterns.shape[0]):
                weight[patterns[lit, frame]] += value

    table_rows = 2 * band_rows

    def some(step, carry):
        left_rows = small_ref[: 2 * table_rows]
        cols_hi = small_ref[2 * table_rows : 2 * table_rows + 2 * half_w]
        cols_lo = small_ref[2 * table_rows + 2 * half_w :]
        backs = []
        for place in range(group):
            q = weight[step * group + place]
            field = field_ref[step * group + place]
            high, low = split(jnp.concatenate([field[:half_h] * q, field[half_h:] * q], axis=0))
            both = mm(left_rows, high)
            back = both[:table_rows] + both[table_rows:] + mm(left_rows[:table_rows], low)
            backs.append(jnp.concatenate([back[:band_rows], back[band_rows:]], axis=1))
        high, low = split(jnp.concatenate(backs, axis=0))
        boxes = mm(high, cols_hi) + mm(high, cols_lo) + mm(low, cols_hi)
        for place in range(group):
            led = step * group + place
            one = boxes[place * band_rows : (place + 1) * band_rows]
            back_re, back_im = one[:, :band_cols], one[:, band_cols:]
            parts = (
                pupil_ref[0] * back_re + pupil_ref[1] * back_im,
                pupil_ref[0] * back_im - pupil_ref[1] * back_re,
            )
            area, down, right = box_area(led_row[led], led_col[led], band_rows, band_cols)
            for part in range(2):
                filled = jnp.concatenate([parts[part], jnp.zeros((8, band_cols), F32)], axis=0)
                filled = pltpu.roll(filled, down, 0)
                filled = jnp.concatenate([filled, jnp.zeros((band_rows + 8, 128), F32)], axis=1)
                grads[(part, *area)] += pltpu.roll(filled, right, 1)
        return carry

    lax.fori_loop(0, leds // group, some, 0)
    fresh_re = spec_ref[0] - (4.0 * STEP) * grads[0, :height, :width]
    fresh_im = spec_ref[1] - (4.0 * STEP) * grads[1, :height, :width]
    fresh_ref[0] = fresh_re
    fresh_ref[1] = fresh_im
    re_hi, re_lo = split(fresh_re)
    im_hi, im_lo = split(fresh_im)
    high = jnp.concatenate([re_hi, im_hi], axis=0)
    low = jnp.concatenate([re_lo, im_lo], axis=0)
    big_load.wait()
    full = 2 * height
    rows_hi, rows_lo = big[:full], big[full : 2 * full]
    spread = mm(rows_hi, high) + mm(rows_lo, high) + mm(rows_hi, low)
    high, low = split(jnp.concatenate([spread[:height], spread[height:]], axis=1))
    high_ref[...] = high
    low_ref[...] = low
    side_rows = 2 * first_ref.shape[0]
    side = big[2 * full :]
    side_hi = jnp.concatenate([side[:side_rows], side[side_rows : 2 * side_rows]], axis=1)
    side_lo = jnp.concatenate([side[2 * side_rows : 3 * side_rows], side[3 * side_rows :]], axis=1)
    sides = across(side_hi, high) + across(side_lo, high) + across(side_hi, low)
    half = side_rows // 2
    to_left, to_right = sides[:half], sides[half:]
    first_ref[...] = jnp.where(is_odd, to_left, to_right)
    second_ref[...] = jnp.where(is_odd, to_right, to_left)


def update(
    field, estimate, window_parts, spectrum, pupil, patterns, led_row, led_col, where, tables,
    margin, group=8,
):
    rows, cols = tables
    leds = led_row.shape[0]
    _, height, width = spectrum.shape
    half_h, half_w = height // 2, width // 2
    fr_re, fr_im = wave(np.arange(height), np.arange(height) - height // 2, height, height)
    full_rows = np.block([[fr_re, -fr_im], [fr_im, fr_re]])
    side_places = np.concatenate([np.arange(margin), width - margin + np.arange(margin)])
    fc_re, fc_im = wave(side_places, np.arange(width) - width // 2, width, width)
    from_re = np.concatenate([fc_re[:margin], fc_im[:margin], fc_re[margin:], fc_im[margin:]])
    from_im = np.concatenate([-fc_im[:margin], fc_re[:margin], -fc_im[margin:], fc_re[margin:]])
    sides = [two_parts(from_re), two_parts(from_im)]
    big = np.concatenate(
        [*two_parts(full_rows), sides[0][0], sides[1][0], sides[0][1], sides[1][1]]
    )
    small = np.concatenate([*two_parts(rows.T), *two_parts(cols.T)])
    out_shape = (
        jax.ShapeDtypeStruct(spectrum.shape, F32),
        jax.ShapeDtypeStruct((height, 2 * width), BF16),
        jax.ShapeDtypeStruct((height, 2 * width), BF16),
        jax.ShapeDtypeStruct((2 * margin, height), F32),
        jax.ShapeDtypeStruct((2 * margin, height), F32),
    )
    return pl.pallas_call(
        functools.partial(update_kernel, group=group),
        out_shape=out_shape,
        in_specs=[pl.BlockSpec(memory_space=SMEM)] * 4
        + vmem_spec(9)
        + [pl.BlockSpec(memory_space=pltpu.HBM)],
        out_specs=tuple(vmem_spec(5)),
        scratch_shapes=[
            pltpu.VMEM((leds, half_h, half_w), F32),
            pltpu.VMEM((2, height + 8, width + 128), F32),
            pltpu.VMEM(big.shape, BF16),
            pltpu.SemaphoreType.DMA,
        ],
        compiler_params=pltpu.CompilerParams(vmem_limit_bytes=LIMIT),
        name="update",
    )(
        led_row, led_col, patterns, where, field, estimate, *window_parts, spectrum, pupil, small,
        pltpu.with_memory_space_constraint(jnp.asarray(big), pltpu.HBM),
    )


def object_kernel(high_ref, low_ref, table_ref, out_ref):
    core = out_ref.shape[1]
    width = high_ref.shape[1] // 2
    re_im_hi, re_im_lo = table_ref[: 2 * core], table_ref[2 * core :]
    parts = []
    for part in range(2):
        cut = slice(part * width, (part + 1) * width)
        z_hi, z_lo = high_ref[:, cut], low_ref[:, cut]
        parts.append(across(re_im_hi, z_hi) + across(re_im_lo, z_hi) + across(re_im_hi, z_lo))
    out_ref[0] = parts[0][:core] - parts[1][core:]
    out_ref[1] = parts[0][core:] + parts[1][:core]


def object_core(high, low, margin, core):
    height, width = high.shape[0], high.shape[1] // 2
    col_re, col_im = wave(margin + np.arange(core), np.arange(width) - width // 2, width, width)
    table = np.concatenate(two_parts(np.concatenate([col_re, col_im])))
    return pl.pallas_call(
        object_kernel,
        out_shape=jax.ShapeDtypeStruct((2, core, height), F32),
        in_specs=vmem_spec(3),
        out_specs=pl.BlockSpec(memory_space=VMEM),
        compiler_params=pltpu.CompilerParams(vmem_limit_bytes=LIMIT),
        cost_estimate=pl.CostEstimate(
            flops=3_000_000_000, bytes_accessed=5_000_000, transcendentals=0
        ),
        name="object",
    )(high, low, table)


def blend_kernel(where, first_ref, second_ref, in_ref, out_ref):
    side = pl.program_id(0)
    tile = where[2]
    is_odd = where[1] == 1
    margin = out_ref.shape[1]
    k = lax.broadcasted_iota(jnp.int32, (margin, 1), 0).astype(F32)
    span = 2.0 * margin
    at_left = side == 0
    own_w = jnp.where(at_left, k + margin + 0.5, span - k - 0.5) / span
    other_w = jnp.where(at_left, margin - k - 0.5, k + 0.5) / span
    has_other = jnp.where(at_left, tile > 0, tile < where[3] - 1)
    own_w = jnp.where(has_other, own_w, 1.0)
    other_w = jnp.where(has_other, other_w, 0.0)
    use_first = jnp.where(at_left, is_odd, jnp.logical_not(is_odd))
    other = jnp.where(use_first, first_ref[...], second_ref[...])
    for part in range(2):
        cut = slice(part * margin, (part + 1) * margin)
        out_ref[part] = in_ref[part] * own_w + other[cut] * other_w


def blend(core_part, first, second, where, margin):
    _, core, height = core_part.shape
    last = core // margin - 1
    block = pl.BlockSpec((2, margin, height), lambda i: (0, i * last, 0))
    whole = pl.BlockSpec(first.shape, lambda i: (0, 0))
    return pl.pallas_call(
        blend_kernel,
        grid=(2,),
        out_shape=jax.ShapeDtypeStruct(core_part.shape, F32),
        in_specs=[pl.BlockSpec(memory_space=SMEM), whole, whole, block],
        out_specs=block,
        input_output_aliases={3: 0},
        compiler_params=pltpu.CompilerParams(vmem_limit_bytes=LIMIT),
        name="blend",
    )(where, first, second, core_part)


def body(raw, scales, flat, spectrum, pupil, patterns, led_row, led_col):
    height, core = flat.shape
    margin = OV // 2
    width = core + OV
    tiles = lax.axis_size("tile")
    tile = lax.axis_index("tile")
    grp = lax.axis_index("grp")
    frames_here = raw.shape[0]
    band_rows, band_cols = pupil.shape[1:]
    spectrum_tile = spectrum[0]
    patterns = patterns.T
    odd = lax.rem(tile, 2)
    where = jnp.stack([grp, odd, tile, jnp.int32(tiles)]).astype(jnp.int32)

    swap_a = [(i, i ^ 1) for i in range(tiles)]
    swap_b = [(i, ((i + 1) ^ 1) - 1) for i in range(1, tiles - 1)]

    def neighbours(for_a, for_b):
        return lax.ppermute(for_a, "tile", swap_a), lax.ppermute(for_b, "tile", swap_b)

    tables = stacked_tables(height, width, band_rows, band_cols)
    passes = (low_pass(height, band_rows), low_pass(width, band_cols).T)

    by_rows = gains_by_rows(flat.T, tiles, width)
    dequantized = dequantize(raw, scales, by_rows, tiles, core, margin)
    gains = lax.all_to_all(by_rows, "tile", split_axis=0, concat_axis=0, tiled=True)
    narrow = strips(dequantized, gains, where, passes[1], frames_here, core, margin)
    arrived = lax.all_to_all(narrow, "tile", split_axis=0, concat_axis=0, tiled=True)
    handed = window_tables(tiles, passes, margin, core)
    field, estimate, rows, small = all_fields(
        spectrum_tile, pupil, patterns, led_row, led_col, tables, handed
    )
    window = windows(arrived, rows, small, frames_here, core)
    field = fetch(field, window)

    swap_core = [(i, i ^ 1) for i in range(4)]
    swap_chip = [(i, i ^ 2) for i in range(4)]
    other = functools.partial(lax.ppermute, axis_name="grp")
    window_2 = other(window, perm=swap_chip)
    window_1 = other(window, perm=swap_core)
    window_2, field = lax.optimization_barrier((window_2, field))
    window_3 = other(window_2, perm=swap_core)

    fresh, high, low, for_a, for_b = update(
        field, estimate, (window, window_1, window_2, window_3), spectrum_tile, pupil, patterns,
        led_row, led_col, where, tables, margin,
    )
    side_a, side_b = neighbours(for_a, for_b)
    core_part = object_core(high, low, margin, core)
    stitched = blend(core_part, side_a, side_b, where, margin)
    return fresh[None], jnp.transpose(stitched, (0, 2, 1))


def solution(mesh):
    return jax.shard_map(
        body,
        mesh=mesh,
        in_specs=(
            P("grp", "tile", None),
            P("grp", "tile", None),
            P(None, "tile"),
            P("tile", None, None, None),
            P(),
            P(),
            P(),
            P(),
        ),
        out_specs=(P("tile", None, None, None), P(None, None, "tile")),
        check_vma=False,
    )
```

```python
import functools
import math

import jax
import jax.numpy as jnp
import ml_dtypes
import numpy as np
from jax import lax
from jax.experimental import pallas as pl
from jax.experimental.pallas import tpu as pltpu
from jax.sharding import PartitionSpec as P

OV = 32
BC = 32
STEP = 0.02
F32 = jnp.float32
BF16 = jnp.bfloat16
VMEM = pltpu.VMEM
SMEM = pltpu.SMEM
LIMIT = 30 << 20


def two_parts(table):
    table = np.asarray(table, np.float64)
    high = table.astype(ml_dtypes.bfloat16)
    low = (table - high.astype(np.float64)).astype(ml_dtypes.bfloat16)
    return high, low


def wave(places, freqs, length, norm):
    turns = np.outer(places, freqs) % length
    angle = turns * (2.0 * math.pi / length)
    return np.cos(angle) / math.sqrt(norm), np.sin(angle) / math.sqrt(norm)


def low_pass(length, band):
    places = 2 * np.arange(length // 2)[:, None] - np.arange(length)[None, :]
    total = np.ones(places.shape)
    for freq in range(1, band):
        total += 2.0 * np.cos(2.0 * math.pi * ((freq * places) % length) / length)
    return total / length


def stacked_tables(height, width, band_rows, band_cols):
    row_re, row_im = wave(
        2 * np.arange(height // 2), np.arange(band_rows) - band_rows // 2, height, band_rows
    )
    rows = np.block([[row_re, -row_im], [row_im, row_re]])
    col_re, col_im = wave(
        np.arange(band_cols) - band_cols // 2, 2 * np.arange(width // 2), width, band_cols
    )
    cols = np.block([[col_re, col_im], [-col_im, col_re]])
    return rows, cols


def split(values):
    high = values.astype(BF16)
    return high, (values - high.astype(F32)).astype(BF16)


def mm(left, right):
    return jnp.dot(left, right, preferred_element_type=F32)


def vmem_spec(count):
    return [pl.BlockSpec(memory_space=VMEM)] * count


def parts_rows(values):
    high = values.astype(BF16).astype(F32)
    return jnp.concatenate([high, values - high], axis=0).astype(BF16)


def rows_value(rows):
    rows = rows.astype(F32)
    return rows[:8, :128] + rows[8:, :128]


def gains_kernel(flat_hbm, out_hbm, flat, out, sems, out_sems):
    core, height = flat_hbm.shape
    tiles, rows_here, width = out_hbm.shape
    spans = [(begin, min(128, core - begin)) for begin in range(0, core, 128)]
    loads = []
    for number, (begin, length) in enumerate(spans):
        part = pl.ds(begin, length)
        load = pltpu.make_async_copy(flat_hbm.at[part], flat.at[part], sems.at[number])
        load.start()
        loads.append(load)
    stores = []
    for number, (load, (begin, length)) in enumerate(zip(loads, spans)):
        load.wait()
        gains = flat[begin : begin + length] - 1.0
        if length < 128:
            gains = jnp.concatenate([gains, jnp.zeros((128 - length, height), F32)], axis=0)
        by_rows = jnp.transpose(gains, (1, 0)).reshape(tiles, rows_here, 128)
        out[:, :, begin : begin + 128] = by_rows.astype(BF16)
        part = (slice(None), slice(None), pl.ds(begin, 128))
        store = pltpu.make_async_copy(out.at[part], out_hbm.at[part], out_sems.at[number])
        store.start()
        stores.append(store)
    for store in stores:
        store.wait()


def gains_by_rows(flat, tiles, width):
    core, height = flat.shape
    return pl.pallas_call(
        gains_kernel,
        out_shape=jax.ShapeDtypeStruct((tiles, height // tiles, width), BF16),
        in_specs=[pl.BlockSpec(memory_space=pltpu.HBM)],
        out_specs=pl.BlockSpec(memory_space=pltpu.HBM),
        scratch_shapes=[
            pltpu.VMEM((core, height), F32),
            pltpu.VMEM((tiles, height // tiles, width), BF16),
            pltpu.SemaphoreType.DMA((-(-core // 128),)),
            pltpu.SemaphoreType.DMA((-(-core // 128),)),
        ],
        compiler_params=pltpu.CompilerParams(vmem_limit_bytes=LIMIT),
        name="gains",
    )(pltpu.with_memory_space_constraint(flat, pltpu.HBM))


def dequantize_kernel(raw_ref, scales_ref, after, out_ref, *, core, margin):
    lines, strip = raw_ref.shape
    coarse_rows, coarse_cols = scales_ref.shape
    tiles, _, width = out_ref.shape
    ratio = lines // coarse_rows
    row = lax.broadcasted_iota(jnp.int32, (lines, coarse_rows), 0)
    pick = lax.broadcasted_iota(jnp.int32, (lines, coarse_rows), 1)
    spread_rows = (row // ratio == pick).astype(F32).astype(BF16)
    factors = mm(spread_rows, scales_ref[...])
    wide = (coarse_cols // 128 + 1) * 128
    factors = jnp.concatenate([factors, jnp.zeros((lines, wide - coarse_cols), F32)], axis=1)

    blocks = []
    for tile in range(tiles):
        begin = (tile * core - margin) // BC
        blocks.append(pltpu.roll(factors, -begin % wide, 1)[:, :128].astype(BF16))
    block = lax.broadcasted_iota(jnp.int32, (128, width), 0)
    place = lax.broadcasted_iota(jnp.int32, (128, width), 1) + (-margin) % BC
    inside = (place >= block * BC) & (place < (block + 1) * BC)
    scales = mm(jnp.concatenate(blocks, axis=0), inside.astype(F32).astype(BF16))
    for tile in range(tiles):
        start = tile * core - margin
        base = max(start, 0) // 128 * 128
        span = min(width + 128, strip - base)
        codes = raw_ref[:, base : base + span].astype(F32)
        turn = (base - start) % span
        if turn:
            codes = pltpu.roll(codes, turn, 1)
        out_ref[tile] = codes[:, :width] * scales[tile * lines : (tile + 1) * lines]


def dequantize(raw, scales, after, tiles, core, margin):
    frames, rows_here, strip = raw.shape
    return pl.pallas_call(
        functools.partial(dequantize_kernel, core=core, margin=margin),
        out_shape=jax.ShapeDtypeStruct((tiles, frames * rows_here, core + 2 * margin), F32),
        in_specs=vmem_spec(2) + [pl.BlockSpec(memory_space=pl.ANY)],
        out_specs=pl.BlockSpec(memory_space=VMEM),
        compiler_params=pltpu.CompilerParams(vmem_limit_bytes=LIMIT),
        cost_estimate=pl.CostEstimate(
            flops=2_000_000_000, bytes_accessed=4_000_000, transcendentals=0
        ),
        name="dequantize",
    )(raw.reshape(frames * rows_here, strip), scales.reshape(-1, scales.shape[-1]), after)


def strips_kernel(where, dq_ref, gains_ref, lc_ref, out_hbm, out_ref, sems, *, frames, core, margin):
    tiles, lines, width = dq_ref.shape
    half_w = lc_ref.shape[1]
    rows_here = lines // frames
    line = lax.broadcasted_iota(jnp.int32, (1, width), 1)
    in_core = ((line >= margin) & (line < margin + core)).astype(F32)
    xc = (line.astype(F32) - margin - (core - 1) / 2.0) * in_core
    first_row = (where[2] * rows_here).astype(F32)
    height = rows_here * tiles
    yc = lax.broadcasted_iota(jnp.int32, (rows_here, 1), 0).astype(F32)
    yc = yc + (first_row - (height - 1) / 2.0)
    lane = lax.broadcasted_iota(jnp.int32, (8, 128), 1)
    narrow_lane = lax.broadcasted_iota(jnp.int32, (1, 128), 1)

    lc_hi, lc_lo = lc_ref[:width], lc_ref[width:]
    own, stores = [], []

    def windowed(tile):
        gains = pltpu.roll(gains_ref[tile].astype(F32), margin, 1)
        if tile > 0:
            end = gains_ref[tile - 1][:, width - 128 :].astype(F32)
            end = pltpu.roll(end, (2 * margin) + margin, 1)
            end = jnp.where(narrow_lane < margin, end, 0.0)
            gains = jnp.concatenate([gains[:, :128] + end, gains[:, 128:]], axis=1)
        if tile < tiles - 1:
            end = gains_ref[tile + 1][:, :128].astype(F32)
            end = pltpu.roll(end, 128 - margin, 1)
            end = jnp.where(narrow_lane >= 128 - margin, end, 0.0)
            gains = jnp.concatenate(
                [gains[:, : width - 128], gains[:, width - 128 :] + end], axis=1
            )
        gains = jnp.concatenate([gains + 1.0] * frames, axis=0)
        flattened = dq_ref[tile] * gains
        sums, lines_y = [], []
        for frame in range(frames):
            cut = slice(frame * rows_here, (frame + 1) * rows_here)
            sums.append(jnp.sum(flattened[cut], axis=0, keepdims=True))
            lines_y.append(jnp.sum(flattened[cut] * yc, axis=0, keepdims=True))
        blank = [jnp.zeros((8 - frames, width), F32)]
        slope_y = jnp.sum(jnp.concatenate(lines_y + blank, axis=0) * in_core, axis=1, keepdims=True)
        slope_x = jnp.sum(jnp.concatenate(sums + blank, axis=0) * xc, axis=1, keepdims=True)
        own.append(jnp.where(lane == 0, slope_y, jnp.where(lane == 1, slope_x, 0.0)))
        return split(flattened)

    def finish(tile, one):
        means, centred = [], []
        for frame in range(frames):
            cut = slice(frame * rows_here, (frame + 1) * rows_here)
            mean = jnp.sum(one[cut], axis=0, keepdims=True)
            mean = jnp.sum(mean, axis=1, keepdims=True) * (1.0 / (rows_here * half_w))
            means.append(mean)
            centred.append(one[cut] - mean)
        centred = jnp.concatenate(centred, axis=0)
        for part in range(half_w // 128):
            columns = centred[:, part * 128 : (part + 1) * 128]
            out_ref[tile, part * lines : (part + 1) * lines] = columns.astype(BF16)
        mean = jnp.concatenate(means + [jnp.zeros((8 - frames, 1), F32)], axis=0)
        packed = own[tile] + jnp.where(lane == 6, mean, 0.0)
        if tile > 0:
            packed += pltpu.roll(own[tile - 1], 2, 1)
        if tile < tiles - 1:
            packed += pltpu.roll(own[tile + 1], 4, 1)
        out_ref[tile, half_w // 128 * lines :] = parts_rows(packed)

    part_tiles = max(tiles // 2, 1)
    waiting = None
    for begin in range(0, tiles, part_tiles):
        both = [windowed(tile) for tile in range(begin, begin + part_tiles)]
        high = jnp.concatenate([pair[0] for pair in both], axis=0)
        low = jnp.concatenate([pair[1] for pair in both], axis=0)
        if waiting is not None:
            finish(*waiting)
        narrow = mm(high, lc_hi) + mm(high, lc_lo) + mm(low, lc_hi)
        for number in range(part_tiles):
            one = (begin + number, narrow[number * lines : (number + 1) * lines])
            if number == part_tiles - 1 and begin + part_tiles < tiles:
                waiting = one
            else:
                finish(*one)
        done = begin + part_tiles - (1 if begin + part_tiles < tiles else 0)
        first = max(begin - 1, 0)
        span = pl.ds(first, done - first)
        store = pltpu.make_async_copy(out_ref.at[span], out_hbm.at[span], sems.at[begin // part_tiles])
        store.start()
        stores.append(store)
    for store in stores:
        store.wait()


def strips(dequantized, gains, where, lc, frames, core, margin):
    tiles, lines, _ = dequantized.shape
    shape = (tiles, lines * (lc.shape[1] // 128) + 16, 128)
    return pl.pallas_call(
        functools.partial(strips_kernel, frames=frames, core=core, margin=margin),
        out_shape=jax.ShapeDtypeStruct(shape, BF16),
        in_specs=[pl.BlockSpec(memory_space=SMEM)] + vmem_spec(3),
        out_specs=pl.BlockSpec(memory_space=pltpu.HBM),
        scratch_shapes=[pltpu.VMEM(shape, BF16), pltpu.SemaphoreType.DMA((2,))],
        compiler_params=pltpu.CompilerParams(vmem_limit_bytes=LIMIT),
        name="strips",
    )(where, dequantized, gains, np.concatenate(two_parts(lc)))


def box_area(top, left, band_rows, band_cols):
    row = top // 8 * 8
    col = left // 128 * 128
    area = (
        pl.ds(pl.multiple_of(row, 8), band_rows + 8),
        pl.ds(pl.multiple_of(col, 128), band_cols + 128),
    )
    return area, top - row, left - col


def field_kernel(
    led_row, led_col, patterns, spec_ref, pupil_ref, cols_ref, rows_ref,
    rows_hbm, small_hbm, field_ref, estimate_ref, rows_out, small_out, wide, bright, sems, *, group,
):
    leds, half_h, half_w = bright.shape
    loads = [
        pltpu.make_async_copy(rows_hbm, rows_out, sems.at[0]),
        pltpu.make_async_copy(small_hbm, small_out, sems.at[1]),
    ]
    for load in loads:
        load.start()
    band_rows, band_cols = pupil_ref.shape[1:]
    width = spec_ref.shape[2]
    depth = 2 * band_cols
    wide[...] = jnp.zeros_like(wide)
    wide[:, : spec_ref.shape[1], :width] = spec_ref[...]

    def some(step, carry):
        boxes = []
        for place in range(group):
            led = step * group + place
            area, down, right = box_area(led_row[led], led_col[led], band_rows, band_cols)
            back = lax.rem(2 * band_cols - right, 2 * band_cols)
            up = lax.rem(band_rows + 8 - down, band_rows + 8)
            parts = []
            for part in range(2):
                strip = pltpu.roll(wide[(part, *area)], back, 1)
                parts.append(pltpu.roll(strip[:, :band_cols], up, 0)[:band_rows])
            lit_re = pupil_ref[0] * parts[0] - pupil_ref[1] * parts[1]
            lit_im = pupil_ref[0] * parts[1] + pupil_ref[1] * parts[0]
            boxes.append(jnp.concatenate([lit_re, lit_im], axis=1))
        high, low = split(jnp.concatenate(boxes, axis=0))
        cols_hi, cols_lo = cols_ref[:depth], cols_ref[depth:]
        spread = mm(high, cols_hi) + mm(high, cols_lo) + mm(low, cols_hi)
        for place in range(group):
            one = spread[place * band_rows : (place + 1) * band_rows]
            high, low = split(jnp.concatenate([one[:, :half_w], one[:, half_w:]], axis=0))
            field = mm(rows_ref[...], jnp.concatenate([high, low, high], axis=0))
            field_ref[step * group + place] = field
            bright[step * group + place] = field[:half_h] ** 2 + field[half_h:] ** 2
        return carry

    lax.fori_loop(0, leds // group, some, 0)

    def one_frame(frame, carry):
        total = bright[patterns[0, frame]]
        for lit in range(1, patterns.shape[0]):
            total += bright[patterns[lit, frame]]
        estimate_ref[frame] = total
        return carry

    lax.fori_loop(0, patterns.shape[1], one_frame, 0)
    for load in loads:
        load.wait()


def all_fields(spectrum, pupil, patterns, led_row, led_col, tables, handed, group=8):
    rows, cols = tables
    leds = led_row.shape[0]
    _, height, width = spectrum.shape
    half_h, half_w = height // 2, width // 2
    high, low = two_parts(rows)
    return pl.pallas_call(
        functools.partial(field_kernel, group=group),
        out_shape=(
            jax.ShapeDtypeStruct((leds, 2 * half_h, half_w), F32),
            jax.ShapeDtypeStruct((patterns.shape[1], half_h, half_w), F32),
            *(jax.ShapeDtypeStruct(table.shape, table.dtype) for table in handed),
        ),
        in_specs=[pl.BlockSpec(memory_space=SMEM)] * 3
        + vmem_spec(4)
        + [pl.BlockSpec(memory_space=pltpu.HBM)] * 2,
        out_specs=tuple(vmem_spec(4)),
        scratch_shapes=[
            pltpu.VMEM((2, height + 8, width + 128), F32),
            pltpu.VMEM((leds, half_h, half_w), F32),
            pltpu.SemaphoreType.DMA((2,)),
        ],
        compiler_params=pltpu.CompilerParams(vmem_limit_bytes=LIMIT),
        cost_estimate=pl.CostEstimate(
            flops=8_000_000_000, bytes_accessed=16_000_000, transcendentals=0
        ),
        name="fields",
    )(
        led_row, led_col, patterns, spectrum, pupil, np.concatenate(two_parts(cols)),
        np.concatenate([high, high, low], axis=1),
        *(pltpu.with_memory_space_constraint(jnp.asarray(t), pltpu.HBM) for t in handed),
    )


def window_kernel(dq_ref, rows_ref, small_ref, window_ref, *, frames, core):
    slabs, lines, _ = dq_ref.shape
    half_h, half_w = rows_ref.shape[0], window_ref.shape[1]
    halves = half_w // 128
    lines = (lines - 16) // halves
    lr_sum, line = small_ref[:half_h, :128], small_ref[half_h:]
    rows_here = lines // frames
    height = slabs * rows_here
    over_y = 1.0 / (core * (height * (height * height - 1) / 12.0))
    over_x = 1.0 / (height * (core * (core * core - 1) / 12.0))
    lane = lax.broadcasted_iota(jnp.int32, (8, 128), 1)
    notes = [rows_value(dq_ref[slab, halves * lines :]) for slab in range(slabs)]
    slopes = functools.reduce(jnp.add, notes)
    slopes = slopes * jnp.where(lane % 2 == 0, over_y, over_x)
    slab_means = jnp.zeros((8, 128), F32)
    for slab in range(slabs):
        slab_means = jnp.where(lane == slab, notes[slab][:, 6:7], slab_means)
    values = []
    for slab in range(slabs):
        parts = [dq_ref[slab, part * lines : (part + 1) * lines] for part in range(halves)]
        values.append(jnp.concatenate(parts, axis=1))
    if rows_here % 16:
        values = [value.astype(F32) for value in values]
    means = []
    for frame in range(frames):
        cut = slice(frame * rows_here, (frame + 1) * rows_here)
        whole = jnp.concatenate([v[cut] for v in values], axis=0).astype(BF16)
        window = mm(rows_ref[...], jnp.concatenate([whole, whole], axis=0))
        level = jnp.sum(lr_sum * slab_means[frame : frame + 1], axis=1, keepdims=True)
        window = window + level
        tilt_y, tilt_x = 0.0, 0.0
        for side in range(3):
            tilt_y += line[2 * side : 2 * side + 1] * slopes[frame : frame + 1, 2 * side : 2 * side + 1]
            tilt_x += line[2 * side + 1 : 2 * side + 2] * slopes[frame : frame + 1, 2 * side + 1 : 2 * side + 2]
        window = window - lr_sum[:, 127:128] * tilt_y - tilt_x
        mean = jnp.sum(window, axis=0, keepdims=True)
        mean = jnp.sum(mean, axis=1, keepdims=True) * (1.0 / (half_h * half_w))
        means.append(jnp.broadcast_to(mean, (1, 128)))
        window_ref[frame * half_h : (frame + 1) * half_h] = (window - mean).astype(BF16)
    means = jnp.concatenate(means + [jnp.zeros((8 - frames, 128), F32)], axis=0)
    notes = parts_rows(means)
    window_ref[frames * half_h :] = jnp.concatenate([notes] * halves, axis=1)


def tilt_lines(width, margin, core, lc):
    local = np.arange(width) - margin
    lines = []
    for begin, end, shift in ((0, core, 0), (-margin, 0, core), (core, core + margin, -core)):
        on = (local >= begin) & (local < end)
        lines.append(on.astype(np.float64) @ lc)
        lines.append(((local + shift - (core - 1) / 2.0) * on) @ lc)
    return np.stack(lines + lines[:2])


def window_tables(tiles, passes, margin, core):
    lr, lc = passes
    half_h, height = lr.shape
    sums = np.zeros((half_h, lc.shape[1]))
    sums[:, :tiles] = lr.reshape(half_h, tiles, height // tiles).sum(axis=2)
    sums[:, 127] = lr @ (np.arange(height) - (height - 1) / 2.0)
    small = np.concatenate([sums, tilt_lines(lc.shape[0], margin, core, lc)])
    return np.concatenate(two_parts(lr), axis=1), small.astype(np.float32)


def windows(arrived, rows, small, frames, core):
    half_h, half_w = rows.shape[0], small.shape[1]
    return pl.pallas_call(
        functools.partial(window_kernel, frames=frames, core=core),
        out_shape=jax.ShapeDtypeStruct((frames * half_h + 16, half_w), BF16),
        in_specs=vmem_spec(3),
        out_specs=pl.BlockSpec(memory_space=VMEM),
        compiler_params=pltpu.CompilerParams(vmem_limit_bytes=LIMIT),
        name="windows",
    )(arrived, rows, small)


def add_frame(weight, patterns, frame, value):
    for lit in range(patterns.shape[0]):
        weight[patterns[lit, frame]] += value


def fetch_kernel(patterns, where, estimate_ref, window, field_hbm, field_ref, weight, sem):
    load = pltpu.make_async_copy(field_hbm, field_ref, sem)
    load.start()
    weight[...] = jnp.zeros_like(weight)
    frames, half_h, _ = estimate_ref.shape
    frames_here = window.shape[0] // half_h

    def one_frame(frame, carry):
        add_frame(weight, patterns, frame, estimate_ref[frame])
        return carry

    lax.fori_loop(0, frames, one_frame, 0)
    means = rows_value(window[frames_here * half_h :])
    for place in range(frames_here):
        value = window[place * half_h : (place + 1) * half_h].astype(F32)
        value = -means[place : place + 1, 0:1] - value
        add_frame(weight, patterns, where[0] * frames_here + place, value)
    load.wait()


def fetch(field, estimate, window, patterns, where):
    leds = field.shape[0]
    return pl.pallas_call(
        fetch_kernel,
        out_shape=(
            jax.ShapeDtypeStruct(field.shape, F32),
            jax.ShapeDtypeStruct((leds, *estimate.shape[1:]), F32),
        ),
        in_specs=[pl.BlockSpec(memory_space=SMEM)] * 2
        + vmem_spec(2)
        + [pl.BlockSpec(memory_space=pltpu.HBM)],
        out_specs=tuple(vmem_spec(2)),
        scratch_shapes=[pltpu.SemaphoreType.DMA],
        compiler_params=pltpu.CompilerParams(vmem_limit_bytes=LIMIT),
        cost_estimate=pl.CostEstimate(flops=0, bytes_accessed=16_000_000, transcendentals=0),
        name="fetch",
    )(patterns, where, estimate, window, pltpu.with_memory_space_constraint(field, pltpu.HBM))


def across(left, right):
    dims = (((1,), (1,)), ((), ()))
    return lax.dot_general(left, right, dims, preferred_element_type=F32)


def update_kernel(
    led_row, led_col, patterns, where, field_ref, weight_in, w1, w2, w3,
    spec_ref, pupil_ref, small_ref, big_hbm,
    fresh_hbm, high_ref, low_ref, first_ref, second_ref, weight,
    grads, fresh_ref, big, big_sem, fresh_sem, *, group,
):
    leds, half_h, half_w = weight.shape
    band_rows, band_cols = pupil_ref.shape[1:]
    height, width = spec_ref.shape[1:]
    frames_here = w1.shape[0] // half_h
    is_odd = where[1] == 1
    big_load = pltpu.make_async_copy(big_hbm, big, big_sem)
    big_load.start()
    grads[...] = jnp.zeros_like(grads)
    for slot, window in enumerate((w1, w2, w3)):
        owner = jnp.bitwise_xor(where[0], slot + 1)
        means = rows_value(window[frames_here * half_h :])
        for place in range(frames_here):
            value = window[place * half_h : (place + 1) * half_h].astype(F32)
            value = -means[place : place + 1, 0:1] - value
            add_frame(weight, patterns, owner * frames_here + place, value)

    table_rows = 2 * band_rows

    def some(step, carry):
        left_rows = small_ref[: 2 * table_rows]
        cols_hi = small_ref[2 * table_rows : 2 * table_rows + 2 * half_w]
        cols_lo = small_ref[2 * table_rows + 2 * half_w :]
        backs = []
        for place in range(group):
            q = weight[step * group + place]
            field = field_ref[step * group + place]
            high, low = split(jnp.concatenate([field[:half_h] * q, field[half_h:] * q], axis=0))
            both = mm(left_rows, high)
            back = both[:table_rows] + both[table_rows:] + mm(left_rows[:table_rows], low)
            backs.append(jnp.concatenate([back[:band_rows], back[band_rows:]], axis=1))
        high, low = split(jnp.concatenate(backs, axis=0))
        boxes = mm(high, cols_hi) + mm(high, cols_lo) + mm(low, cols_hi)
        for place in range(group):
            led = step * group + place
            one = boxes[place * band_rows : (place + 1) * band_rows]
            back_re, back_im = one[:, :band_cols], one[:, band_cols:]
            parts = (
                pupil_ref[0] * back_re + pupil_ref[1] * back_im,
                pupil_ref[0] * back_im - pupil_ref[1] * back_re,
            )
            area, down, right = box_area(led_row[led], led_col[led], band_rows, band_cols)
            for part in range(2):
                filled = jnp.concatenate([parts[part], jnp.zeros((8, band_cols), F32)], axis=0)
                filled = pltpu.roll(filled, down, 0)
                filled = jnp.concatenate([filled, jnp.zeros((band_rows + 8, 128), F32)], axis=1)
                grads[(part, *area)] += pltpu.roll(filled, right, 1)
        return carry

    lax.fori_loop(0, leds // group, some, 0)
    fresh_re = spec_ref[0] - (4.0 * STEP) * grads[0, :height, :width]
    fresh_im = spec_ref[1] - (4.0 * STEP) * grads[1, :height, :width]
    fresh_ref[0] = fresh_re
    fresh_ref[1] = fresh_im
    store = pltpu.make_async_copy(fresh_ref, fresh_hbm, fresh_sem)
    store.start()
    re_hi, re_lo = split(fresh_re)
    im_hi, im_lo = split(fresh_im)
    high = jnp.concatenate([re_hi, im_hi], axis=0)
    low = jnp.concatenate([re_lo, im_lo], axis=0)
    big_load.wait()
    full = 2 * height
    rows_hi, rows_lo = big[:full], big[full : 2 * full]
    spread = mm(rows_hi, high) + mm(rows_lo, high) + mm(rows_hi, low)
    high, low = split(jnp.concatenate([spread[:height], spread[height:]], axis=1))
    high_ref[...] = high
    low_ref[...] = low
    side_rows = 2 * first_ref.shape[0]
    side = big[2 * full :]
    side_hi = jnp.concatenate([side[:side_rows], side[side_rows : 2 * side_rows]], axis=1)
    side_lo = jnp.concatenate([side[2 * side_rows : 3 * side_rows], side[3 * side_rows :]], axis=1)
    sides = across(side_hi, high) + across(side_lo, high) + across(side_hi, low)
    half = side_rows // 2
    to_left, to_right = sides[:half], sides[half:]
    first_ref[...] = jnp.where(is_odd, to_left, to_right)
    second_ref[...] = jnp.where(is_odd, to_right, to_left)
    store.wait()


def update(
    field, weight, window_parts, spectrum, pupil, patterns, led_row, led_col, where, tables,
    margin, group=8,
):
    rows, cols = tables
    leds = led_row.shape[0]
    _, height, width = spectrum.shape
    half_h, half_w = height // 2, width // 2
    fr_re, fr_im = wave(np.arange(height), np.arange(height) - height // 2, height, height)
    full_rows = np.block([[fr_re, -fr_im], [fr_im, fr_re]])
    side_places = np.concatenate([np.arange(margin), width - margin + np.arange(margin)])
    fc_re, fc_im = wave(side_places, np.arange(width) - width // 2, width, width)
    from_re = np.concatenate([fc_re[:margin], fc_im[:margin], fc_re[margin:], fc_im[margin:]])
    from_im = np.concatenate([-fc_im[:margin], fc_re[:margin], -fc_im[margin:], fc_re[margin:]])
    sides = [two_parts(from_re), two_parts(from_im)]
    big = np.concatenate(
        [*two_parts(full_rows), sides[0][0], sides[1][0], sides[0][1], sides[1][1]]
    )
    small = np.concatenate([*two_parts(rows.T), *two_parts(cols.T)])
    out_shape = (
        jax.ShapeDtypeStruct(spectrum.shape, F32),
        jax.ShapeDtypeStruct((height, 2 * width), BF16),
        jax.ShapeDtypeStruct((height, 2 * width), BF16),
        jax.ShapeDtypeStruct((2 * margin, height), F32),
        jax.ShapeDtypeStruct((2 * margin, height), F32),
        jax.ShapeDtypeStruct(weight.shape, F32),
    )
    return pl.pallas_call(
        functools.partial(update_kernel, group=group),
        out_shape=out_shape,
        in_specs=[pl.BlockSpec(memory_space=SMEM)] * 4
        + vmem_spec(8)
        + [pl.BlockSpec(memory_space=pltpu.HBM)],
        out_specs=(pl.BlockSpec(memory_space=pltpu.HBM), *vmem_spec(5)),
        input_output_aliases={5: 5},
        scratch_shapes=[
            pltpu.VMEM((2, height + 8, width + 128), F32),
            pltpu.VMEM(spectrum.shape, F32),
            pltpu.VMEM(big.shape, BF16),
            pltpu.SemaphoreType.DMA,
            pltpu.SemaphoreType.DMA,
        ],
        compiler_params=pltpu.CompilerParams(vmem_limit_bytes=LIMIT),
        name="update",
    )(
        led_row, led_col, patterns, where, field, weight, *window_parts, spectrum, pupil, small,
        pltpu.with_memory_space_constraint(jnp.asarray(big), pltpu.HBM),
    )[:5]


def object_kernel(high_ref, low_ref, table_ref, out_hbm, edges_ref, out, sems):
    core = out.shape[1]
    margin = edges_ref.shape[2]
    width = high_ref.shape[1] // 2
    stores = []
    for part in range(2):
        total = None
        for other in range(2):
            rows = slice((part ^ other) * core, (part ^ other) * core + core)
            more = slice(rows.start + 2 * core, rows.stop + 2 * core)
            cut = slice(other * width, (other + 1) * width)
            z_hi, z_lo = high_ref[:, cut], low_ref[:, cut]
            one = across(table_ref[rows], z_hi) + across(table_ref[more], z_hi)
            one = one + across(table_ref[rows], z_lo)
            if total is None:
                total = one
            else:
                total = total + one if part else total - one
        out[part] = total
        edges_ref[part, 0] = total[:margin]
        edges_ref[part, 1] = total[core - margin :]
        store = pltpu.make_async_copy(out.at[part], out_hbm.at[part], sems.at[part])
        store.start()
        stores.append(store)
    for store in stores:
        store.wait()


def object_core(high, low, margin, core):
    height, width = high.shape[0], high.shape[1] // 2
    col_re, col_im = wave(margin + np.arange(core), np.arange(width) - width // 2, width, width)
    table = np.concatenate(two_parts(np.concatenate([col_re, col_im])))
    return pl.pallas_call(
        object_kernel,
        out_shape=(
            jax.ShapeDtypeStruct((2, core, height), F32),
            jax.ShapeDtypeStruct((2, 2, margin, height), F32),
        ),
        in_specs=vmem_spec(3),
        out_specs=(pl.BlockSpec(memory_space=pltpu.HBM), pl.BlockSpec(memory_space=VMEM)),
        scratch_shapes=[pltpu.VMEM((2, core, height), F32), pltpu.SemaphoreType.DMA((2,))],
        compiler_params=pltpu.CompilerParams(vmem_limit_bytes=LIMIT),
        cost_estimate=pl.CostEstimate(
            flops=3_000_000_000, bytes_accessed=5_000_000, transcendentals=0
        ),
        name="object",
    )(high, low, table)


def blend_kernel(where, first_ref, second_ref, edges_ref, core_hbm, out_hbm, mixed, sems):
    tile = where[2]
    is_odd = where[1] == 1
    margin, core = edges_ref.shape[2], out_hbm.shape[1]
    k = lax.broadcasted_iota(jnp.int32, (margin, 1), 0).astype(F32)
    span = 2.0 * margin
    from_left = jnp.where(is_odd, first_ref[...], second_ref[...])
    from_right = jnp.where(is_odd, second_ref[...], first_ref[...])
    sides = (
        ((k + margin + 0.5) / span, (margin - k - 0.5) / span, tile > 0, from_left, 0),
        (
            (span - k - 0.5) / span, (k + 0.5) / span, tile < where[3] - 1, from_right,
            core - margin,
        ),
    )
    stores = []
    for side, (own_w, other_w, has_other, other, begin) in enumerate(sides):
        own_w = jnp.where(has_other, own_w, 1.0)
        other_w = jnp.where(has_other, other_w, 0.0)
        for part in range(2):
            cut = slice(part * margin, (part + 1) * margin)
            mixed[part, side] = edges_ref[part, side] * own_w + other[cut] * other_w
            store = pltpu.make_async_copy(
                mixed.at[part, side], out_hbm.at[part, pl.ds(begin, margin)],
                sems.at[2 * side + part],
            )
            store.start()
            stores.append(store)
    for store in stores:
        store.wait()


def blend(core_part, edges, first, second, where):
    return pl.pallas_call(
        blend_kernel,
        out_shape=jax.ShapeDtypeStruct(core_part.shape, F32),
        in_specs=[pl.BlockSpec(memory_space=SMEM)]
        + vmem_spec(3)
        + [pl.BlockSpec(memory_space=pltpu.HBM)],
        out_specs=pl.BlockSpec(memory_space=pltpu.HBM),
        input_output_aliases={4: 0},
        scratch_shapes=[pltpu.VMEM(edges.shape, F32), pltpu.SemaphoreType.DMA((4,))],
        compiler_params=pltpu.CompilerParams(vmem_limit_bytes=LIMIT),
        name="blend",
    )(where, first, second, edges, core_part)


def body(raw, scales, flat, spectrum, pupil, patterns, led_row, led_col):
    height, core = flat.shape
    margin = OV // 2
    width = core + OV
    tiles = lax.axis_size("tile")
    tile = lax.axis_index("tile")
    grp = lax.axis_index("grp")
    frames_here = raw.shape[0]
    band_rows, band_cols = pupil.shape[1:]
    spectrum_tile = spectrum[0]
    patterns = patterns.T
    odd = lax.rem(tile, 2)
    where = jnp.stack([grp, odd, tile, jnp.int32(tiles)]).astype(jnp.int32)

    swap_a = [(i, i ^ 1) for i in range(tiles)]
    swap_b = [(i, ((i + 1) ^ 1) - 1) for i in range(1, tiles - 1)]

    def neighbours(for_a, for_b):
        return lax.ppermute(for_a, "tile", swap_a), lax.ppermute(for_b, "tile", swap_b)

    tables = stacked_tables(height, width, band_rows, band_cols)
    passes = (low_pass(height, band_rows), low_pass(width, band_cols).T)

    by_rows = gains_by_rows(flat.T, tiles, width)
    dequantized = dequantize(raw, scales, by_rows, tiles, core, margin)
    gains = lax.all_to_all(by_rows, "tile", split_axis=0, concat_axis=0, tiled=True)
    narrow = strips(dequantized, gains, where, passes[1], frames_here, core, margin)
    arrived = lax.all_to_all(narrow, "tile", split_axis=0, concat_axis=0, tiled=True)
    handed = window_tables(tiles, passes, margin, core)
    field, estimate, rows, small = all_fields(
        spectrum_tile, pupil, patterns, led_row, led_col, tables, handed
    )
    window = windows(arrived, rows, small, frames_here, core)
    field, weight = fetch(field, estimate, window, patterns, where)

    swap_core = [(i, i ^ 1) for i in range(4)]
    swap_chip = [(i, i ^ 2) for i in range(4)]
    other = functools.partial(lax.ppermute, axis_name="grp")
    window_2 = other(window, perm=swap_chip)
    window_1 = other(window, perm=swap_core)
    window_2, field, weight = lax.optimization_barrier((window_2, field, weight))
    window_3 = other(window_2, perm=swap_core)

    fresh, high, low, for_a, for_b = update(
        field, weight, (window_1, window_2, window_3), spectrum_tile, pupil, patterns,
        led_row, led_col, where, tables, margin,
    )
    side_a, side_b = neighbours(for_a, for_b)
    core_part, edges = object_core(high, low, margin, core)
    stitched = blend(core_part, edges, side_a, side_b, where)
    return fresh[None], jnp.transpose(stitched, (0, 2, 1))


def solution(mesh):
    return jax.shard_map(
        body,
        mesh=mesh,
        in_specs=(
            P("grp", "tile", None),
            P("grp", "tile", None),
            P(None, "tile"),
            P("tile", None, None, None),
            P(),
            P(),
            P(),
            P(),
        ),
        out_specs=(P("tile", None, None, None), P(None, None, "tile")),
        check_vma=False,
    )
```

```python
import functools
import math

import jax
import jax.numpy as jnp
import ml_dtypes
import numpy as np
from jax import lax
from jax.experimental import pallas as pl
from jax.experimental.pallas import tpu as pltpu
from jax.sharding import PartitionSpec as P

OV = 32
BC = 32
STEP = 0.02
F32 = jnp.float32
BF16 = jnp.bfloat16
VMEM = pltpu.VMEM
SMEM = pltpu.SMEM
LIMIT = 30 << 20


def two_parts(table):
    table = np.asarray(table, np.float64)
    high = table.astype(ml_dtypes.bfloat16)
    low = (table - high.astype(np.float64)).astype(ml_dtypes.bfloat16)
    return high, low


def wave(places, freqs, length, norm):
    turns = np.outer(places, freqs) % length
    angle = turns * (2.0 * math.pi / length)
    return np.cos(angle) / math.sqrt(norm), np.sin(angle) / math.sqrt(norm)


def pairs(length):
    first = np.arange(1, length // 2, 2)
    return np.concatenate([first, length - first])


def low_pass(length, band):
    places = pairs(length)[:, None] - np.arange(length)[None, :]
    total = np.ones(places.shape)
    for freq in range(1, band):
        total += 2.0 * np.cos(2.0 * math.pi * ((freq * places) % length) / length)
    return total / length


def stacked_tables(height, width, band_rows, band_cols):
    row_re, row_im = wave(
        pairs(height), np.arange(band_rows) - band_rows // 2, height, band_rows
    )
    rows = np.block([[row_re, -row_im], [row_im, row_re]])
    col_re, col_im = wave(
        np.arange(band_cols) - band_cols // 2, pairs(width), width, band_cols
    )
    cols = np.block([[col_re, col_im], [-col_im, col_re]])
    half_rows, half_cols = height // 4, width // 4
    high, low = two_parts(np.concatenate([row_re[:half_rows], row_im[:half_rows]]).T)
    back_rows = np.block([[high, high], [low, np.zeros_like(low)]])
    back_cols = np.concatenate(
        two_parts(np.concatenate([col_re[:, :half_cols], col_im[:, :half_cols]], axis=1).T), axis=1
    )
    return rows, cols, back_rows, back_cols


def split(values):
    high = values.astype(BF16)
    return high, (values - high.astype(F32)).astype(BF16)


def mm(left, right):
    return jnp.dot(left, right, preferred_element_type=F32)


def vmem_spec(count):
    return [pl.BlockSpec(memory_space=VMEM)] * count


def lane_blocks(values):
    return [values[:, begin : begin + 128] for begin in range(0, values.shape[1], 128)]


def parts_rows(values):
    high = values.astype(BF16).astype(F32)
    return jnp.concatenate([high, values - high], axis=0).astype(BF16)


def rows_value(rows):
    rows = rows.astype(F32)
    return rows[:8, :128] + rows[8:, :128]


def gains_kernel(flat_hbm, out_hbm, flat, out, sems, out_sems):
    core, height = flat_hbm.shape
    tiles, rows_here, width = out_hbm.shape
    spans = [(begin, min(128, core - begin)) for begin in range(0, core, 128)]
    loads = []
    for number, (begin, length) in enumerate(spans):
        part = pl.ds(begin, length)
        load = pltpu.make_async_copy(flat_hbm.at[part], flat.at[part], sems.at[number])
        load.start()
        loads.append(load)
    stores = []
    for number, (load, (begin, length)) in enumerate(zip(loads, spans)):
        load.wait()
        gains = flat[begin : begin + length] - 1.0
        if length < 128:
            gains = jnp.concatenate([gains, jnp.zeros((128 - length, height), F32)], axis=0)
        by_rows = jnp.transpose(gains, (1, 0)).reshape(tiles, rows_here, 128)
        out[:, :, begin : begin + 128] = by_rows.astype(BF16)
        part = (slice(None), slice(None), pl.ds(begin, 128))
        store = pltpu.make_async_copy(out.at[part], out_hbm.at[part], out_sems.at[number])
        store.start()
        stores.append(store)
    for store in stores:
        store.wait()


def gains_by_rows(flat, tiles, width):
    core, height = flat.shape
    return pl.pallas_call(
        gains_kernel,
        out_shape=jax.ShapeDtypeStruct((tiles, height // tiles, width), BF16),
        in_specs=[pl.BlockSpec(memory_space=pltpu.HBM)],
        out_specs=pl.BlockSpec(memory_space=pltpu.HBM),
        scratch_shapes=[
            pltpu.VMEM((core, height), F32),
            pltpu.VMEM((tiles, height // tiles, width), BF16),
            pltpu.SemaphoreType.DMA((-(-core // 128),)),
            pltpu.SemaphoreType.DMA((-(-core // 128),)),
        ],
        compiler_params=pltpu.CompilerParams(vmem_limit_bytes=LIMIT),
        name="gains",
    )(pltpu.with_memory_space_constraint(flat, pltpu.HBM))


def dequantize_kernel(raw_ref, scales_ref, after, out_ref, *, core, margin):
    lines, strip = raw_ref.shape
    coarse_rows, coarse_cols = scales_ref.shape
    tiles, _, width = out_ref.shape
    ratio = lines // coarse_rows
    row = lax.broadcasted_iota(jnp.int32, (lines, coarse_rows), 0)
    pick = lax.broadcasted_iota(jnp.int32, (lines, coarse_rows), 1)
    spread_rows = (row // ratio == pick).astype(F32).astype(BF16)
    factors = mm(spread_rows, scales_ref[...])
    wide = (coarse_cols // 128 + 1) * 128
    factors = jnp.concatenate([factors, jnp.zeros((lines, wide - coarse_cols), F32)], axis=1)

    blocks = []
    for tile in range(tiles):
        begin = (tile * core - margin) // BC
        blocks.append(pltpu.roll(factors, -begin % wide, 1)[:, :128].astype(BF16))
    block = lax.broadcasted_iota(jnp.int32, (128, width), 0)
    place = lax.broadcasted_iota(jnp.int32, (128, width), 1) + (-margin) % BC
    inside = (place >= block * BC) & (place < (block + 1) * BC)
    scales = mm(jnp.concatenate(blocks, axis=0), inside.astype(F32).astype(BF16))
    for tile in range(tiles):
        start = tile * core - margin
        base = max(start, 0) // 128 * 128
        span = min(width + 128, strip - base)
        codes = raw_ref[:, base : base + span].astype(F32)
        turn = (base - start) % span
        if turn:
            codes = pltpu.roll(codes, turn, 1)
        out_ref[tile] = codes[:, :width] * scales[tile * lines : (tile + 1) * lines]


def dequantize(raw, scales, after, tiles, core, margin):
    frames, rows_here, strip = raw.shape
    return pl.pallas_call(
        functools.partial(dequantize_kernel, core=core, margin=margin),
        out_shape=jax.ShapeDtypeStruct((tiles, frames * rows_here, core + 2 * margin), F32),
        in_specs=vmem_spec(2) + [pl.BlockSpec(memory_space=pl.ANY)],
        out_specs=pl.BlockSpec(memory_space=VMEM),
        compiler_params=pltpu.CompilerParams(vmem_limit_bytes=LIMIT),
        cost_estimate=pl.CostEstimate(
            flops=2_000_000_000, bytes_accessed=4_000_000, transcendentals=0
        ),
        name="dequantize",
    )(raw.reshape(frames * rows_here, strip), scales.reshape(-1, scales.shape[-1]), after)


def strips_kernel(where, dq_ref, gains_ref, lc_ref, out_hbm, out_ref, sems, *, frames, core, margin):
    tiles, lines, width = dq_ref.shape
    half_w = lc_ref.shape[1]
    rows_here = lines // frames
    line = lax.broadcasted_iota(jnp.int32, (1, width), 1)
    in_core = ((line >= margin) & (line < margin + core)).astype(F32)
    xc = (line.astype(F32) - margin - (core - 1) / 2.0) * in_core
    first_row = (where[2] * rows_here).astype(F32)
    height = rows_here * tiles
    yc = lax.broadcasted_iota(jnp.int32, (rows_here, 1), 0).astype(F32)
    yc = yc + (first_row - (height - 1) / 2.0)
    lane = lax.broadcasted_iota(jnp.int32, (8, 128), 1)
    narrow_lane = lax.broadcasted_iota(jnp.int32, (1, 128), 1)

    lc_hi, lc_lo = lc_ref[:width], lc_ref[width:]
    own, stores = [], []

    def windowed(tile):
        gains = pltpu.roll(gains_ref[tile].astype(F32), margin, 1)
        if tile > 0:
            end = gains_ref[tile - 1][:, width - 128 :].astype(F32)
            end = pltpu.roll(end, (2 * margin) + margin, 1)
            end = jnp.where(narrow_lane < margin, end, 0.0)
            gains = jnp.concatenate([gains[:, :128] + end, gains[:, 128:]], axis=1)
        if tile < tiles - 1:
            end = gains_ref[tile + 1][:, :128].astype(F32)
            end = pltpu.roll(end, 128 - margin, 1)
            end = jnp.where(narrow_lane >= 128 - margin, end, 0.0)
            gains = jnp.concatenate(
                [gains[:, : width - 128], gains[:, width - 128 :] + end], axis=1
            )
        gains = jnp.concatenate([gains + 1.0] * frames, axis=0)
        flattened = dq_ref[tile] * gains
        sums, lines_y = [], []
        for frame in range(frames):
            cut = slice(frame * rows_here, (frame + 1) * rows_here)
            sums.append(jnp.sum(flattened[cut], axis=0, keepdims=True))
            lines_y.append(jnp.sum(flattened[cut] * yc, axis=0, keepdims=True))
        blank = [jnp.zeros((8 - frames, width), F32)]
        slope_y = jnp.sum(jnp.concatenate(lines_y + blank, axis=0) * in_core, axis=1, keepdims=True)
        slope_x = jnp.sum(jnp.concatenate(sums + blank, axis=0) * xc, axis=1, keepdims=True)
        own.append(jnp.where(lane == 0, slope_y, jnp.where(lane == 1, slope_x, 0.0)))
        return split(flattened)

    def finish(tile, one):
        means, centred = [], []
        for frame in range(frames):
            cut = slice(frame * rows_here, (frame + 1) * rows_here)
            mean = jnp.sum(one[cut], axis=0, keepdims=True)
            mean = jnp.sum(mean, axis=1, keepdims=True) * (1.0 / (rows_here * half_w))
            means.append(mean)
            centred.append(one[cut] - mean)
        centred = jnp.concatenate(centred, axis=0)
        for part in range(half_w // 128):
            columns = centred[:, part * 128 : (part + 1) * 128]
            out_ref[tile, part * lines : (part + 1) * lines] = columns.astype(BF16)
        mean = jnp.concatenate(means + [jnp.zeros((8 - frames, 1), F32)], axis=0)
        packed = own[tile] + jnp.where(lane == 6, mean, 0.0)
        if tile > 0:
            packed += pltpu.roll(own[tile - 1], 2, 1)
        if tile < tiles - 1:
            packed += pltpu.roll(own[tile + 1], 4, 1)
        out_ref[tile, half_w // 128 * lines :] = parts_rows(packed)

    part_tiles = max(tiles // 2, 1)
    waiting = None
    for begin in range(0, tiles, part_tiles):
        both = [windowed(tile) for tile in range(begin, begin + part_tiles)]
        high = jnp.concatenate([pair[0] for pair in both], axis=0)
        low = jnp.concatenate([pair[1] for pair in both], axis=0)
        if waiting is not None:
            finish(*waiting)
        narrow = mm(high, lc_hi) + mm(high, lc_lo) + mm(low, lc_hi)
        for number in range(part_tiles):
            one = (begin + number, narrow[number * lines : (number + 1) * lines])
            if number == part_tiles - 1 and begin + part_tiles < tiles:
                waiting = one
            else:
                finish(*one)
        done = begin + part_tiles - (1 if begin + part_tiles < tiles else 0)
        first = max(begin - 1, 0)
        span = pl.ds(first, done - first)
        store = pltpu.make_async_copy(out_ref.at[span], out_hbm.at[span], sems.at[begin // part_tiles])
        store.start()
        stores.append(store)
    for store in stores:
        store.wait()


def strips(dequantized, gains, where, lc, frames, core, margin):
    tiles, lines, _ = dequantized.shape
    shape = (tiles, lines * (lc.shape[1] // 128) + 16, 128)
    return pl.pallas_call(
        functools.partial(strips_kernel, frames=frames, core=core, margin=margin),
        out_shape=jax.ShapeDtypeStruct(shape, BF16),
        in_specs=[pl.BlockSpec(memory_space=SMEM)] + vmem_spec(3),
        out_specs=pl.BlockSpec(memory_space=pltpu.HBM),
        scratch_shapes=[pltpu.VMEM(shape, BF16), pltpu.SemaphoreType.DMA((2,))],
        compiler_params=pltpu.CompilerParams(vmem_limit_bytes=LIMIT),
        name="strips",
    )(where, dequantized, gains, np.concatenate(two_parts(lc)))


def box_area(top, left, band_rows, band_cols):
    row = top // 8 * 8
    col = left // 128 * 128
    area = (
        pl.ds(pl.multiple_of(row, 8), band_rows + 8),
        pl.ds(pl.multiple_of(col, 128), band_cols + 128),
    )
    return area, top - row, left - col


def field_kernel(
    led_row, led_col, patterns, spec_ref, pupil_ref, cols_ref, rows_ref,
    rows_hbm, small_hbm, field_ref, estimate_ref, rows_out, small_out, wide, bright, sems, *, group,
):
    leds, half_h, half_w = bright.shape
    loads = [
        pltpu.make_async_copy(rows_hbm, rows_out, sems.at[0]),
        pltpu.make_async_copy(small_hbm, small_out, sems.at[1]),
    ]
    for load in loads:
        load.start()
    band_rows, band_cols = pupil_ref.shape[1:]
    width = spec_ref.shape[2]
    depth = 2 * band_cols
    wide[...] = jnp.zeros_like(wide)
    wide[:, : spec_ref.shape[1], :width] = spec_ref[...]

    def some(step, carry):
        boxes = []
        for place in range(group):
            led = step * group + place
            area, down, right = box_area(led_row[led], led_col[led], band_rows, band_cols)
            back = lax.rem(2 * band_cols - right, 2 * band_cols)
            up = lax.rem(band_rows + 8 - down, band_rows + 8)
            parts = []
            for part in range(2):
                strip = pltpu.roll(wide[(part, *area)], back, 1)
                parts.append(pltpu.roll(strip[:, :band_cols], up, 0)[:band_rows])
            lit_re = pupil_ref[0] * parts[0] - pupil_ref[1] * parts[1]
            lit_im = pupil_ref[0] * parts[1] + pupil_ref[1] * parts[0]
            boxes.append(jnp.concatenate([lit_re, lit_im], axis=1))
        high, low = split(jnp.concatenate(boxes, axis=0))
        cols_hi, cols_lo = cols_ref[:depth], cols_ref[depth:]
        spread = mm(high, cols_hi) + mm(high, cols_lo) + mm(low, cols_hi)
        for place in range(group):
            one = spread[place * band_rows : (place + 1) * band_rows]
            high, low = split(jnp.concatenate([one[:, :half_w], one[:, half_w:]], axis=0))
            field = mm(rows_ref[...], jnp.concatenate([high, low, high], axis=0))
            field_ref[step * group + place] = field
            bright[step * group + place] = field[:half_h] ** 2 + field[half_h:] ** 2
        return carry

    lax.fori_loop(0, leds // group, some, 0)

    def one_frame(frame, carry):
        total = bright[patterns[0, frame]]
        for lit in range(1, patterns.shape[0]):
            total += bright[patterns[lit, frame]]
        estimate_ref[frame] = total
        return carry

    lax.fori_loop(0, patterns.shape[1], one_frame, 0)
    for load in loads:
        load.wait()


def all_fields(spectrum, pupil, patterns, led_row, led_col, tables, handed, group=8):
    rows, cols, _, _ = tables
    leds = led_row.shape[0]
    _, height, width = spectrum.shape
    half_h, half_w = height // 2, width // 2
    high, low = two_parts(rows)
    return pl.pallas_call(
        functools.partial(field_kernel, group=group),
        out_shape=(
            jax.ShapeDtypeStruct((leds, 2 * half_h, half_w), F32),
            jax.ShapeDtypeStruct((patterns.shape[1], half_h, half_w), F32),
            *(jax.ShapeDtypeStruct(table.shape, table.dtype) for table in handed),
        ),
        in_specs=[pl.BlockSpec(memory_space=SMEM)] * 3
        + vmem_spec(4)
        + [pl.BlockSpec(memory_space=pltpu.HBM)] * 2,
        out_specs=tuple(vmem_spec(4)),
        scratch_shapes=[
            pltpu.VMEM((2, height + 8, width + 128), F32),
            pltpu.VMEM((leds, half_h, half_w), F32),
            pltpu.SemaphoreType.DMA((2,)),
        ],
        compiler_params=pltpu.CompilerParams(vmem_limit_bytes=LIMIT),
        cost_estimate=pl.CostEstimate(
            flops=8_000_000_000, bytes_accessed=16_000_000, transcendentals=0
        ),
        name="fields",
    )(
        led_row, led_col, patterns, spectrum, pupil, np.concatenate(two_parts(cols)),
        np.concatenate([high, high, low], axis=1),
        *(pltpu.with_memory_space_constraint(jnp.asarray(t), pltpu.HBM) for t in handed),
    )


def window_kernel(dq_ref, rows_ref, small_ref, window_ref, *, frames, core):
    slabs, lines, _ = dq_ref.shape
    half_h, half_w = rows_ref.shape[0], window_ref.shape[1]
    halves = half_w // 128
    lines = (lines - 16) // halves
    lr_sum, line = small_ref[:half_h, :128], small_ref[half_h:]
    rows_here = lines // frames
    height = slabs * rows_here
    over_y = 1.0 / (core * (height * (height * height - 1) / 12.0))
    over_x = 1.0 / (height * (core * (core * core - 1) / 12.0))
    lane = lax.broadcasted_iota(jnp.int32, (8, 128), 1)
    notes = [rows_value(dq_ref[slab, halves * lines :]) for slab in range(slabs)]
    slopes = functools.reduce(jnp.add, notes)
    slopes = slopes * jnp.where(lane % 2 == 0, over_y, over_x)
    slab_means = jnp.zeros((8, 128), F32)
    for slab in range(slabs):
        slab_means = jnp.where(lane == slab, notes[slab][:, 6:7], slab_means)
    values = []
    for slab in range(slabs):
        parts = [dq_ref[slab, part * lines : (part + 1) * lines] for part in range(halves)]
        values.append(jnp.concatenate(parts, axis=1))
    if rows_here % 16:
        values = [value.astype(F32) for value in values]
    means = []
    for frame in range(frames):
        cut = slice(frame * rows_here, (frame + 1) * rows_here)
        whole = jnp.concatenate([v[cut] for v in values], axis=0).astype(BF16)
        window = mm(rows_ref[...], jnp.concatenate([whole, whole], axis=0))
        level = jnp.sum(lr_sum * slab_means[frame : frame + 1], axis=1, keepdims=True)
        window = window + level
        tilt_y, tilt_x = 0.0, 0.0
        for side in range(3):
            tilt_y += line[2 * side : 2 * side + 1] * slopes[frame : frame + 1, 2 * side : 2 * side + 1]
            tilt_x += line[2 * side + 1 : 2 * side + 2] * slopes[frame : frame + 1, 2 * side + 1 : 2 * side + 2]
        window = window - lr_sum[:, 127:128] * tilt_y - tilt_x
        mean = jnp.sum(window, axis=0, keepdims=True)
        mean = jnp.sum(mean, axis=1, keepdims=True) * (1.0 / (half_h * half_w))
        means.append(jnp.broadcast_to(mean, (1, 128)))
        window_ref[frame * half_h : (frame + 1) * half_h] = (window - mean).astype(BF16)
    means = jnp.concatenate(means + [jnp.zeros((8 - frames, 128), F32)], axis=0)
    notes = parts_rows(means)
    window_ref[frames * half_h :] = jnp.concatenate([notes] * halves, axis=1)


def tilt_lines(width, margin, core, lc):
    local = np.arange(width) - margin
    lines = []
    for begin, end, shift in ((0, core, 0), (-margin, 0, core), (core, core + margin, -core)):
        on = (local >= begin) & (local < end)
        lines.append(on.astype(np.float64) @ lc)
        lines.append(((local + shift - (core - 1) / 2.0) * on) @ lc)
    return np.stack(lines + lines[:2])


def window_tables(tiles, passes, margin, core):
    lr, lc = passes
    half_h, height = lr.shape
    sums = np.zeros((half_h, lc.shape[1]))
    sums[:, :tiles] = lr.reshape(half_h, tiles, height // tiles).sum(axis=2)
    sums[:, 127] = lr @ (np.arange(height) - (height - 1) / 2.0)
    small = np.concatenate([sums, tilt_lines(lc.shape[0], margin, core, lc)])
    return np.concatenate(two_parts(lr), axis=1), small.astype(np.float32)


def windows(arrived, rows, small, frames, core):
    half_h, half_w = rows.shape[0], small.shape[1]
    return pl.pallas_call(
        functools.partial(window_kernel, frames=frames, core=core),
        out_shape=jax.ShapeDtypeStruct((frames * half_h + 16, half_w), BF16),
        in_specs=vmem_spec(3),
        out_specs=pl.BlockSpec(memory_space=VMEM),
        compiler_params=pltpu.CompilerParams(vmem_limit_bytes=LIMIT),
        name="windows",
    )(arrived, rows, small)


def add_frame(weight, patterns, frame, value):
    for lit in range(patterns.shape[0]):
        weight[patterns[lit, frame]] += value


def fetch_kernel(patterns, where, estimate_ref, window, field_hbm, field_ref, weight, sem):
    load = pltpu.make_async_copy(field_hbm, field_ref, sem)
    load.start()
    weight[...] = jnp.zeros_like(weight)
    frames, half_h, _ = estimate_ref.shape
    frames_here = window.shape[0] // half_h

    def one_frame(frame, carry):
        add_frame(weight, patterns, frame, estimate_ref[frame])
        return carry

    lax.fori_loop(0, frames, one_frame, 0)
    means = rows_value(window[frames_here * half_h :])
    for place in range(frames_here):
        value = window[place * half_h : (place + 1) * half_h].astype(F32)
        value = -means[place : place + 1, 0:1] - value
        add_frame(weight, patterns, where[0] * frames_here + place, value)
    load.wait()


def fetch(field, estimate, window, patterns, where):
    leds = field.shape[0]
    return pl.pallas_call(
        fetch_kernel,
        out_shape=(
            jax.ShapeDtypeStruct(field.shape, F32),
            jax.ShapeDtypeStruct((leds, *estimate.shape[1:]), F32),
        ),
        in_specs=[pl.BlockSpec(memory_space=SMEM)] * 2
        + vmem_spec(2)
        + [pl.BlockSpec(memory_space=pltpu.HBM)],
        out_specs=tuple(vmem_spec(2)),
        scratch_shapes=[pltpu.SemaphoreType.DMA],
        compiler_params=pltpu.CompilerParams(vmem_limit_bytes=LIMIT),
        cost_estimate=pl.CostEstimate(flops=0, bytes_accessed=16_000_000, transcendentals=0),
        name="fetch",
    )(patterns, where, estimate, window, pltpu.with_memory_space_constraint(field, pltpu.HBM))


def across(left, right):
    dims = (((1,), (1,)), ((), ()))
    return lax.dot_general(left, right, dims, preferred_element_type=F32)


def update_kernel(
    led_row, led_col, patterns, where, field_ref, weight_in, w1, w2, w3,
    spec_ref, pupil_ref, back_ref, big_hbm,
    fresh_hbm, high_ref, low_ref, first_ref, second_ref, weight,
    grads, fresh_ref, big, sides_ref, big_sem, fresh_sems, *, group,
):
    leds, half_h, half_w = weight.shape
    band_rows, band_cols = pupil_ref.shape[1:]
    height, width = spec_ref.shape[1:]
    frames_here = w1.shape[0] // half_h
    is_odd = where[1] == 1
    big_load = pltpu.make_async_copy(big_hbm, big, big_sem)
    big_load.start()
    grads[...] = jnp.zeros_like(grads)
    for slot, window in enumerate((w1, w2, w3)):
        owner = jnp.bitwise_xor(where[0], slot + 1)
        means = rows_value(window[frames_here * half_h :])
        for place in range(frames_here):
            value = window[place * half_h : (place + 1) * half_h].astype(F32)
            value = -means[place : place + 1, 0:1] - value
            add_frame(weight, patterns, owner * frames_here + place, value)

    left_rows = 2 * band_rows
    pair_rows, pair_cols = half_h // 2, half_w // 2

    def some(step, carry):
        backs = []
        for place in range(group):
            q = weight[step * group + place]
            field = field_ref[step * group + place]
            g_re, g_im = field[:half_h] * q, field[half_h:] * q
            re_a, re_b = g_re[:pair_rows], g_re[pair_rows:]
            im_a, im_b = g_im[:pair_rows], g_im[pair_rows:]
            to_re = jnp.concatenate([re_a + re_b, im_a - im_b], axis=0)
            to_im = jnp.concatenate([im_a + im_b, re_b - re_a], axis=0)
            high, low = split(jnp.concatenate([to_re, to_im], axis=1))
            both = mm(back_ref[:left_rows], jnp.concatenate([high, low], axis=0))
            back = both[:band_rows] + both[band_rows:]
            re_a, re_b = back[:, :pair_cols], back[:, pair_cols : 2 * pair_cols]
            im_a, im_b = back[:, 2 * pair_cols : 3 * pair_cols], back[:, 3 * pair_cols :]
            backs.append(jnp.concatenate([re_a + re_b, im_a - im_b], axis=1))
            backs.append(jnp.concatenate([im_a + im_b, re_b - re_a], axis=1))
        high, low = split(jnp.concatenate(backs, axis=0))
        cols = back_ref[left_rows:]
        both = mm(jnp.concatenate([high, low], axis=1), jnp.concatenate([cols, cols], axis=0))
        boxes = both[:, :band_cols] + both[:, band_cols:]
        for place in range(group):
            led = step * group + place
            begin = 2 * place * band_rows
            back_re = boxes[begin : begin + band_rows]
            back_im = boxes[begin + band_rows : begin + 2 * band_rows]
            parts = (
                pupil_ref[0] * back_re + pupil_ref[1] * back_im,
                pupil_ref[0] * back_im - pupil_ref[1] * back_re,
            )
            area, down, right = box_area(led_row[led], led_col[led], band_rows, band_cols)
            for part in range(2):
                filled = jnp.concatenate([parts[part], jnp.zeros((8, band_cols), F32)], axis=0)
                filled = pltpu.roll(filled, down, 0)
                filled = jnp.concatenate([filled, jnp.zeros((band_rows + 8, 128), F32)], axis=1)
                grads[(part, *area)] += pltpu.roll(filled, right, 1)
        return carry

    lax.fori_loop(0, leds // group, some, 0)
    fresh_re = spec_ref[0] - (4.0 * STEP) * grads[0, :height, :width]
    fresh_im = spec_ref[1] - (4.0 * STEP) * grads[1, :height, :width]
    for part, fresh in enumerate((fresh_re, fresh_im)):
        for number, block in enumerate(lane_blocks(fresh)):
            fresh_ref[part, number] = block
    stores = []
    for number in range(width // 128):
        store = pltpu.make_async_copy(
            fresh_ref.at[:, number], fresh_hbm.at[:, :, pl.ds(number * 128, 128)],
            fresh_sems.at[number],
        )
        store.start()
        stores.append(store)
    big_load.wait()

    def spread(parity, table):
        rows = pl.ds(parity, height // 2, stride=2)
        parts = [
            jnp.concatenate([fresh_ref[part, n, rows] for n in range(width // 128)], axis=1)
            for part in range(2)
        ]
        high, low = split(jnp.concatenate(parts, axis=0))
        table_hi, table_lo = big[table : table + height], big[table + height : table + 2 * height]
        left = jnp.concatenate([table_hi, table_lo, table_hi], axis=1)
        return mm(left, jnp.concatenate([high, high, low], axis=0))

    even, odd = spread(0, 0), spread(1, 2 * height)
    upper, lower = even + odd, even - odd
    half = height // 2
    z_re = jnp.concatenate([upper[:half], lower[:half]], axis=0)
    z_im = jnp.concatenate([upper[half:], lower[half:]], axis=0)

    near = [z[:, : width // 2] for z in (z_re, z_im)]
    far = [z[:, width // 2 :] for z in (z_re, z_im)]
    mixed = [a + b for a, b in zip(near, far)] + [a - b for a, b in zip(near, far)]
    high, low = split(jnp.concatenate(mixed, axis=1))
    high_ref[...] = high
    low_ref[...] = low
    count = sides_ref.shape[1] // 2
    for parity in range(2):
        table = 4 * height + 4 * count * parity
        cut = slice(parity * width, (parity + 1) * width)
        side_hi = jnp.concatenate([big[table : table + count], big[table + count : table + 2 * count]], axis=1)
        side_lo = jnp.concatenate(
            [big[table + 2 * count : table + 3 * count], big[table + 3 * count : table + 4 * count]], axis=1
        )
        one = across(side_hi, high[:, cut]) + across(side_lo, high[:, cut])
        one = one + across(side_hi, low[:, cut])
        for number, block in enumerate(lane_blocks(one)):
            sides_ref[number, pl.ds(parity, count, stride=2)] = block
    sides = jnp.concatenate([sides_ref[n] for n in range(height // 128)], axis=1)
    to_left, to_right = sides[:count], sides[count:]
    first_ref[...] = jnp.where(is_odd, to_left, to_right)
    second_ref[...] = jnp.where(is_odd, to_right, to_left)
    for store in stores:
        store.wait()


def update(
    field, weight, window_parts, spectrum, pupil, patterns, led_row, led_col, where, tables,
    margin, group=8,
):
    _, _, back_rows, back_cols = tables
    leds = led_row.shape[0]
    _, height, width = spectrum.shape
    half_h, half_w = height // 2, width // 2
    big = []
    for parity in range(2):
        freqs = np.arange(parity, height, 2) - height // 2
        re, im = wave(np.arange(height // 2), freqs, height, height)
        big += two_parts(np.block([[re, -im], [im, re]]))
    for parity in range(2):
        left = np.arange(parity, margin, 2)
        freqs = np.arange(width // 2) - width // 2
        l_re, l_im = wave(left, freqs, width, width)
        r_re, r_im = wave(left + width - margin, freqs, width, width)
        from_re = two_parts(np.concatenate([l_re, l_im, r_re, r_im]))
        from_im = two_parts(np.concatenate([-l_im, l_re, -r_im, r_re]))
        big += [from_re[0], from_im[0], from_re[1], from_im[1]]
    big = np.concatenate(big)
    back = np.concatenate([back_rows, back_cols])
    out_shape = (
        jax.ShapeDtypeStruct(spectrum.shape, F32),
        jax.ShapeDtypeStruct((height, 2 * width), BF16),
        jax.ShapeDtypeStruct((height, 2 * width), BF16),
        jax.ShapeDtypeStruct((2 * margin, height), F32),
        jax.ShapeDtypeStruct((2 * margin, height), F32),
        jax.ShapeDtypeStruct(weight.shape, F32),
    )
    return pl.pallas_call(
        functools.partial(update_kernel, group=group),
        out_shape=out_shape,
        in_specs=[pl.BlockSpec(memory_space=SMEM)] * 4
        + vmem_spec(8)
        + [pl.BlockSpec(memory_space=pltpu.HBM)],
        out_specs=(pl.BlockSpec(memory_space=pltpu.HBM), *vmem_spec(5)),
        input_output_aliases={5: 5},
        scratch_shapes=[
            pltpu.VMEM((2, height + 8, width + 128), F32),
            pltpu.VMEM((2, width // 128, height, 128), F32),
            pltpu.VMEM(big.shape, BF16),
            pltpu.VMEM((height // 128, 4 * margin, 128), F32),
            pltpu.SemaphoreType.DMA,
            pltpu.SemaphoreType.DMA((width // 128,)),
        ],
        compiler_params=pltpu.CompilerParams(vmem_limit_bytes=LIMIT),
        name="update",
    )(
        led_row, led_col, patterns, where, field, weight, *window_parts, spectrum, pupil, back,
        pltpu.with_memory_space_constraint(jnp.asarray(big), pltpu.HBM),
    )[:5]


def object_kernel(high_ref, low_ref, table_ref, out_hbm, edges_ref, out, sems):
    core = out.shape[2]
    margin = edges_ref.shape[2]
    half = core // 2
    depth = high_ref.shape[1] // 4
    cuts = (slice(0, half // 2 // 16 * 16 + 16), slice(half // 2 // 16 * 16 + 16, half))
    stores = []
    for number, cut in enumerate(cuts):
        for parity in range(2):
            lefts = []
            for begin in (4 * parity * half, (4 * parity + 1) * half):
                rows = slice(begin + cut.start, begin + cut.stop)
                more = slice(rows.start + 2 * half, rows.stop + 2 * half)
                lefts.append(jnp.concatenate([table_ref[rows], table_ref[more], table_ref[rows]], axis=1))
            left = jnp.concatenate(lefts, axis=0)
            products = []
            for part in range(2):
                lanes = slice((2 * parity + part) * depth, (2 * parity + part + 1) * depth)
                z_hi, z_lo = high_ref[:, lanes], low_ref[:, lanes]
                products.append(across(left, jnp.concatenate([z_hi, z_hi, z_lo], axis=1)))
            count = cut.stop - cut.start
            rows = pl.ds(2 * cut.start + parity, count, stride=2)
            real = products[0][:count] - products[1][count:]
            imaginary = products[0][count:] + products[1][:count]
            for part, values in enumerate((real, imaginary)):
                for lanes, block in enumerate(lane_blocks(values)):
                    out[part, lanes, rows] = block
        span = pl.ds(2 * cut.start, 2 * (cut.stop - cut.start))
        for lanes in range(out.shape[1]):
            store = pltpu.make_async_copy(
                out.at[:, lanes, span], out_hbm.at[:, span, pl.ds(lanes * 128, 128)],
                sems.at[number, lanes],
            )
            store.start()
            stores.append(store)
    for part in range(2):
        for side, begin in enumerate((0, core - margin)):
            edge = [out[part, n, begin : begin + margin] for n in range(out.shape[1])]
            edges_ref[part, side] = jnp.concatenate(edge, axis=1)
    for store in stores:
        store.wait()


def object_core(high, low, margin, core):
    height, width = high.shape[0], high.shape[1] // 2
    table = []
    for parity in range(2):
        places = margin + np.arange(parity, core, 2)
        table += two_parts(
            np.concatenate(wave(places, np.arange(width // 2) - width // 2, width, width))
        )
    table = np.concatenate(table)
    return pl.pallas_call(
        object_kernel,
        out_shape=(
            jax.ShapeDtypeStruct((2, core, height), F32),
            jax.ShapeDtypeStruct((2, 2, margin, height), F32),
        ),
        in_specs=vmem_spec(3),
        out_specs=(pl.BlockSpec(memory_space=pltpu.HBM), pl.BlockSpec(memory_space=VMEM)),
        scratch_shapes=[
            pltpu.VMEM((2, height // 128, core, 128), F32),
            pltpu.SemaphoreType.DMA((2, height // 128)),
        ],
        compiler_params=pltpu.CompilerParams(vmem_limit_bytes=LIMIT),
        cost_estimate=pl.CostEstimate(
            flops=3_000_000_000, bytes_accessed=5_000_000, transcendentals=0
        ),
        name="object",
    )(high, low, table)


def blend_kernel(where, first_ref, second_ref, edges_ref, core_hbm, out_hbm, mixed, sems):
    tile = where[2]
    is_odd = where[1] == 1
    margin, core = edges_ref.shape[2], out_hbm.shape[1]
    k = lax.broadcasted_iota(jnp.int32, (margin, 1), 0).astype(F32)
    span = 2.0 * margin
    from_left = jnp.where(is_odd, first_ref[...], second_ref[...])
    from_right = jnp.where(is_odd, second_ref[...], first_ref[...])
    sides = (
        ((k + margin + 0.5) / span, (margin - k - 0.5) / span, tile > 0, from_left, 0),
        (
            (span - k - 0.5) / span, (k + 0.5) / span, tile < where[3] - 1, from_right,
            core - margin,
        ),
    )
    stores = []
    for side, (own_w, other_w, has_other, other, begin) in enumerate(sides):
        own_w = jnp.where(has_other, own_w, 1.0)
        other_w = jnp.where(has_other, other_w, 0.0)
        for part in range(2):
            cut = slice(part * margin, (part + 1) * margin)
            mixed[part, side] = edges_ref[part, side] * own_w + other[cut] * other_w
            store = pltpu.make_async_copy(
                mixed.at[part, side], out_hbm.at[part, pl.ds(begin, margin)],
                sems.at[2 * side + part],
            )
            store.start()
            stores.append(store)
    for store in stores:
        store.wait()


def blend(core_part, edges, first, second, where):
    return pl.pallas_call(
        blend_kernel,
        out_shape=jax.ShapeDtypeStruct(core_part.shape, F32),
        in_specs=[pl.BlockSpec(memory_space=SMEM)]
        + vmem_spec(3)
        + [pl.BlockSpec(memory_space=pltpu.HBM)],
        out_specs=pl.BlockSpec(memory_space=pltpu.HBM),
        input_output_aliases={4: 0},
        scratch_shapes=[pltpu.VMEM(edges.shape, F32), pltpu.SemaphoreType.DMA((4,))],
        compiler_params=pltpu.CompilerParams(vmem_limit_bytes=LIMIT),
        name="blend",
    )(where, first, second, edges, core_part)


def body(raw, scales, flat, spectrum, pupil, patterns, led_row, led_col):
    height, core = flat.shape
    margin = OV // 2
    width = core + OV
    tiles = lax.axis_size("tile")
    tile = lax.axis_index("tile")
    grp = lax.axis_index("grp")
    frames_here = raw.shape[0]
    band_rows, band_cols = pupil.shape[1:]
    spectrum_tile = spectrum[0]
    patterns = patterns.T
    odd = lax.rem(tile, 2)
    where = jnp.stack([grp, odd, tile, jnp.int32(tiles)]).astype(jnp.int32)

    swap_a = [(i, i ^ 1) for i in range(tiles)]
    swap_b = [(i, ((i + 1) ^ 1) - 1) for i in range(1, tiles - 1)]

    def neighbours(for_a, for_b):
        return lax.ppermute(for_a, "tile", swap_a), lax.ppermute(for_b, "tile", swap_b)

    tables = stacked_tables(height, width, band_rows, band_cols)
    passes = (low_pass(height, band_rows), low_pass(width, band_cols).T)

    by_rows = gains_by_rows(flat.T, tiles, width)
    dequantized = dequantize(raw, scales, by_rows, tiles, core, margin)
    gains = lax.all_to_all(by_rows, "tile", split_axis=0, concat_axis=0, tiled=True)
    narrow = strips(dequantized, gains, where, passes[1], frames_here, core, margin)
    arrived = lax.all_to_all(narrow, "tile", split_axis=0, concat_axis=0, tiled=True)
    handed = window_tables(tiles, passes, margin, core)
    field, estimate, rows, small = all_fields(
        spectrum_tile, pupil, patterns, led_row, led_col, tables, handed
    )
    window = windows(arrived, rows, small, frames_here, core)
    field, weight = fetch(field, estimate, window, patterns, where)

    swap_core = [(i, i ^ 1) for i in range(4)]
    swap_chip = [(i, i ^ 2) for i in range(4)]
    other = functools.partial(lax.ppermute, axis_name="grp")
    window_2 = other(window, perm=swap_chip)
    window_1 = other(window, perm=swap_core)
    window_2, field, weight = lax.optimization_barrier((window_2, field, weight))
    window_3 = other(window_2, perm=swap_core)

    fresh, high, low, for_a, for_b = update(
        field, weight, (window_1, window_2, window_3), spectrum_tile, pupil, patterns,
        led_row, led_col, where, tables, margin,
    )
    side_a, side_b = neighbours(for_a, for_b)
    core_part, edges = object_core(high, low, margin, core)
    stitched = blend(core_part, edges, side_a, side_b, where)
    return fresh[None], jnp.transpose(stitched, (0, 2, 1))


def solution(mesh):
    return jax.shard_map(
        body,
        mesh=mesh,
        in_specs=(
            P("grp", "tile", None),
            P("grp", "tile", None),
            P(None, "tile"),
            P("tile", None, None, None),
            P(),
            P(),
            P(),
            P(),
        ),
        out_specs=(P("tile", None, None, None), P(None, None, "tile")),
        check_vma=False,
    )
```

```python
import functools
import math

import jax
import jax.numpy as jnp
import ml_dtypes
import numpy as np
from jax import lax
from jax.experimental import pallas as pl
from jax.experimental.pallas import tpu as pltpu
from jax.sharding import PartitionSpec as P

OV = 32
BC = 32
STEP = 0.02
F32 = jnp.float32
BF16 = jnp.bfloat16
VMEM = pltpu.VMEM
SMEM = pltpu.SMEM
LIMIT = 30 << 20


def two_parts(table):
    table = np.asarray(table, np.float64)
    high = table.astype(ml_dtypes.bfloat16)
    low = (table - high.astype(np.float64)).astype(ml_dtypes.bfloat16)
    return high, low


def wave(places, freqs, length, norm):
    turns = np.outer(places, freqs) % length
    angle = turns * (2.0 * math.pi / length)
    return np.cos(angle) / math.sqrt(norm), np.sin(angle) / math.sqrt(norm)


def pairs(length):
    first = np.arange(1, length // 2, 2)
    return np.concatenate([first, length - first])


def low_pass(length, band):
    places = pairs(length)[:, None] - np.arange(length)[None, :]
    total = np.ones(places.shape)
    for freq in range(1, band):
        total += 2.0 * np.cos(2.0 * math.pi * ((freq * places) % length) / length)
    return total / length


def stacked_tables(height, width, band_rows, band_cols):
    row_re, row_im = wave(
        pairs(height), np.arange(band_rows) - band_rows // 2, height, band_rows
    )
    rows = np.block([[row_re, -row_im], [row_im, row_re]])
    col_re, col_im = wave(
        np.arange(band_cols) - band_cols // 2, pairs(width), width, band_cols
    )
    cols = np.block([[col_re, col_im], [-col_im, col_re]])
    half_rows, half_cols = height // 4, width // 4
    high, low = two_parts(np.concatenate([row_re[:half_rows], row_im[:half_rows]]).T)
    back_rows = np.block([[high, high], [low, np.zeros_like(low)]])
    back_cols = np.concatenate(
        two_parts(np.concatenate([col_re[:, :half_cols], col_im[:, :half_cols]], axis=1).T), axis=1
    )
    return rows, cols, back_rows, back_cols


def split(values):
    high = values.astype(BF16)
    return high, (values - high.astype(F32)).astype(BF16)


def mm(left, right):
    return jnp.dot(left, right, preferred_element_type=F32)


def vmem_spec(count):
    return [pl.BlockSpec(memory_space=VMEM)] * count


def lane_blocks(values):
    return [values[:, begin : begin + 128] for begin in range(0, values.shape[1], 128)]


def parts_rows(values):
    high = values.astype(BF16).astype(F32)
    return jnp.concatenate([high, values - high], axis=0).astype(BF16)


def rows_value(rows):
    rows = rows.astype(F32)
    return rows[:8, :128] + rows[8:, :128]


def gains_kernel(flat_ref, out_hbm, out, sems):
    core, height = flat_ref.shape
    tiles, rows_here, width = out_hbm.shape
    stores = []
    for number, begin in enumerate(range(0, width, 128)):
        length = min(128, core - begin)
        gains = flat_ref[begin : begin + length] - 1.0
        if length < 128:
            gains = jnp.concatenate([gains, jnp.zeros((128 - length, height), F32)], axis=0)
        by_rows = jnp.transpose(gains, (1, 0)).reshape(tiles, rows_here, 128)
        out[:, :, begin : begin + 128] = by_rows.astype(BF16)
        part = (slice(None), slice(None), pl.ds(begin, 128))
        store = pltpu.make_async_copy(out.at[part], out_hbm.at[part], sems.at[number])
        store.start()
        stores.append(store)
    for store in stores:
        store.wait()


def gains_by_rows(flat, tiles, width):
    core, height = flat.shape
    shape = (tiles, height // tiles, width)
    return pl.pallas_call(
        gains_kernel,
        out_shape=jax.ShapeDtypeStruct(shape, BF16),
        in_specs=vmem_spec(1),
        out_specs=pl.BlockSpec(memory_space=pltpu.HBM),
        scratch_shapes=[pltpu.VMEM(shape, BF16), pltpu.SemaphoreType.DMA((width // 128,))],
        compiler_params=pltpu.CompilerParams(vmem_limit_bytes=LIMIT),
        name="gains",
    )(flat)


def dequantize_kernel(raw_ref, scales_ref, after, out_ref, *, core, margin):
    lines, strip = raw_ref.shape
    coarse_rows, coarse_cols = scales_ref.shape
    tiles, _, width = out_ref.shape
    ratio = lines // coarse_rows
    row = lax.broadcasted_iota(jnp.int32, (lines, coarse_rows), 0)
    pick = lax.broadcasted_iota(jnp.int32, (lines, coarse_rows), 1)
    spread_rows = (row // ratio == pick).astype(F32).astype(BF16)
    factors = mm(spread_rows, scales_ref[...])
    wide = (coarse_cols // 128 + 1) * 128
    factors = jnp.concatenate([factors, jnp.zeros((lines, wide - coarse_cols), F32)], axis=1)

    blocks = []
    for tile in range(tiles):
        begin = (tile * core - margin) // BC
        blocks.append(pltpu.roll(factors, -begin % wide, 1)[:, :128].astype(BF16))
    block = lax.broadcasted_iota(jnp.int32, (128, width), 0)
    place = lax.broadcasted_iota(jnp.int32, (128, width), 1) + (-margin) % BC
    inside = (place >= block * BC) & (place < (block + 1) * BC)
    scales = mm(jnp.concatenate(blocks, axis=0), inside.astype(F32).astype(BF16))
    for tile in range(tiles):
        start = tile * core - margin
        base = max(start, 0) // 128 * 128
        span = min(width + 128, strip - base)
        codes = raw_ref[:, base : base + span].astype(F32)
        turn = (base - start) % span
        if turn:
            codes = pltpu.roll(codes, turn, 1)
        out_ref[tile] = codes[:, :width] * scales[tile * lines : (tile + 1) * lines]


def dequantize(raw, scales, after, tiles, core, margin):
    frames, rows_here, strip = raw.shape
    return pl.pallas_call(
        functools.partial(dequantize_kernel, core=core, margin=margin),
        out_shape=jax.ShapeDtypeStruct((tiles, frames * rows_here, core + 2 * margin), F32),
        in_specs=vmem_spec(2) + [pl.BlockSpec(memory_space=pl.ANY)],
        out_specs=pl.BlockSpec(memory_space=VMEM),
        compiler_params=pltpu.CompilerParams(vmem_limit_bytes=LIMIT),
        cost_estimate=pl.CostEstimate(
            flops=2_000_000_000, bytes_accessed=4_000_000, transcendentals=0
        ),
        name="dequantize",
    )(raw.reshape(frames * rows_here, strip), scales.reshape(-1, scales.shape[-1]), after)


def strips_kernel(dq_ref, gains_ref, lc_ref, out_hbm, out_ref, sems, *, frames, core, margin):
    tiles, lines, width = dq_ref.shape
    half_w = lc_ref.shape[1]
    rows_here = lines // frames
    line = lax.broadcasted_iota(jnp.int32, (1, width), 1)
    in_core = ((line >= margin) & (line < margin + core)).astype(F32)
    xc = (line.astype(F32) - margin - (core - 1) / 2.0) * in_core
    first_row = (lax.axis_index("tile") * rows_here).astype(F32)
    height = rows_here * tiles
    yc = lax.broadcasted_iota(jnp.int32, (rows_here, 1), 0).astype(F32)
    yc = yc + (first_row - (height - 1) / 2.0)
    lane = lax.broadcasted_iota(jnp.int32, (8, 128), 1)
    narrow_lane = lax.broadcasted_iota(jnp.int32, (1, 128), 1)

    lc_hi, lc_lo = lc_ref[:width], lc_ref[width:]
    own, stores = [], []

    def windowed(tile):
        gains = pltpu.roll(gains_ref[tile].astype(F32), margin, 1)
        if tile > 0:
            end = gains_ref[tile - 1][:, width - 128 :].astype(F32)
            end = pltpu.roll(end, (2 * margin) + margin, 1)
            end = jnp.where(narrow_lane < margin, end, 0.0)
            gains = jnp.concatenate([gains[:, :128] + end, gains[:, 128:]], axis=1)
        if tile < tiles - 1:
            end = gains_ref[tile + 1][:, :128].astype(F32)
            end = pltpu.roll(end, 128 - margin, 1)
            end = jnp.where(narrow_lane >= 128 - margin, end, 0.0)
            gains = jnp.concatenate(
                [gains[:, : width - 128], gains[:, width - 128 :] + end], axis=1
            )
        gains = jnp.concatenate([gains + 1.0] * frames, axis=0)
        flattened = dq_ref[tile] * gains
        sums, lines_y = [], []
        for frame in range(frames):
            cut = slice(frame * rows_here, (frame + 1) * rows_here)
            sums.append(jnp.sum(flattened[cut], axis=0, keepdims=True))
            lines_y.append(jnp.sum(flattened[cut] * yc, axis=0, keepdims=True))
        blank = [jnp.zeros((8 - frames, width), F32)]
        slope_y = jnp.sum(jnp.concatenate(lines_y + blank, axis=0) * in_core, axis=1, keepdims=True)
        slope_x = jnp.sum(jnp.concatenate(sums + blank, axis=0) * xc, axis=1, keepdims=True)
        own.append(jnp.where(lane == 0, slope_y, jnp.where(lane == 1, slope_x, 0.0)))
        return flattened.astype(BF16)

    def finish(tile, one):
        means, centred = [], []
        for frame in range(frames):
            cut = slice(frame * rows_here, (frame + 1) * rows_here)
            mean = jnp.sum(one[cut], axis=0, keepdims=True)
            mean = jnp.sum(mean, axis=1, keepdims=True) * (1.0 / (rows_here * half_w))
            means.append(mean)
            centred.append(one[cut] - mean)
        centred = jnp.concatenate(centred, axis=0)
        for part in range(half_w // 128):
            columns = centred[:, part * 128 : (part + 1) * 128]
            out_ref[tile, part * lines : (part + 1) * lines] = columns.astype(BF16)
        mean = jnp.concatenate(means + [jnp.zeros((8 - frames, 1), F32)], axis=0)
        packed = own[tile] + jnp.where(lane == 6, mean, 0.0)
        if tile > 0:
            packed += pltpu.roll(own[tile - 1], 2, 1)
        if tile < tiles - 1:
            packed += pltpu.roll(own[tile + 1], 4, 1)
        out_ref[tile, half_w // 128 * lines :] = parts_rows(packed)

    part_tiles = max(tiles // 2, 1)
    waiting = None
    for begin in range(0, tiles, part_tiles):
        pixels = jnp.concatenate([windowed(t) for t in range(begin, begin + part_tiles)], axis=0)
        if waiting is not None:
            finish(*waiting)
        narrow = mm(pixels, lc_hi) + mm(pixels, lc_lo)
        for number in range(part_tiles):
            one = (begin + number, narrow[number * lines : (number + 1) * lines])
            if number == part_tiles - 1 and begin + part_tiles < tiles:
                waiting = one
            else:
                finish(*one)
        done = begin + part_tiles - (1 if begin + part_tiles < tiles else 0)
        first = max(begin - 1, 0)
        span = pl.ds(first, done - first)
        store = pltpu.make_async_copy(out_ref.at[span], out_hbm.at[span], sems.at[begin // part_tiles])
        store.start()
        stores.append(store)
    for store in stores:
        store.wait()


def strips(dequantized, gains, lc, frames, core, margin):
    tiles, lines, _ = dequantized.shape
    shape = (tiles, lines * (lc.shape[1] // 128) + 16, 128)
    return pl.pallas_call(
        functools.partial(strips_kernel, frames=frames, core=core, margin=margin),
        out_shape=jax.ShapeDtypeStruct(shape, BF16),
        in_specs=vmem_spec(3),
        out_specs=pl.BlockSpec(memory_space=pltpu.HBM),
        scratch_shapes=[pltpu.VMEM(shape, BF16), pltpu.SemaphoreType.DMA((2,))],
        compiler_params=pltpu.CompilerParams(vmem_limit_bytes=LIMIT),
        name="strips",
    )(dequantized, gains, np.concatenate(two_parts(lc)))


def box_area(top, left, band_rows, band_cols):
    row = top // 8 * 8
    col = left // 128 * 128
    area = (
        pl.ds(pl.multiple_of(row, 8), band_rows + 8),
        pl.ds(pl.multiple_of(col, 128), band_cols + 128),
    )
    return area, top - row, left - col


def field_kernel(
    led_row, led_col, patterns, spec_ref, pupil_ref, cols_ref, rows_ref,
    rows_hbm, small_hbm, field_ref, estimate_ref, rows_out, small_out, wide, bright, sems, *, group,
):
    leds, half_h, half_w = bright.shape
    loads = [
        pltpu.make_async_copy(rows_hbm, rows_out, sems.at[0]),
        pltpu.make_async_copy(small_hbm, small_out, sems.at[1]),
    ]
    for load in loads:
        load.start()
    band_rows, band_cols = pupil_ref.shape[1:]
    width = spec_ref.shape[2]
    depth = 2 * band_cols
    wide[...] = jnp.zeros_like(wide)
    wide[:, : spec_ref.shape[1], :width] = spec_ref[...]

    def some(step, carry):
        boxes = []
        for place in range(group):
            led = step * group + place
            area, down, right = box_area(led_row[led], led_col[led], band_rows, band_cols)
            back = lax.rem(2 * band_cols - right, 2 * band_cols)
            up = lax.rem(band_rows + 8 - down, band_rows + 8)
            parts = []
            for part in range(2):
                strip = pltpu.roll(wide[(part, *area)], back, 1)
                parts.append(pltpu.roll(strip[:, :band_cols], up, 0)[:band_rows])
            lit_re = pupil_ref[0] * parts[0] - pupil_ref[1] * parts[1]
            lit_im = pupil_ref[0] * parts[1] + pupil_ref[1] * parts[0]
            boxes.append(jnp.concatenate([lit_re, lit_im], axis=1))
        high, low = split(jnp.concatenate(boxes, axis=0))
        cols_hi, cols_lo = cols_ref[:depth], cols_ref[depth:]
        spread = mm(high, cols_hi) + mm(high, cols_lo) + mm(low, cols_hi)
        for place in range(group):
            one = spread[place * band_rows : (place + 1) * band_rows]
            high, low = split(jnp.concatenate([one[:, :half_w], one[:, half_w:]], axis=0))
            field = mm(rows_ref[...], jnp.concatenate([high, low, high], axis=0))
            field_ref[step * group + place] = field
            bright[step * group + place] = field[:half_h] ** 2 + field[half_h:] ** 2
        return carry

    lax.fori_loop(0, leds // group, some, 0)

    def one_frame(frame, carry):
        total = bright[patterns[0, frame]]
        for lit in range(1, patterns.shape[0]):
            total += bright[patterns[lit, frame]]
        estimate_ref[frame] = total
        return carry

    lax.fori_loop(0, patterns.shape[1], one_frame, 0)
    for load in loads:
        load.wait()


def all_fields(spectrum, pupil, patterns, led_row, led_col, tables, handed, group=8):
    rows, cols, _, _ = tables
    leds = led_row.shape[0]
    _, height, width = spectrum.shape
    half_h, half_w = height // 2, width // 2
    high, low = two_parts(rows)
    return pl.pallas_call(
        functools.partial(field_kernel, group=group),
        out_shape=(
            jax.ShapeDtypeStruct((leds, 2 * half_h, half_w), F32),
            jax.ShapeDtypeStruct((patterns.shape[1], half_h, half_w), F32),
            *(jax.ShapeDtypeStruct(table.shape, table.dtype) for table in handed),
        ),
        in_specs=[pl.BlockSpec(memory_space=SMEM)] * 3
        + vmem_spec(4)
        + [pl.BlockSpec(memory_space=pltpu.HBM)] * 2,
        out_specs=tuple(vmem_spec(4)),
        scratch_shapes=[
            pltpu.VMEM((2, height + 8, width + 128), F32),
            pltpu.VMEM((leds, half_h, half_w), F32),
            pltpu.SemaphoreType.DMA((2,)),
        ],
        compiler_params=pltpu.CompilerParams(vmem_limit_bytes=LIMIT),
        cost_estimate=pl.CostEstimate(
            flops=8_000_000_000, bytes_accessed=16_000_000, transcendentals=0
        ),
        name="fields",
    )(
        led_row, led_col, patterns, spectrum, pupil, np.concatenate(two_parts(cols)),
        np.concatenate([high, high, low], axis=1),
        *(pltpu.with_memory_space_constraint(jnp.asarray(t), pltpu.HBM) for t in handed),
    )


def window_kernel(dq_ref, rows_ref, small_ref, window_ref, *, frames, core):
    slabs, lines, _ = dq_ref.shape
    half_h, half_w = rows_ref.shape[0], window_ref.shape[1]
    halves = half_w // 128
    lines = (lines - 16) // halves
    lr_sum, line = small_ref[:half_h, :128], small_ref[half_h:]
    rows_here = lines // frames
    height = slabs * rows_here
    over_y = 1.0 / (core * (height * (height * height - 1) / 12.0))
    over_x = 1.0 / (height * (core * (core * core - 1) / 12.0))
    lane = lax.broadcasted_iota(jnp.int32, (8, 128), 1)
    notes = [rows_value(dq_ref[slab, halves * lines :]) for slab in range(slabs)]
    slopes = functools.reduce(jnp.add, notes)
    slopes = slopes * jnp.where(lane % 2 == 0, over_y, over_x)
    slab_means = jnp.zeros((8, 128), F32)
    for slab in range(slabs):
        slab_means = jnp.where(lane == slab, notes[slab][:, 6:7], slab_means)
    values = []
    for slab in range(slabs):
        parts = [dq_ref[slab, part * lines : (part + 1) * lines] for part in range(halves)]
        values.append(jnp.concatenate(parts, axis=1))
    if rows_here % 16:
        values = [value.astype(F32) for value in values]
    means = []
    for frame in range(frames):
        cut = slice(frame * rows_here, (frame + 1) * rows_here)
        whole = jnp.concatenate([v[cut] for v in values], axis=0).astype(BF16)
        window = mm(rows_ref[...], jnp.concatenate([whole, whole], axis=0))
        level = jnp.sum(lr_sum * slab_means[frame : frame + 1], axis=1, keepdims=True)
        window = window + level
        tilt_y, tilt_x = 0.0, 0.0
        for side in range(3):
            tilt_y += line[2 * side : 2 * side + 1] * slopes[frame : frame + 1, 2 * side : 2 * side + 1]
            tilt_x += line[2 * side + 1 : 2 * side + 2] * slopes[frame : frame + 1, 2 * side + 1 : 2 * side + 2]
        window = window - lr_sum[:, 127:128] * tilt_y - tilt_x
        mean = jnp.sum(window, axis=0, keepdims=True)
        mean = jnp.sum(mean, axis=1, keepdims=True) * (1.0 / (half_h * half_w))
        means.append(jnp.broadcast_to(mean, (1, 128)))
        window_ref[frame * half_h : (frame + 1) * half_h] = (window - mean).astype(BF16)
    means = jnp.concatenate(means + [jnp.zeros((8 - frames, 128), F32)], axis=0)
    notes = parts_rows(means)
    window_ref[frames * half_h :] = jnp.concatenate([notes] * halves, axis=1)


def tilt_lines(width, margin, core, lc):
    local = np.arange(width) - margin
    lines = []
    for begin, end, shift in ((0, core, 0), (-margin, 0, core), (core, core + margin, -core)):
        on = (local >= begin) & (local < end)
        lines.append(on.astype(np.float64) @ lc)
        lines.append(((local + shift - (core - 1) / 2.0) * on) @ lc)
    return np.stack(lines + lines[:2])


def window_tables(tiles, passes, margin, core):
    lr, lc = passes
    half_h, height = lr.shape
    sums = np.zeros((half_h, lc.shape[1]))
    sums[:, :tiles] = lr.reshape(half_h, tiles, height // tiles).sum(axis=2)
    sums[:, 127] = lr @ (np.arange(height) - (height - 1) / 2.0)
    small = np.concatenate([sums, tilt_lines(lc.shape[0], margin, core, lc)])
    return np.concatenate(two_parts(lr), axis=1), small.astype(np.float32)


def windows(arrived, rows, small, frames, core):
    half_h, half_w = rows.shape[0], small.shape[1]
    return pl.pallas_call(
        functools.partial(window_kernel, frames=frames, core=core),
        out_shape=jax.ShapeDtypeStruct((frames * half_h + 16, half_w), BF16),
        in_specs=vmem_spec(3),
        out_specs=pl.BlockSpec(memory_space=VMEM),
        compiler_params=pltpu.CompilerParams(vmem_limit_bytes=LIMIT),
        name="windows",
    )(arrived, rows, small)


def add_frame(weight, patterns, frame, value):
    for lit in range(patterns.shape[0]):
        weight[patterns[lit, frame]] += value


def fetch_kernel(patterns, estimate_ref, window, field_hbm, field_ref, weight, sem):
    load = pltpu.make_async_copy(field_hbm, field_ref, sem)
    load.start()
    weight[...] = jnp.zeros_like(weight)
    frames, half_h, _ = estimate_ref.shape
    frames_here = window.shape[0] // half_h

    def one_frame(frame, carry):
        add_frame(weight, patterns, frame, estimate_ref[frame])
        return carry

    lax.fori_loop(0, frames, one_frame, 0)
    means = rows_value(window[frames_here * half_h :])
    for place in range(frames_here):
        value = window[place * half_h : (place + 1) * half_h].astype(F32)
        value = -means[place : place + 1, 0:1] - value
        add_frame(weight, patterns, lax.axis_index("grp") * frames_here + place, value)
    load.wait()


def fetch(field, estimate, window, patterns):
    leds = field.shape[0]
    return pl.pallas_call(
        fetch_kernel,
        out_shape=(
            jax.ShapeDtypeStruct(field.shape, F32),
            jax.ShapeDtypeStruct((leds, *estimate.shape[1:]), F32),
        ),
        in_specs=[pl.BlockSpec(memory_space=SMEM)]
        + vmem_spec(2)
        + [pl.BlockSpec(memory_space=pltpu.HBM)],
        out_specs=tuple(vmem_spec(2)),
        scratch_shapes=[pltpu.SemaphoreType.DMA],
        compiler_params=pltpu.CompilerParams(vmem_limit_bytes=LIMIT),
        cost_estimate=pl.CostEstimate(flops=0, bytes_accessed=16_000_000, transcendentals=0),
        name="fetch",
    )(patterns, estimate, window, pltpu.with_memory_space_constraint(field, pltpu.HBM))


def across(left, right):
    dims = (((1,), (1,)), ((), ()))
    return lax.dot_general(left, right, dims, preferred_element_type=F32)


def update_kernel(
    led_row, led_col, patterns, field_ref, weight_in, w1, w2, w3,
    spec_ref, pupil_ref, back_ref, big_hbm,
    fresh_hbm, high_ref, low_ref, first_ref, second_ref, weight,
    grads, fresh_ref, big, sides_ref, big_sem, fresh_sems, *, group,
):
    leds, half_h, half_w = weight.shape
    band_rows, band_cols = pupil_ref.shape[1:]
    height, width = spec_ref.shape[1:]
    frames_here = w1.shape[0] // half_h
    is_odd = lax.rem(lax.axis_index("tile"), 2) == 1
    big_load = pltpu.make_async_copy(big_hbm, big, big_sem)
    big_load.start()
    grads[...] = jnp.zeros_like(grads)
    for slot, window in enumerate((w1, w2, w3)):
        owner = jnp.bitwise_xor(lax.axis_index("grp"), slot + 1)
        means = rows_value(window[frames_here * half_h :])
        for place in range(frames_here):
            value = window[place * half_h : (place + 1) * half_h].astype(F32)
            value = -means[place : place + 1, 0:1] - value
            add_frame(weight, patterns, owner * frames_here + place, value)

    left_rows = 2 * band_rows
    pair_rows, pair_cols = half_h // 2, half_w // 2

    def some(step, carry):
        backs = []
        for place in range(group):
            q = weight[step * group + place]
            field = field_ref[step * group + place]
            g_re, g_im = field[:half_h] * q, field[half_h:] * q
            re_a, re_b = g_re[:pair_rows], g_re[pair_rows:]
            im_a, im_b = g_im[:pair_rows], g_im[pair_rows:]
            to_re = jnp.concatenate([re_a + re_b, im_a - im_b], axis=0)
            to_im = jnp.concatenate([im_a + im_b, re_b - re_a], axis=0)
            high, low = split(jnp.concatenate([to_re, to_im], axis=1))
            both = mm(back_ref[:left_rows], jnp.concatenate([high, low], axis=0))
            back = both[:band_rows] + both[band_rows:]
            re_a, re_b = back[:, :pair_cols], back[:, pair_cols : 2 * pair_cols]
            im_a, im_b = back[:, 2 * pair_cols : 3 * pair_cols], back[:, 3 * pair_cols :]
            backs.append(jnp.concatenate([re_a + re_b, im_a - im_b], axis=1))
            backs.append(jnp.concatenate([im_a + im_b, re_b - re_a], axis=1))
        high, low = split(jnp.concatenate(backs, axis=0))
        cols = back_ref[left_rows:]
        both = mm(jnp.concatenate([high, low], axis=1), jnp.concatenate([cols, cols], axis=0))
        boxes = both[:, :band_cols] + both[:, band_cols:]
        for place in range(group):
            led = step * group + place
            begin = 2 * place * band_rows
            back_re = boxes[begin : begin + band_rows]
            back_im = boxes[begin + band_rows : begin + 2 * band_rows]
            parts = (
                pupil_ref[0] * back_re + pupil_ref[1] * back_im,
                pupil_ref[0] * back_im - pupil_ref[1] * back_re,
            )
            area, down, right = box_area(led_row[led], led_col[led], band_rows, band_cols)
            for part in range(2):
                filled = jnp.concatenate([parts[part], jnp.zeros((8, band_cols), F32)], axis=0)
                filled = pltpu.roll(filled, down, 0)
                filled = jnp.concatenate([filled, jnp.zeros((band_rows + 8, 128), F32)], axis=1)
                grads[(part, *area)] += pltpu.roll(filled, right, 1)
        return carry

    lax.fori_loop(0, leds // group, some, 0)
    fresh_re = spec_ref[0] - (4.0 * STEP) * grads[0, :height, :width]
    fresh_im = spec_ref[1] - (4.0 * STEP) * grads[1, :height, :width]
    for part, fresh in enumerate((fresh_re, fresh_im)):
        for number, block in enumerate(lane_blocks(fresh)):
            fresh_ref[part, number] = block
    stores = []
    for number in range(width // 128):
        store = pltpu.make_async_copy(
            fresh_ref.at[:, number], fresh_hbm.at[:, :, pl.ds(number * 128, 128)],
            fresh_sems.at[number],
        )
        store.start()
        stores.append(store)
    big_load.wait()

    def spread(parity, table):
        rows = pl.ds(parity, height // 2, stride=2)
        parts = [
            jnp.concatenate([fresh_ref[part, n, rows] for n in range(width // 128)], axis=1)
            for part in range(2)
        ]
        high, low = split(jnp.concatenate(parts, axis=0))
        table_hi, table_lo = big[table : table + height], big[table + height : table + 2 * height]
        left = jnp.concatenate([table_hi, table_lo, table_hi], axis=1)
        return mm(left, jnp.concatenate([high, high, low], axis=0))

    even, odd = spread(0, 0), spread(1, 2 * height)
    upper, lower = even + odd, even - odd
    half = height // 2
    z_re = jnp.concatenate([upper[:half], lower[:half]], axis=0)
    z_im = jnp.concatenate([upper[half:], lower[half:]], axis=0)

    near = [z[:, : width // 2] for z in (z_re, z_im)]
    far = [z[:, width // 2 :] for z in (z_re, z_im)]
    mixed = [a + b for a, b in zip(near, far)] + [a - b for a, b in zip(near, far)]
    high, low = split(jnp.concatenate(mixed, axis=1))
    high_ref[...] = high
    low_ref[...] = low
    count = sides_ref.shape[1] // 2
    for parity in range(2):
        table = 4 * height + 4 * count * parity
        cut = slice(parity * width, (parity + 1) * width)
        side_hi = jnp.concatenate([big[table : table + count], big[table + count : table + 2 * count]], axis=1)
        side_lo = jnp.concatenate(
            [big[table + 2 * count : table + 3 * count], big[table + 3 * count : table + 4 * count]], axis=1
        )
        one = across(side_hi, high[:, cut]) + across(side_lo, high[:, cut])
        one = one + across(side_hi, low[:, cut])
        for number, block in enumerate(lane_blocks(one)):
            sides_ref[number, pl.ds(parity, count, stride=2)] = block
    sides = jnp.concatenate([sides_ref[n] for n in range(height // 128)], axis=1)
    to_left, to_right = sides[:count], sides[count:]
    first_ref[...] = jnp.where(is_odd, to_left, to_right)
    second_ref[...] = jnp.where(is_odd, to_right, to_left)
    for store in stores:
        store.wait()


def update(
    field, weight, window_parts, spectrum, pupil, patterns, led_row, led_col, tables,
    margin, group=8,
):
    _, _, back_rows, back_cols = tables
    leds = led_row.shape[0]
    _, height, width = spectrum.shape
    half_h, half_w = height // 2, width // 2
    big = []
    for parity in range(2):
        freqs = np.arange(parity, height, 2) - height // 2
        re, im = wave(np.arange(height // 2), freqs, height, height)
        big += two_parts(np.block([[re, -im], [im, re]]))
    for parity in range(2):
        left = np.arange(parity, margin, 2)
        freqs = np.arange(width // 2) - width // 2
        l_re, l_im = wave(left, freqs, width, width)
        r_re, r_im = wave(left + width - margin, freqs, width, width)
        from_re = two_parts(np.concatenate([l_re, l_im, r_re, r_im]))
        from_im = two_parts(np.concatenate([-l_im, l_re, -r_im, r_re]))
        big += [from_re[0], from_im[0], from_re[1], from_im[1]]
    big = np.concatenate(big)
    back = np.concatenate([back_rows, back_cols])
    out_shape = (
        jax.ShapeDtypeStruct(spectrum.shape, F32),
        jax.ShapeDtypeStruct((height, 2 * width), BF16),
        jax.ShapeDtypeStruct((height, 2 * width), BF16),
        jax.ShapeDtypeStruct((2 * margin, height), F32),
        jax.ShapeDtypeStruct((2 * margin, height), F32),
        jax.ShapeDtypeStruct(weight.shape, F32),
    )
    return pl.pallas_call(
        functools.partial(update_kernel, group=group),
        out_shape=out_shape,
        in_specs=[pl.BlockSpec(memory_space=SMEM)] * 3
        + vmem_spec(8)
        + [pl.BlockSpec(memory_space=pltpu.HBM)],
        out_specs=(pl.BlockSpec(memory_space=pltpu.HBM), *vmem_spec(5)),
        input_output_aliases={4: 5},
        scratch_shapes=[
            pltpu.VMEM((2, height + 8, width + 128), F32),
            pltpu.VMEM((2, width // 128, height, 128), F32),
            pltpu.VMEM(big.shape, BF16),
            pltpu.VMEM((height // 128, 4 * margin, 128), F32),
            pltpu.SemaphoreType.DMA,
            pltpu.SemaphoreType.DMA((width // 128,)),
        ],
        compiler_params=pltpu.CompilerParams(vmem_limit_bytes=LIMIT),
        name="update",
    )(
        led_row, led_col, patterns, field, weight, *window_parts, spectrum, pupil, back,
        pltpu.with_memory_space_constraint(jnp.asarray(big), pltpu.HBM),
    )[:5]


def object_kernel(high_ref, low_ref, table_ref, out_hbm, edges_ref, out, sems):
    core = out.shape[2]
    margin = edges_ref.shape[2]
    half = core // 2
    depth = high_ref.shape[1] // 4
    cuts = (slice(0, half // 2 // 16 * 16 + 16), slice(half // 2 // 16 * 16 + 16, half))
    stores = []
    for number, cut in enumerate(cuts):
        for parity in range(2):
            lefts = []
            for begin in (4 * parity * half, (4 * parity + 1) * half):
                rows = slice(begin + cut.start, begin + cut.stop)
                more = slice(rows.start + 2 * half, rows.stop + 2 * half)
                lefts.append(jnp.concatenate([table_ref[rows], table_ref[more], table_ref[rows]], axis=1))
            left = jnp.concatenate(lefts, axis=0)
            products = []
            for part in range(2):
                lanes = slice((2 * parity + part) * depth, (2 * parity + part + 1) * depth)
                z_hi, z_lo = high_ref[:, lanes], low_ref[:, lanes]
                products.append(across(left, jnp.concatenate([z_hi, z_hi, z_lo], axis=1)))
            count = cut.stop - cut.start
            rows = pl.ds(2 * cut.start + parity, count, stride=2)
            real = products[0][:count] - products[1][count:]
            imaginary = products[0][count:] + products[1][:count]
            for part, values in enumerate((real, imaginary)):
                for lanes, block in enumerate(lane_blocks(values)):
                    out[part, lanes, rows] = block
        span = pl.ds(2 * cut.start, 2 * (cut.stop - cut.start))
        for lanes in range(out.shape[1]):
            store = pltpu.make_async_copy(
                out.at[:, lanes, span], out_hbm.at[:, span, pl.ds(lanes * 128, 128)],
                sems.at[number, lanes],
            )
            store.start()
            stores.append(store)
    for part in range(2):
        for side, begin in enumerate((0, core - margin)):
            edge = [out[part, n, begin : begin + margin] for n in range(out.shape[1])]
            edges_ref[part, side] = jnp.concatenate(edge, axis=1)
    for store in stores:
        store.wait()


def object_core(high, low, margin, core):
    height, width = high.shape[0], high.shape[1] // 2
    table = []
    for parity in range(2):
        places = margin + np.arange(parity, core, 2)
        table += two_parts(
            np.concatenate(wave(places, np.arange(width // 2) - width // 2, width, width))
        )
    table = np.concatenate(table)
    return pl.pallas_call(
        object_kernel,
        out_shape=(
            jax.ShapeDtypeStruct((2, core, height), F32),
            jax.ShapeDtypeStruct((2, 2, margin, height), F32),
        ),
        in_specs=vmem_spec(3),
        out_specs=(pl.BlockSpec(memory_space=pltpu.HBM), pl.BlockSpec(memory_space=VMEM)),
        scratch_shapes=[
            pltpu.VMEM((2, height // 128, core, 128), F32),
            pltpu.SemaphoreType.DMA((2, height // 128)),
        ],
        compiler_params=pltpu.CompilerParams(vmem_limit_bytes=LIMIT),
        cost_estimate=pl.CostEstimate(
            flops=3_000_000_000, bytes_accessed=5_000_000, transcendentals=0
        ),
        name="object",
    )(high, low, table)


def blend_kernel(first_ref, second_ref, edges_ref, core_hbm, out_hbm, mixed, sems):
    tile = lax.axis_index("tile")
    is_odd = lax.rem(tile, 2) == 1
    margin, core = edges_ref.shape[2], out_hbm.shape[1]
    k = lax.broadcasted_iota(jnp.int32, (margin, 1), 0).astype(F32)
    span = 2.0 * margin
    from_left = jnp.where(is_odd, first_ref[...], second_ref[...])
    from_right = jnp.where(is_odd, second_ref[...], first_ref[...])
    sides = (
        ((k + margin + 0.5) / span, (margin - k - 0.5) / span, tile > 0, from_left, 0),
        (
            (span - k - 0.5) / span, (k + 0.5) / span, tile < lax.axis_size("tile") - 1, from_right,
            core - margin,
        ),
    )
    stores = []
    for side, (own_w, other_w, has_other, other, begin) in enumerate(sides):
        own_w = jnp.where(has_other, own_w, 1.0)
        other_w = jnp.where(has_other, other_w, 0.0)
        for part in range(2):
            cut = slice(part * margin, (part + 1) * margin)
            mixed[side, part] = edges_ref[part, side] * own_w + other[cut] * other_w
        store = pltpu.make_async_copy(
            mixed.at[side], out_hbm.at[:, pl.ds(begin, margin)], sems.at[side]
        )
        store.start()
        stores.append(store)
    for store in stores:
        store.wait()


def blend(core_part, edges, first, second):
    return pl.pallas_call(
        blend_kernel,
        out_shape=jax.ShapeDtypeStruct(core_part.shape, F32),
        in_specs=vmem_spec(3) + [pl.BlockSpec(memory_space=pltpu.HBM)],
        out_specs=pl.BlockSpec(memory_space=pltpu.HBM),
        input_output_aliases={3: 0},
        scratch_shapes=[pltpu.VMEM(edges.shape, F32), pltpu.SemaphoreType.DMA((2,))],
        compiler_params=pltpu.CompilerParams(vmem_limit_bytes=LIMIT),
        name="blend",
    )(first, second, edges, core_part)


def body(raw, scales, flat, spectrum, pupil, patterns, led_row, led_col):
    height, core = flat.shape
    margin = OV // 2
    width = core + OV
    tiles = lax.axis_size("tile")
    frames_here = raw.shape[0]
    band_rows, band_cols = pupil.shape[1:]
    spectrum_tile = spectrum[0]
    patterns = patterns.T

    swap_a = [(i, i ^ 1) for i in range(tiles)]
    swap_b = [(i, ((i + 1) ^ 1) - 1) for i in range(1, tiles - 1)]

    def neighbours(for_a, for_b):
        return lax.ppermute(for_a, "tile", swap_a), lax.ppermute(for_b, "tile", swap_b)

    tables = stacked_tables(height, width, band_rows, band_cols)
    passes = (low_pass(height, band_rows), low_pass(width, band_cols).T)

    by_rows = gains_by_rows(flat.T, tiles, width)
    dequantized = dequantize(raw, scales, by_rows, tiles, core, margin)
    gains = lax.all_to_all(by_rows, "tile", split_axis=0, concat_axis=0, tiled=True)
    narrow = strips(dequantized, gains, passes[1], frames_here, core, margin)
    arrived = lax.all_to_all(narrow, "tile", split_axis=0, concat_axis=0, tiled=True)
    handed = window_tables(tiles, passes, margin, core)
    field, estimate, rows, small = all_fields(
        spectrum_tile, pupil, patterns, led_row, led_col, tables, handed
    )
    window = windows(arrived, rows, small, frames_here, core)
    field, weight = fetch(field, estimate, window, patterns)

    swap_core = [(i, i ^ 1) for i in range(4)]
    swap_chip = [(i, i ^ 2) for i in range(4)]
    other = functools.partial(lax.ppermute, axis_name="grp")
    window_2 = other(window, perm=swap_chip)
    window_1 = other(window, perm=swap_core)
    window_2, field, weight = lax.optimization_barrier((window_2, field, weight))
    window_3 = other(window_2, perm=swap_core)

    fresh, high, low, for_a, for_b = update(
        field, weight, (window_1, window_2, window_3), spectrum_tile, pupil, patterns,
        led_row, led_col, tables, margin,
    )
    side_a, side_b = neighbours(for_a, for_b)
    core_part, edges = object_core(high, low, margin, core)
    stitched = blend(core_part, edges, side_a, side_b)
    return fresh[None], jnp.transpose(stitched, (0, 2, 1))


def solution(mesh):
    return jax.shard_map(
        body,
        mesh=mesh,
        in_specs=(
            P("grp", "tile", None),
            P("grp", "tile", None),
            P(None, "tile"),
            P("tile", None, None, None),
            P(),
            P(),
            P(),
            P(),
        ),
        out_specs=(P("tile", None, None, None), P(None, None, "tile")),
        check_vma=False,
    )
```

```python
import functools
import math

import jax
import jax.numpy as jnp
import ml_dtypes
import numpy as np
from jax import lax
from jax.experimental import pallas as pl
from jax.experimental.pallas import tpu as pltpu
from jax.sharding import PartitionSpec as P

OV = 32
BC = 32
STEP = 0.02
F32 = jnp.float32
BF16 = jnp.bfloat16
VMEM = pltpu.VMEM
SMEM = pltpu.SMEM
LIMIT = 30 << 20


def two_parts(table):
    table = np.asarray(table, np.float64)
    high = table.astype(ml_dtypes.bfloat16)
    low = (table - high.astype(np.float64)).astype(ml_dtypes.bfloat16)
    return high, low


def wave(places, freqs, length, norm):
    turns = np.outer(places, freqs) % length
    angle = turns * (2.0 * math.pi / length)
    return np.cos(angle) / math.sqrt(norm), np.sin(angle) / math.sqrt(norm)


def pairs(length):
    first = np.arange(1, length // 2, 2)
    return np.concatenate([first, length - first])


def low_pass(length, band):
    places = pairs(length)[:, None] - np.arange(length)[None, :]
    total = np.ones(places.shape)
    for freq in range(1, band):
        total += 2.0 * np.cos(2.0 * math.pi * ((freq * places) % length) / length)
    return total / length


def stacked_tables(height, width, band_rows, band_cols):
    row_re, row_im = wave(
        pairs(height), np.arange(band_rows) - band_rows // 2, height, band_rows
    )
    rows = np.block([[row_re, -row_im], [row_im, row_re]])
    col_re, col_im = wave(
        np.arange(band_cols) - band_cols // 2, pairs(width), width, band_cols
    )
    cols = np.block([[col_re, col_im], [-col_im, col_re]])
    half_rows, half_cols = height // 4, width // 4
    high, low = two_parts(np.concatenate([row_re[:half_rows], row_im[:half_rows]]).T)
    back_rows = np.block([[high, high], [low, np.zeros_like(low)]])
    back_cols = np.concatenate(
        two_parts(np.concatenate([col_re[:, :half_cols], col_im[:, :half_cols]], axis=1).T), axis=1
    )
    return rows, cols, back_rows, back_cols


def split(values):
    high = values.astype(BF16)
    return high, (values - high.astype(F32)).astype(BF16)


def mm(left, right):
    return jnp.dot(left, right, preferred_element_type=F32)


def vmem_spec(count):
    return [pl.BlockSpec(memory_space=VMEM)] * count


def lane_blocks(values):
    return [values[:, begin : begin + 128] for begin in range(0, values.shape[1], 128)]


def parts_rows(values):
    high = values.astype(BF16).astype(F32)
    return jnp.concatenate([high, values - high], axis=0).astype(BF16)


def rows_value(rows):
    rows = rows.astype(F32)
    return rows[:8, :128] + rows[8:, :128]


def gains_kernel(flat_ref, out_hbm, out, sems):
    core, height = flat_ref.shape
    tiles, rows_here, width = out_hbm.shape
    stores = []
    for number, begin in enumerate(range(0, width, 128)):
        length = min(128, core - begin)
        gains = flat_ref[begin : begin + length] - 1.0
        if length < 128:
            gains = jnp.concatenate([gains, jnp.zeros((128 - length, height), F32)], axis=0)
        by_rows = jnp.transpose(gains, (1, 0)).reshape(tiles, rows_here, 128)
        out[:, :, begin : begin + 128] = by_rows.astype(BF16)
        part = (slice(None), slice(None), pl.ds(begin, 128))
        store = pltpu.make_async_copy(out.at[part], out_hbm.at[part], sems.at[number])
        store.start()
        stores.append(store)
    for store in stores:
        store.wait()


def gains_by_rows(flat, tiles, width):
    core, height = flat.shape
    shape = (tiles, height // tiles, width)
    return pl.pallas_call(
        gains_kernel,
        out_shape=jax.ShapeDtypeStruct(shape, BF16),
        in_specs=vmem_spec(1),
        out_specs=pl.BlockSpec(memory_space=pltpu.HBM),
        scratch_shapes=[pltpu.VMEM(shape, BF16), pltpu.SemaphoreType.DMA((width // 128,))],
        compiler_params=pltpu.CompilerParams(vmem_limit_bytes=LIMIT),
        name="gains",
    )(flat)


def dequantize_kernel(raw_ref, scales_ref, after, out_ref, *, core, margin):
    lines, strip = raw_ref.shape
    coarse_rows, coarse_cols = scales_ref.shape
    tiles, _, width = out_ref.shape
    ratio = lines // coarse_rows
    row = lax.broadcasted_iota(jnp.int32, (lines, coarse_rows), 0)
    pick = lax.broadcasted_iota(jnp.int32, (lines, coarse_rows), 1)
    spread_rows = (row // ratio == pick).astype(F32).astype(BF16)
    factors = mm(spread_rows, scales_ref[...])
    wide = (coarse_cols // 128 + 1) * 128
    factors = jnp.concatenate([factors, jnp.zeros((lines, wide - coarse_cols), F32)], axis=1)

    blocks = []
    for tile in range(tiles):
        begin = (tile * core - margin) // BC
        blocks.append(pltpu.roll(factors, -begin % wide, 1)[:, :128].astype(BF16))
    block = lax.broadcasted_iota(jnp.int32, (128, width), 0)
    place = lax.broadcasted_iota(jnp.int32, (128, width), 1) + (-margin) % BC
    inside = (place >= block * BC) & (place < (block + 1) * BC)
    scales = mm(jnp.concatenate(blocks, axis=0), inside.astype(F32).astype(BF16))
    for tile in range(tiles):
        start = tile * core - margin
        base = max(start, 0) // 128 * 128
        span = min(width + 128, strip - base)
        codes = raw_ref[:, base : base + span].astype(F32)
        turn = (base - start) % span
        if turn:
            codes = pltpu.roll(codes, turn, 1)
        out_ref[tile] = codes[:, :width] * scales[tile * lines : (tile + 1) * lines]


def dequantize(raw, scales, after, tiles, core, margin):
    frames, rows_here, strip = raw.shape
    return pl.pallas_call(
        functools.partial(dequantize_kernel, core=core, margin=margin),
        out_shape=jax.ShapeDtypeStruct((tiles, frames * rows_here, core + 2 * margin), F32),
        in_specs=vmem_spec(2) + [pl.BlockSpec(memory_space=pl.ANY)],
        out_specs=pl.BlockSpec(memory_space=VMEM),
        compiler_params=pltpu.CompilerParams(vmem_limit_bytes=LIMIT),
        cost_estimate=pl.CostEstimate(
            flops=2_000_000_000, bytes_accessed=4_000_000, transcendentals=0
        ),
        name="dequantize",
    )(raw.reshape(frames * rows_here, strip), scales.reshape(-1, scales.shape[-1]), after)


def strips_kernel(dq_ref, gains_ref, lc_ref, out_hbm, out_ref, sems, *, frames, core, margin):
    tiles, lines, width = dq_ref.shape
    half_w = lc_ref.shape[1]
    rows_here = lines // frames
    line = lax.broadcasted_iota(jnp.int32, (1, width), 1)
    in_core = ((line >= margin) & (line < margin + core)).astype(F32)
    xc = (line.astype(F32) - margin - (core - 1) / 2.0) * in_core
    first_row = (lax.axis_index("tile") * rows_here).astype(F32)
    height = rows_here * tiles
    yc = lax.broadcasted_iota(jnp.int32, (rows_here, 1), 0).astype(F32)
    yc = yc + (first_row - (height - 1) / 2.0)
    lane = lax.broadcasted_iota(jnp.int32, (8, 128), 1)
    narrow_lane = lax.broadcasted_iota(jnp.int32, (1, 128), 1)

    lc_hi, lc_lo = lc_ref[:width], lc_ref[width:]
    own, stores = [], []

    all_yc = jnp.concatenate([yc] * frames, axis=0)

    def by_frame(values, weights):
        sums = []
        for frame in range(frames):
            one = values[frame * rows_here : (frame + 1) * rows_here]
            one = functools.reduce(
                jnp.add, [one[row : row + 8] for row in range(0, rows_here, 8)]
            )
            if weights is not None:
                one = one * weights
            one = functools.reduce(jnp.add, lane_blocks(one))
            one = jnp.sum(one, axis=1, keepdims=True)
            sums.append(jnp.sum(one, axis=0, keepdims=True))
        return jnp.concatenate(sums + [jnp.zeros((8 - frames, 1), F32)], axis=0)

    def windowed(tile):
        gains = pltpu.roll(gains_ref[tile].astype(F32), margin, 1)
        if tile > 0:
            end = gains_ref[tile - 1][:, width - 128 :].astype(F32)
            end = pltpu.roll(end, (2 * margin) + margin, 1)
            end = jnp.where(narrow_lane < margin, end, 0.0)
            gains = jnp.concatenate([gains[:, :128] + end, gains[:, 128:]], axis=1)
        if tile < tiles - 1:
            end = gains_ref[tile + 1][:, :128].astype(F32)
            end = pltpu.roll(end, 128 - margin, 1)
            end = jnp.where(narrow_lane >= 128 - margin, end, 0.0)
            gains = jnp.concatenate(
                [gains[:, : width - 128], gains[:, width - 128 :] + end], axis=1
            )
        gains = jnp.concatenate([gains + 1.0] * frames, axis=0)
        flattened = dq_ref[tile] * gains
        slope_y = by_frame(flattened * all_yc, in_core)
        slope_x = by_frame(flattened, xc)
        own.append(jnp.where(lane == 0, slope_y, jnp.where(lane == 1, slope_x, 0.0)))
        return flattened.astype(BF16)

    def finish(tile, one):
        mean = by_frame(one, None) * (1.0 / (rows_here * half_w))
        centred = []
        for frame in range(frames):
            cut = slice(frame * rows_here, (frame + 1) * rows_here)
            centred.append(one[cut] - mean[frame : frame + 1])
        centred = jnp.concatenate(centred, axis=0)
        for part in range(half_w // 128):
            columns = centred[:, part * 128 : (part + 1) * 128]
            out_ref[tile, part * lines : (part + 1) * lines] = columns.astype(BF16)
        packed = own[tile] + jnp.where(lane == 6, mean, 0.0)
        if tile > 0:
            packed += pltpu.roll(own[tile - 1], 2, 1)
        if tile < tiles - 1:
            packed += pltpu.roll(own[tile + 1], 4, 1)
        out_ref[tile, half_w // 128 * lines :] = parts_rows(packed)

    part_tiles = max(tiles // 2, 1)
    waiting = None
    for begin in range(0, tiles, part_tiles):
        pixels = jnp.concatenate([windowed(t) for t in range(begin, begin + part_tiles)], axis=0)
        if waiting is not None:
            finish(*waiting)
        narrow = mm(pixels, lc_hi) + mm(pixels, lc_lo)
        for number in range(part_tiles):
            one = (begin + number, narrow[number * lines : (number + 1) * lines])
            if number == part_tiles - 1 and begin + part_tiles < tiles:
                waiting = one
            else:
                finish(*one)
        done = begin + part_tiles - (1 if begin + part_tiles < tiles else 0)
        first = max(begin - 1, 0)
        span = pl.ds(first, done - first)
        store = pltpu.make_async_copy(out_ref.at[span], out_hbm.at[span], sems.at[begin // part_tiles])
        store.start()
        stores.append(store)
    for store in stores:
        store.wait()


def strips(dequantized, gains, lc, frames, core, margin):
    tiles, lines, _ = dequantized.shape
    shape = (tiles, lines * (lc.shape[1] // 128) + 16, 128)
    return pl.pallas_call(
        functools.partial(strips_kernel, frames=frames, core=core, margin=margin),
        out_shape=jax.ShapeDtypeStruct(shape, BF16),
        in_specs=vmem_spec(3),
        out_specs=pl.BlockSpec(memory_space=pltpu.HBM),
        scratch_shapes=[pltpu.VMEM(shape, BF16), pltpu.SemaphoreType.DMA((2,))],
        compiler_params=pltpu.CompilerParams(vmem_limit_bytes=LIMIT),
        name="strips",
    )(dequantized, gains, np.concatenate(two_parts(lc)))


def box_area(top, left, band_rows, band_cols):
    row = top // 8 * 8
    col = left // 128 * 128
    area = (
        pl.ds(pl.multiple_of(row, 8), band_rows + 8),
        pl.ds(pl.multiple_of(col, 128), band_cols + 128),
    )
    return area, top - row, left - col


def field_kernel(
    led_row, led_col, patterns, spec_ref, pupil_ref, cols_ref, rows_ref,
    rows_hbm, small_hbm, field_ref, estimate_ref, rows_out, small_out, wide, bright, sems, *, group,
):
    leds, half_h, half_w = bright.shape
    loads = [
        pltpu.make_async_copy(rows_hbm, rows_out, sems.at[0]),
        pltpu.make_async_copy(small_hbm, small_out, sems.at[1]),
    ]
    for load in loads:
        load.start()
    band_rows, band_cols = pupil_ref.shape[1:]
    width = spec_ref.shape[2]
    depth = 2 * band_cols
    wide[...] = jnp.zeros_like(wide)
    wide[:, : spec_ref.shape[1], :width] = spec_ref[...]

    def some(step, carry):
        boxes = []
        for place in range(group):
            led = step * group + place
            area, down, right = box_area(led_row[led], led_col[led], band_rows, band_cols)
            back = lax.rem(2 * band_cols - right, 2 * band_cols)
            up = lax.rem(band_rows + 8 - down, band_rows + 8)
            parts = []
            for part in range(2):
                strip = pltpu.roll(wide[(part, *area)], back, 1)
                parts.append(pltpu.roll(strip[:, :band_cols], up, 0)[:band_rows])
            lit_re = pupil_ref[0] * parts[0] - pupil_ref[1] * parts[1]
            lit_im = pupil_ref[0] * parts[1] + pupil_ref[1] * parts[0]
            boxes.append(jnp.concatenate([lit_re, lit_im], axis=1))
        high, low = split(jnp.concatenate(boxes, axis=0))
        cols_hi, cols_lo = cols_ref[:depth], cols_ref[depth:]
        spread = mm(high, cols_hi) + mm(high, cols_lo) + mm(low, cols_hi)
        for place in range(group):
            one = spread[place * band_rows : (place + 1) * band_rows]
            high, low = split(jnp.concatenate([one[:, :half_w], one[:, half_w:]], axis=0))
            field = mm(rows_ref[...], jnp.concatenate([high, low, high], axis=0))
            field_ref[step * group + place] = field
            bright[step * group + place] = field[:half_h] ** 2 + field[half_h:] ** 2
        return carry

    lax.fori_loop(0, leds // group, some, 0)

    def one_frame(frame, carry):
        total = bright[patterns[0, frame]]
        for lit in range(1, patterns.shape[0]):
            total += bright[patterns[lit, frame]]
        estimate_ref[frame] = total
        return carry

    lax.fori_loop(0, patterns.shape[1], one_frame, 0)
    for load in loads:
        load.wait()


def all_fields(spectrum, pupil, patterns, led_row, led_col, tables, handed, group=8):
    rows, cols, _, _ = tables
    leds = led_row.shape[0]
    _, height, width = spectrum.shape
    half_h, half_w = height // 2, width // 2
    high, low = two_parts(rows)
    return pl.pallas_call(
        functools.partial(field_kernel, group=group),
        out_shape=(
            jax.ShapeDtypeStruct((leds, 2 * half_h, half_w), F32),
            jax.ShapeDtypeStruct((patterns.shape[1], half_h, half_w), F32),
            *(jax.ShapeDtypeStruct(table.shape, table.dtype) for table in handed),
        ),
        in_specs=[pl.BlockSpec(memory_space=SMEM)] * 3
        + vmem_spec(4)
        + [pl.BlockSpec(memory_space=pltpu.HBM)] * 2,
        out_specs=tuple(vmem_spec(4)),
        scratch_shapes=[
            pltpu.VMEM((2, height + 8, width + 128), F32),
            pltpu.VMEM((leds, half_h, half_w), F32),
            pltpu.SemaphoreType.DMA((2,)),
        ],
        compiler_params=pltpu.CompilerParams(vmem_limit_bytes=LIMIT),
        cost_estimate=pl.CostEstimate(
            flops=8_000_000_000, bytes_accessed=16_000_000, transcendentals=0
        ),
        name="fields",
    )(
        led_row, led_col, patterns, spectrum, pupil, np.concatenate(two_parts(cols)),
        np.concatenate([high, high, low], axis=1),
        *(pltpu.with_memory_space_constraint(jnp.asarray(t), pltpu.HBM) for t in handed),
    )


def window_kernel(dq_ref, rows_ref, small_ref, window_ref, *, frames, core):
    slabs, lines, _ = dq_ref.shape
    half_h, half_w = rows_ref.shape[0], window_ref.shape[1]
    halves = half_w // 128
    lines = (lines - 16) // halves
    lr_sum, line = small_ref[:half_h, :128], small_ref[half_h:]
    rows_here = lines // frames
    height = slabs * rows_here
    over_y = 1.0 / (core * (height * (height * height - 1) / 12.0))
    over_x = 1.0 / (height * (core * (core * core - 1) / 12.0))
    lane = lax.broadcasted_iota(jnp.int32, (8, 128), 1)
    notes = [rows_value(dq_ref[slab, halves * lines :]) for slab in range(slabs)]
    slopes = functools.reduce(jnp.add, notes)
    slopes = slopes * jnp.where(lane % 2 == 0, over_y, over_x)
    slab_means = jnp.zeros((8, 128), F32)
    for slab in range(slabs):
        slab_means = jnp.where(lane == slab, notes[slab][:, 6:7], slab_means)
    values = []
    for slab in range(slabs):
        parts = [dq_ref[slab, part * lines : (part + 1) * lines] for part in range(halves)]
        values.append(jnp.concatenate(parts, axis=1))
    if rows_here % 16:
        values = [value.astype(F32) for value in values]
    means = []
    for frame in range(frames):
        cut = slice(frame * rows_here, (frame + 1) * rows_here)
        whole = jnp.concatenate([v[cut] for v in values], axis=0).astype(BF16)
        window = mm(rows_ref[...], jnp.concatenate([whole, whole], axis=0))
        level = jnp.sum(lr_sum * slab_means[frame : frame + 1], axis=1, keepdims=True)
        window = window + level
        tilt_y, tilt_x = 0.0, 0.0
        for side in range(3):
            tilt_y += line[2 * side : 2 * side + 1] * slopes[frame : frame + 1, 2 * side : 2 * side + 1]
            tilt_x += line[2 * side + 1 : 2 * side + 2] * slopes[frame : frame + 1, 2 * side + 1 : 2 * side + 2]
        window = window - lr_sum[:, 127:128] * tilt_y - tilt_x
        mean = jnp.sum(window, axis=0, keepdims=True)
        mean = jnp.sum(mean, axis=1, keepdims=True) * (1.0 / (half_h * half_w))
        means.append(jnp.broadcast_to(mean, (1, 128)))
        window_ref[frame * half_h : (frame + 1) * half_h] = (window - mean).astype(BF16)
    means = jnp.concatenate(means + [jnp.zeros((8 - frames, 128), F32)], axis=0)
    notes = parts_rows(means)
    window_ref[frames * half_h :] = jnp.concatenate([notes] * halves, axis=1)


def tilt_lines(width, margin, core, lc):
    local = np.arange(width) - margin
    lines = []
    for begin, end, shift in ((0, core, 0), (-margin, 0, core), (core, core + margin, -core)):
        on = (local >= begin) & (local < end)
        lines.append(on.astype(np.float64) @ lc)
        lines.append(((local + shift - (core - 1) / 2.0) * on) @ lc)
    return np.stack(lines + lines[:2])


def window_tables(tiles, passes, margin, core):
    lr, lc = passes
    half_h, height = lr.shape
    sums = np.zeros((half_h, lc.shape[1]))
    sums[:, :tiles] = lr.reshape(half_h, tiles, height // tiles).sum(axis=2)
    sums[:, 127] = lr @ (np.arange(height) - (height - 1) / 2.0)
    small = np.concatenate([sums, tilt_lines(lc.shape[0], margin, core, lc)])
    return np.concatenate(two_parts(lr), axis=1), small.astype(np.float32)


def windows(arrived, rows, small, frames, core):
    half_h, half_w = rows.shape[0], small.shape[1]
    return pl.pallas_call(
        functools.partial(window_kernel, frames=frames, core=core),
        out_shape=jax.ShapeDtypeStruct((frames * half_h + 16, half_w), BF16),
        in_specs=vmem_spec(3),
        out_specs=pl.BlockSpec(memory_space=VMEM),
        compiler_params=pltpu.CompilerParams(vmem_limit_bytes=LIMIT),
        name="windows",
    )(arrived, rows, small)


def add_frame(weight, patterns, frame, value):
    for lit in range(patterns.shape[0]):
        weight[patterns[lit, frame]] += value


def take_windows(weight, patterns, windows_here, slots, half_h):
    for window, slot in zip(windows_here, slots):
        frames_here = window.shape[0] // half_h
        owner = jnp.bitwise_xor(lax.axis_index("grp"), slot)
        means = rows_value(window[frames_here * half_h :])
        for place in range(frames_here):
            value = window[place * half_h : (place + 1) * half_h].astype(F32)
            value = -means[place : place + 1, 0:1] - value
            add_frame(weight, patterns, owner * frames_here + place, value)


def fetch_kernel(patterns, estimate_ref, window, field_hbm, field_ref, weight, sem):
    load = pltpu.make_async_copy(field_hbm, field_ref, sem)
    load.start()
    weight[...] = jnp.zeros_like(weight)
    frames, half_h, _ = estimate_ref.shape

    def one_frame(frame, carry):
        add_frame(weight, patterns, frame, estimate_ref[frame])
        return carry

    lax.fori_loop(0, frames, one_frame, 0)
    take_windows(weight, patterns, (window,), (0,), half_h)
    load.wait()


def fetch(field, estimate, window, patterns):
    leds = field.shape[0]
    return pl.pallas_call(
        fetch_kernel,
        out_shape=(
            jax.ShapeDtypeStruct(field.shape, F32),
            jax.ShapeDtypeStruct((leds, *estimate.shape[1:]), F32),
        ),
        in_specs=[pl.BlockSpec(memory_space=SMEM)]
        + vmem_spec(2)
        + [pl.BlockSpec(memory_space=pltpu.HBM)],
        out_specs=tuple(vmem_spec(2)),
        scratch_shapes=[pltpu.SemaphoreType.DMA],
        compiler_params=pltpu.CompilerParams(vmem_limit_bytes=LIMIT),
        cost_estimate=pl.CostEstimate(flops=0, bytes_accessed=16_000_000, transcendentals=0),
        name="fetch",
    )(patterns, estimate, window, pltpu.with_memory_space_constraint(field, pltpu.HBM))


def collect_kernel(patterns, w1, w2, weight_in, weight):
    take_windows(weight, patterns, (w1, w2), (1, 2), weight.shape[1])


def collect(weight, w1, w2, patterns):
    return pl.pallas_call(
        collect_kernel,
        out_shape=jax.ShapeDtypeStruct(weight.shape, F32),
        in_specs=[pl.BlockSpec(memory_space=SMEM)] + vmem_spec(3),
        out_specs=pl.BlockSpec(memory_space=VMEM),
        input_output_aliases={3: 0},
        compiler_params=pltpu.CompilerParams(vmem_limit_bytes=LIMIT),
        name="collect",
    )(patterns, w1, w2, weight)


def across(left, right):
    dims = (((1,), (1,)), ((), ()))
    return lax.dot_general(left, right, dims, preferred_element_type=F32)


def update_kernel(
    led_row, led_col, patterns, field_ref, weight_in, w3,
    spec_ref, pupil_ref, back_ref, big_hbm,
    fresh_hbm, high_ref, low_ref, first_ref, second_ref, weight,
    grads, fresh_ref, big, sides_ref, big_sem, fresh_sems, *, group,
):
    leds, half_h, half_w = weight.shape
    band_rows, band_cols = pupil_ref.shape[1:]
    height, width = spec_ref.shape[1:]
    is_odd = lax.rem(lax.axis_index("tile"), 2) == 1
    big_load = pltpu.make_async_copy(big_hbm, big, big_sem)
    big_load.start()
    grads[...] = jnp.zeros_like(grads)
    take_windows(weight, patterns, (w3,), (3,), half_h)

    left_rows = 2 * band_rows
    pair_rows, pair_cols = half_h // 2, half_w // 2

    def some(step, carry):
        backs = []
        for place in range(group):
            q = weight[step * group + place]
            field = field_ref[step * group + place]
            g_re, g_im = field[:half_h] * q, field[half_h:] * q
            re_a, re_b = g_re[:pair_rows], g_re[pair_rows:]
            im_a, im_b = g_im[:pair_rows], g_im[pair_rows:]
            to_re = jnp.concatenate([re_a + re_b, im_a - im_b], axis=0)
            to_im = jnp.concatenate([im_a + im_b, re_b - re_a], axis=0)
            high, low = split(jnp.concatenate([to_re, to_im], axis=1))
            both = mm(back_ref[:left_rows], jnp.concatenate([high, low], axis=0))
            back = both[:band_rows] + both[band_rows:]
            re_a, re_b = back[:, :pair_cols], back[:, pair_cols : 2 * pair_cols]
            im_a, im_b = back[:, 2 * pair_cols : 3 * pair_cols], back[:, 3 * pair_cols :]
            backs.append(jnp.concatenate([re_a + re_b, im_a - im_b], axis=1))
            backs.append(jnp.concatenate([im_a + im_b, re_b - re_a], axis=1))
        high, low = split(jnp.concatenate(backs, axis=0))
        cols = back_ref[left_rows:]
        both = mm(jnp.concatenate([high, low], axis=1), jnp.concatenate([cols, cols], axis=0))
        boxes = both[:, :band_cols] + both[:, band_cols:]
        for place in range(group):
            led = step * group + place
            begin = 2 * place * band_rows
            back_re = boxes[begin : begin + band_rows]
            back_im = boxes[begin + band_rows : begin + 2 * band_rows]
            parts = (
                pupil_ref[0] * back_re + pupil_ref[1] * back_im,
                pupil_ref[0] * back_im - pupil_ref[1] * back_re,
            )
            area, down, right = box_area(led_row[led], led_col[led], band_rows, band_cols)
            for part in range(2):
                filled = jnp.concatenate([parts[part], jnp.zeros((8, band_cols), F32)], axis=0)
                filled = pltpu.roll(filled, down, 0)
                filled = jnp.concatenate([filled, jnp.zeros((band_rows + 8, 128), F32)], axis=1)
                grads[(part, *area)] += pltpu.roll(filled, right, 1)
        return carry

    lax.fori_loop(0, leds // group, some, 0)
    fresh_re = spec_ref[0] - (4.0 * STEP) * grads[0, :height, :width]
    fresh_im = spec_ref[1] - (4.0 * STEP) * grads[1, :height, :width]
    for part, fresh in enumerate((fresh_re, fresh_im)):
        for number, block in enumerate(lane_blocks(fresh)):
            fresh_ref[part, number] = block
    stores = []
    for number in range(width // 128):
        store = pltpu.make_async_copy(
            fresh_ref.at[:, number], fresh_hbm.at[:, :, pl.ds(number * 128, 128)],
            fresh_sems.at[number],
        )
        store.start()
        stores.append(store)
    big_load.wait()

    def spread(parity, table):
        rows = pl.ds(parity, height // 2, stride=2)
        parts = [
            jnp.concatenate([fresh_ref[part, n, rows] for n in range(width // 128)], axis=1)
            for part in range(2)
        ]
        high, low = split(jnp.concatenate(parts, axis=0))
        table_hi, table_lo = big[table : table + height], big[table + height : table + 2 * height]
        left = jnp.concatenate([table_hi, table_lo, table_hi], axis=1)
        return mm(left, jnp.concatenate([high, high, low], axis=0))

    even, odd = spread(0, 0), spread(1, 2 * height)
    upper, lower = even + odd, even - odd
    half = height // 2
    z_re = jnp.concatenate([upper[:half], lower[:half]], axis=0)
    z_im = jnp.concatenate([upper[half:], lower[half:]], axis=0)

    near = [z[:, : width // 2] for z in (z_re, z_im)]
    far = [z[:, width // 2 :] for z in (z_re, z_im)]
    mixed = [a + b for a, b in zip(near, far)] + [a - b for a, b in zip(near, far)]
    high, low = split(jnp.concatenate(mixed, axis=1))
    high_ref[...] = high
    low_ref[...] = low
    count = sides_ref.shape[1] // 2
    for parity in range(2):
        table = 4 * height + 4 * count * parity
        cut = slice(parity * width, (parity + 1) * width)
        side_hi = jnp.concatenate([big[table : table + count], big[table + count : table + 2 * count]], axis=1)
        side_lo = jnp.concatenate(
            [big[table + 2 * count : table + 3 * count], big[table + 3 * count : table + 4 * count]], axis=1
        )
        one = across(side_hi, high[:, cut]) + across(side_lo, high[:, cut])
        one = one + across(side_hi, low[:, cut])
        for number, block in enumerate(lane_blocks(one)):
            sides_ref[number, pl.ds(parity, count, stride=2)] = block
    sides = jnp.concatenate([sides_ref[n] for n in range(height // 128)], axis=1)
    to_left, to_right = sides[:count], sides[count:]
    first_ref[...] = jnp.where(is_odd, to_left, to_right)
    second_ref[...] = jnp.where(is_odd, to_right, to_left)
    for store in stores:
        store.wait()


def update(
    field, weight, window, spectrum, pupil, patterns, led_row, led_col, tables,
    margin, group=8,
):
    _, _, back_rows, back_cols = tables
    leds = led_row.shape[0]
    _, height, width = spectrum.shape
    half_h, half_w = height // 2, width // 2
    big = []
    for parity in range(2):
        freqs = np.arange(parity, height, 2) - height // 2
        re, im = wave(np.arange(height // 2), freqs, height, height)
        big += two_parts(np.block([[re, -im], [im, re]]))
    for parity in range(2):
        left = np.arange(parity, margin, 2)
        freqs = np.arange(width // 2) - width // 2
        l_re, l_im = wave(left, freqs, width, width)
        r_re, r_im = wave(left + width - margin, freqs, width, width)
        from_re = two_parts(np.concatenate([l_re, l_im, r_re, r_im]))
        from_im = two_parts(np.concatenate([-l_im, l_re, -r_im, r_re]))
        big += [from_re[0], from_im[0], from_re[1], from_im[1]]
    big = np.concatenate(big)
    back = np.concatenate([back_rows, back_cols])
    out_shape = (
        jax.ShapeDtypeStruct(spectrum.shape, F32),
        jax.ShapeDtypeStruct((height, 2 * width), BF16),
        jax.ShapeDtypeStruct((height, 2 * width), BF16),
        jax.ShapeDtypeStruct((2 * margin, height), F32),
        jax.ShapeDtypeStruct((2 * margin, height), F32),
        jax.ShapeDtypeStruct(weight.shape, F32),
    )
    return pl.pallas_call(
        functools.partial(update_kernel, group=group),
        out_shape=out_shape,
        in_specs=[pl.BlockSpec(memory_space=SMEM)] * 3
        + vmem_spec(6)
        + [pl.BlockSpec(memory_space=pltpu.HBM)],
        out_specs=(pl.BlockSpec(memory_space=pltpu.HBM), *vmem_spec(5)),
        input_output_aliases={4: 5},
        scratch_shapes=[
            pltpu.VMEM((2, height + 8, width + 128), F32),
            pltpu.VMEM((2, width // 128, height, 128), F32),
            pltpu.VMEM(big.shape, BF16),
            pltpu.VMEM((height // 128, 4 * margin, 128), F32),
            pltpu.SemaphoreType.DMA,
            pltpu.SemaphoreType.DMA((width // 128,)),
        ],
        compiler_params=pltpu.CompilerParams(vmem_limit_bytes=LIMIT),
        name="update",
    )(
        led_row, led_col, patterns, field, weight, window, spectrum, pupil, back,
        pltpu.with_memory_space_constraint(jnp.asarray(big), pltpu.HBM),
    )[:5]


def object_kernel(high_ref, low_ref, table_ref, out_hbm, edges_ref, out, sems):
    core = out.shape[2]
    margin = edges_ref.shape[2]
    half = core // 2
    depth = high_ref.shape[1] // 4
    cuts = (slice(0, half // 2 // 16 * 16 + 16), slice(half // 2 // 16 * 16 + 16, half))
    stores = []
    for number, cut in enumerate(cuts):
        for parity in range(2):
            lefts = []
            for begin in (4 * parity * half, (4 * parity + 1) * half):
                rows = slice(begin + cut.start, begin + cut.stop)
                more = slice(rows.start + 2 * half, rows.stop + 2 * half)
                lefts.append(jnp.concatenate([table_ref[rows], table_ref[more], table_ref[rows]], axis=1))
            left = jnp.concatenate(lefts, axis=0)
            products = []
            for part in range(2):
                lanes = slice((2 * parity + part) * depth, (2 * parity + part + 1) * depth)
                z_hi, z_lo = high_ref[:, lanes], low_ref[:, lanes]
                products.append(across(left, jnp.concatenate([z_hi, z_hi, z_lo], axis=1)))
            count = cut.stop - cut.start
            rows = pl.ds(2 * cut.start + parity, count, stride=2)
            real = products[0][:count] - products[1][count:]
            imaginary = products[0][count:] + products[1][:count]
            for part, values in enumerate((real, imaginary)):
                for lanes, block in enumerate(lane_blocks(values)):
                    out[part, lanes, rows] = block
        span = pl.ds(2 * cut.start, 2 * (cut.stop - cut.start))
        for lanes in range(out.shape[1]):
            store = pltpu.make_async_copy(
                out.at[:, lanes, span], out_hbm.at[:, span, pl.ds(lanes * 128, 128)],
                sems.at[number, lanes],
            )
            store.start()
            stores.append(store)
    for part in range(2):
        for side, begin in enumerate((0, core - margin)):
            edge = [out[part, n, begin : begin + margin] for n in range(out.shape[1])]
            edges_ref[part, side] = jnp.concatenate(edge, axis=1)
    for store in stores:
        store.wait()


def object_core(high, low, margin, core):
    height, width = high.shape[0], high.shape[1] // 2
    table = []
    for parity in range(2):
        places = margin + np.arange(parity, core, 2)
        table += two_parts(
            np.concatenate(wave(places, np.arange(width // 2) - width // 2, width, width))
        )
    table = np.concatenate(table)
    return pl.pallas_call(
        object_kernel,
        out_shape=(
            jax.ShapeDtypeStruct((2, core, height), F32),
            jax.ShapeDtypeStruct((2, 2, margin, height), F32),
        ),
        in_specs=vmem_spec(3),
        out_specs=(pl.BlockSpec(memory_space=pltpu.HBM), pl.BlockSpec(memory_space=VMEM)),
        scratch_shapes=[
            pltpu.VMEM((2, height // 128, core, 128), F32),
            pltpu.SemaphoreType.DMA((2, height // 128)),
        ],
        compiler_params=pltpu.CompilerParams(vmem_limit_bytes=LIMIT),
        cost_estimate=pl.CostEstimate(
            flops=3_000_000_000, bytes_accessed=5_000_000, transcendentals=0
        ),
        name="object",
    )(high, low, table)


def blend_kernel(first_ref, second_ref, edges_ref, core_hbm, out_hbm, mixed, sems):
    tile = lax.axis_index("tile")
    is_odd = lax.rem(tile, 2) == 1
    margin, core = edges_ref.shape[2], out_hbm.shape[1]
    k = lax.broadcasted_iota(jnp.int32, (margin, 1), 0).astype(F32)
    span = 2.0 * margin
    from_left = jnp.where(is_odd, first_ref[...], second_ref[...])
    from_right = jnp.where(is_odd, second_ref[...], first_ref[...])
    sides = (
        ((k + margin + 0.5) / span, (margin - k - 0.5) / span, tile > 0, from_left, 0),
        (
            (span - k - 0.5) / span, (k + 0.5) / span, tile < lax.axis_size("tile") - 1, from_right,
            core - margin,
        ),
    )
    stores = []
    for side, (own_w, other_w, has_other, other, begin) in enumerate(sides):
        own_w = jnp.where(has_other, own_w, 1.0)
        other_w = jnp.where(has_other, other_w, 0.0)
        for part in range(2):
            cut = slice(part * margin, (part + 1) * margin)
            mixed[side, part] = edges_ref[part, side] * own_w + other[cut] * other_w
        store = pltpu.make_async_copy(
            mixed.at[side], out_hbm.at[:, pl.ds(begin, margin)], sems.at[side]
        )
        store.start()
        stores.append(store)
    for store in stores:
        store.wait()


def blend(core_part, edges, first, second):
    return pl.pallas_call(
        blend_kernel,
        out_shape=jax.ShapeDtypeStruct(core_part.shape, F32),
        in_specs=vmem_spec(3) + [pl.BlockSpec(memory_space=pltpu.HBM)],
        out_specs=pl.BlockSpec(memory_space=pltpu.HBM),
        input_output_aliases={3: 0},
        scratch_shapes=[pltpu.VMEM(edges.shape, F32), pltpu.SemaphoreType.DMA((2,))],
        compiler_params=pltpu.CompilerParams(vmem_limit_bytes=LIMIT),
        name="blend",
    )(first, second, edges, core_part)


def body(raw, scales, flat, spectrum, pupil, patterns, led_row, led_col):
    height, core = flat.shape
    margin = OV // 2
    width = core + OV
    tiles = lax.axis_size("tile")
    frames_here = raw.shape[0]
    band_rows, band_cols = pupil.shape[1:]
    spectrum_tile = spectrum[0]
    patterns = patterns.T

    swap_a = [(i, i ^ 1) for i in range(tiles)]
    swap_b = [(i, ((i + 1) ^ 1) - 1) for i in range(1, tiles - 1)]

    def neighbours(for_a, for_b):
        return lax.ppermute(for_a, "tile", swap_a), lax.ppermute(for_b, "tile", swap_b)

    tables = stacked_tables(height, width, band_rows, band_cols)
    passes = (low_pass(height, band_rows), low_pass(width, band_cols).T)

    by_rows = gains_by_rows(flat.T, tiles, width)
    dequantized = dequantize(raw, scales, by_rows, tiles, core, margin)
    gains = lax.all_to_all(by_rows, "tile", split_axis=0, concat_axis=0, tiled=True)
    narrow = strips(dequantized, gains, passes[1], frames_here, core, margin)
    arrived = lax.all_to_all(narrow, "tile", split_axis=0, concat_axis=0, tiled=True)
    handed = window_tables(tiles, passes, margin, core)
    field, estimate, rows, small = all_fields(
        spectrum_tile, pupil, patterns, led_row, led_col, tables, handed
    )
    window = windows(arrived, rows, small, frames_here, core)
    field, weight = fetch(field, estimate, window, patterns)

    swap_core = [(i, i ^ 1) for i in range(4)]
    swap_chip = [(i, i ^ 2) for i in range(4)]
    other = functools.partial(lax.ppermute, axis_name="grp")
    window_2 = other(window, perm=swap_chip)
    window_1 = other(window, perm=swap_core)
    window_2, field, weight = lax.optimization_barrier((window_2, field, weight))
    window_3 = other(window_2, perm=swap_core)
    weight = collect(weight, window_1, window_2, patterns)

    fresh, high, low, for_a, for_b = update(
        field, weight, window_3, spectrum_tile, pupil, patterns,
        led_row, led_col, tables, margin,
    )
    side_a, side_b = neighbours(for_a, for_b)
    core_part, edges = object_core(high, low, margin, core)
    stitched = blend(core_part, edges, side_a, side_b)
    return fresh[None], jnp.transpose(stitched, (0, 2, 1))


def solution(mesh):
    return jax.shard_map(
        body,
        mesh=mesh,
        in_specs=(
            P("grp", "tile", None),
            P("grp", "tile", None),
            P(None, "tile"),
            P("tile", None, None, None),
            P(),
            P(),
            P(),
            P(),
        ),
        out_specs=(P("tile", None, None, None), P(None, None, "tile")),
        check_vma=False,
    )
```

```python
import functools
import math

import jax
import jax.numpy as jnp
import ml_dtypes
import numpy as np
from jax import lax
from jax.experimental import pallas as pl
from jax.experimental.pallas import tpu as pltpu
from jax.sharding import PartitionSpec as P

OV = 32
BC = 32
STEP = 0.02
F32 = jnp.float32
BF16 = jnp.bfloat16
VMEM = pltpu.VMEM
SMEM = pltpu.SMEM
LIMIT = 30 << 20


def two_parts(table):
    table = np.asarray(table, np.float64)
    high = table.astype(ml_dtypes.bfloat16)
    low = (table - high.astype(np.float64)).astype(ml_dtypes.bfloat16)
    return high, low


def wave(places, freqs, length, norm):
    turns = np.outer(places, freqs) % length
    angle = turns * (2.0 * math.pi / length)
    return np.cos(angle) / math.sqrt(norm), np.sin(angle) / math.sqrt(norm)


def pairs(length):
    first = np.arange(1, length // 2, 2)
    return np.concatenate([first, length - first])


def low_pass(length, band):
    places = pairs(length)[:, None] - np.arange(length)[None, :]
    total = np.ones(places.shape)
    for freq in range(1, band):
        total += 2.0 * np.cos(2.0 * math.pi * ((freq * places) % length) / length)
    return total / length


def stacked_tables(height, width, band_rows, band_cols):
    row_re, row_im = wave(
        pairs(height), np.arange(band_rows) - band_rows // 2, height, band_rows
    )
    rows = np.block([[row_re, -row_im], [row_im, row_re]])
    col_re, col_im = wave(
        np.arange(band_cols) - band_cols // 2, pairs(width), width, band_cols
    )
    cols = np.block([[col_re, col_im], [-col_im, col_re]])
    half_rows, half_cols = height // 4, width // 4
    high, low = two_parts(np.concatenate([row_re[:half_rows], row_im[:half_rows]]).T)
    back_rows = np.block([[high, high], [low, np.zeros_like(low)]])
    back_cols = np.concatenate(
        two_parts(np.concatenate([col_re[:, :half_cols], col_im[:, :half_cols]], axis=1).T), axis=1
    )
    return rows, cols, back_rows, back_cols


def split(values):
    high = values.astype(BF16)
    return high, (values - high.astype(F32)).astype(BF16)


def mm(left, right):
    return jnp.dot(left, right, preferred_element_type=F32)


def vmem_spec(count):
    return [pl.BlockSpec(memory_space=VMEM)] * count


def lane_blocks(values):
    return [values[:, begin : begin + 128] for begin in range(0, values.shape[1], 128)]


def parts_rows(values):
    high = values.astype(BF16).astype(F32)
    return jnp.concatenate([high, values - high], axis=0).astype(BF16)


def rows_value(rows):
    rows = rows.astype(F32)
    return rows[:8, :128] + rows[8:, :128]


def gains_kernel(flat_ref, out_hbm, out, sems):
    core, height = flat_ref.shape
    tiles, rows_here, width = out_hbm.shape
    stores = []
    for number, begin in enumerate(range(0, width, 128)):
        length = min(128, core - begin)
        gains = flat_ref[begin : begin + length] - 1.0
        if length < 128:
            gains = jnp.concatenate([gains, jnp.zeros((128 - length, height), F32)], axis=0)
        by_rows = jnp.transpose(gains, (1, 0)).reshape(tiles, rows_here, 128)
        out[:, :, begin : begin + 128] = by_rows.astype(BF16)
        part = (slice(None), slice(None), pl.ds(begin, 128))
        store = pltpu.make_async_copy(out.at[part], out_hbm.at[part], sems.at[number])
        store.start()
        stores.append(store)
    for store in stores:
        store.wait()


def gains_by_rows(flat, tiles, width):
    core, height = flat.shape
    shape = (tiles, height // tiles, width)
    return pl.pallas_call(
        gains_kernel,
        out_shape=jax.ShapeDtypeStruct(shape, BF16),
        in_specs=vmem_spec(1),
        out_specs=pl.BlockSpec(memory_space=pltpu.HBM),
        scratch_shapes=[pltpu.VMEM(shape, BF16), pltpu.SemaphoreType.DMA((width // 128,))],
        compiler_params=pltpu.CompilerParams(vmem_limit_bytes=LIMIT),
        name="gains",
    )(flat)


def dequantize_kernel(raw_ref, scales_ref, after, out_ref, *, core, margin):
    lines, strip = raw_ref.shape
    coarse_rows, coarse_cols = scales_ref.shape
    tiles, _, width = out_ref.shape
    ratio = lines // coarse_rows
    row = lax.broadcasted_iota(jnp.int32, (lines, coarse_rows), 0)
    pick = lax.broadcasted_iota(jnp.int32, (lines, coarse_rows), 1)
    spread_rows = (row // ratio == pick).astype(F32).astype(BF16)
    factors = mm(spread_rows, scales_ref[...])
    wide = (coarse_cols // 128 + 1) * 128
    factors = jnp.concatenate([factors, jnp.zeros((lines, wide - coarse_cols), F32)], axis=1)

    blocks = []
    for tile in range(tiles):
        begin = (tile * core - margin) // BC
        blocks.append(pltpu.roll(factors, -begin % wide, 1)[:, :128].astype(BF16))
    block = lax.broadcasted_iota(jnp.int32, (128, width), 0)
    place = lax.broadcasted_iota(jnp.int32, (128, width), 1) + (-margin) % BC
    inside = (place >= block * BC) & (place < (block + 1) * BC)
    scales = mm(jnp.concatenate(blocks, axis=0), inside.astype(F32).astype(BF16))
    for tile in range(tiles):
        start = tile * core - margin
        base = max(start, 0) // 128 * 128
        span = min(width + 128, strip - base)
        codes = raw_ref[:, base : base + span].astype(F32)
        turn = (base - start) % span
        if turn:
            codes = pltpu.roll(codes, turn, 1)
        out_ref[tile] = codes[:, :width] * scales[tile * lines : (tile + 1) * lines]


def dequantize(raw, scales, after, tiles, core, margin):
    frames, rows_here, strip = raw.shape
    return pl.pallas_call(
        functools.partial(dequantize_kernel, core=core, margin=margin),
        out_shape=jax.ShapeDtypeStruct((tiles, frames * rows_here, core + 2 * margin), F32),
        in_specs=vmem_spec(2) + [pl.BlockSpec(memory_space=pl.ANY)],
        out_specs=pl.BlockSpec(memory_space=VMEM),
        compiler_params=pltpu.CompilerParams(vmem_limit_bytes=LIMIT),
        cost_estimate=pl.CostEstimate(
            flops=2_000_000_000, bytes_accessed=4_000_000, transcendentals=0
        ),
        name="dequantize",
    )(raw.reshape(frames * rows_here, strip), scales.reshape(-1, scales.shape[-1]), after)


def strips_kernel(dq_ref, gains_ref, lc_ref, out_hbm, out_ref, sems, *, frames, core, margin):
    tiles, lines, width = dq_ref.shape
    half_w = lc_ref.shape[1]
    rows_here = lines // frames
    line = lax.broadcasted_iota(jnp.int32, (1, width), 1)
    in_core = ((line >= margin) & (line < margin + core)).astype(F32)
    xc = (line.astype(F32) - margin - (core - 1) / 2.0) * in_core
    first_row = (lax.axis_index("tile") * rows_here).astype(F32)
    height = rows_here * tiles
    yc = lax.broadcasted_iota(jnp.int32, (rows_here, 1), 0).astype(F32)
    yc = yc + (first_row - (height - 1) / 2.0)
    lane = lax.broadcasted_iota(jnp.int32, (8, 128), 1)
    narrow_lane = lax.broadcasted_iota(jnp.int32, (1, 128), 1)

    lc_hi, lc_lo = lc_ref[:width], lc_ref[width:]
    own, stores = [], []

    all_yc = jnp.concatenate([yc] * frames, axis=0)

    def by_frame(values, weights):
        sums = []
        for frame in range(frames):
            one = values[frame * rows_here : (frame + 1) * rows_here]
            one = functools.reduce(
                jnp.add, [one[row : row + 8] for row in range(0, rows_here, 8)]
            )
            if weights is not None:
                one = one * weights
            one = functools.reduce(jnp.add, lane_blocks(one))
            one = jnp.sum(one, axis=1, keepdims=True)
            sums.append(jnp.sum(one, axis=0, keepdims=True))
        return jnp.concatenate(sums + [jnp.zeros((8 - frames, 1), F32)], axis=0)

    def windowed(tile):
        gains = pltpu.roll(gains_ref[tile].astype(F32), margin, 1)
        if tile > 0:
            end = gains_ref[tile - 1][:, width - 128 :].astype(F32)
            end = pltpu.roll(end, (2 * margin) + margin, 1)
            end = jnp.where(narrow_lane < margin, end, 0.0)
            gains = jnp.concatenate([gains[:, :128] + end, gains[:, 128:]], axis=1)
        if tile < tiles - 1:
            end = gains_ref[tile + 1][:, :128].astype(F32)
            end = pltpu.roll(end, 128 - margin, 1)
            end = jnp.where(narrow_lane >= 128 - margin, end, 0.0)
            gains = jnp.concatenate(
                [gains[:, : width - 128], gains[:, width - 128 :] + end], axis=1
            )
        gains = jnp.concatenate([gains + 1.0] * frames, axis=0)
        flattened = dq_ref[tile] * gains
        slope_y = by_frame(flattened * all_yc, in_core)
        slope_x = by_frame(flattened, xc)
        own.append(jnp.where(lane == 0, slope_y, jnp.where(lane == 1, slope_x, 0.0)))
        return flattened.astype(BF16)

    def finish(tile, one):
        mean = by_frame(one, None) * (1.0 / (rows_here * half_w))
        centred = []
        for frame in range(frames):
            cut = slice(frame * rows_here, (frame + 1) * rows_here)
            centred.append(one[cut] - mean[frame : frame + 1])
        centred = jnp.concatenate(centred, axis=0)
        for part in range(half_w // 128):
            columns = centred[:, part * 128 : (part + 1) * 128]
            out_ref[tile, part * lines : (part + 1) * lines] = columns.astype(BF16)
        packed = own[tile] + jnp.where(lane == 6, mean, 0.0)
        if tile > 0:
            packed += pltpu.roll(own[tile - 1], 2, 1)
        if tile < tiles - 1:
            packed += pltpu.roll(own[tile + 1], 4, 1)
        out_ref[tile, half_w // 128 * lines :] = parts_rows(packed)

    part_tiles = max(tiles // 2, 1)
    waiting = None
    for begin in range(0, tiles, part_tiles):
        pixels = jnp.concatenate([windowed(t) for t in range(begin, begin + part_tiles)], axis=0)
        if waiting is not None:
            finish(*waiting)
        narrow = mm(pixels, lc_hi) + mm(pixels, lc_lo)
        for number in range(part_tiles):
            one = (begin + number, narrow[number * lines : (number + 1) * lines])
            if number == part_tiles - 1 and begin + part_tiles < tiles:
                waiting = one
            else:
                finish(*one)
        done = begin + part_tiles - (1 if begin + part_tiles < tiles else 0)
        first = max(begin - 1, 0)
        span = pl.ds(first, done - first)
        store = pltpu.make_async_copy(out_ref.at[span], out_hbm.at[span], sems.at[begin // part_tiles])
        store.start()
        stores.append(store)
    for store in stores:
        store.wait()


def strips(dequantized, gains, lc, frames, core, margin):
    tiles, lines, _ = dequantized.shape
    shape = (tiles, lines * (lc.shape[1] // 128) + 16, 128)
    return pl.pallas_call(
        functools.partial(strips_kernel, frames=frames, core=core, margin=margin),
        out_shape=jax.ShapeDtypeStruct(shape, BF16),
        in_specs=vmem_spec(3),
        out_specs=pl.BlockSpec(memory_space=pltpu.HBM),
        scratch_shapes=[pltpu.VMEM(shape, BF16), pltpu.SemaphoreType.DMA((2,))],
        compiler_params=pltpu.CompilerParams(vmem_limit_bytes=LIMIT),
        name="strips",
    )(dequantized, gains, np.concatenate(two_parts(lc)))


def box_area(top, left, band_rows, band_cols):
    row = top // 8 * 8
    col = left // 128 * 128
    area = (
        pl.ds(pl.multiple_of(row, 8), band_rows + 8),
        pl.ds(pl.multiple_of(col, 128), band_cols + 128),
    )
    return area, top - row, left - col


def field_kernel(
    led_row, led_col, patterns, spec_ref, pupil_ref, cols_ref, rows_ref,
    rows_hbm, small_hbm, field_ref, estimate_ref, rows_out, small_out, wide, bright, sems, *, group,
):
    leds, half_h, half_w = bright.shape
    loads = [
        pltpu.make_async_copy(rows_hbm, rows_out, sems.at[0]),
        pltpu.make_async_copy(small_hbm, small_out, sems.at[1]),
    ]
    for load in loads:
        load.start()
    band_rows, band_cols = pupil_ref.shape[1:]
    width = spec_ref.shape[2]
    depth = 2 * band_cols
    wide[...] = jnp.zeros_like(wide)
    wide[:, : spec_ref.shape[1], :width] = spec_ref[...]

    def some(step, carry):
        boxes = []
        for place in range(group):
            led = step * group + place
            area, down, right = box_area(led_row[led], led_col[led], band_rows, band_cols)
            back = lax.rem(2 * band_cols - right, 2 * band_cols)
            up = lax.rem(band_rows + 8 - down, band_rows + 8)
            parts = []
            for part in range(2):
                strip = pltpu.roll(wide[(part, *area)], back, 1)
                parts.append(pltpu.roll(strip[:, :band_cols], up, 0)[:band_rows])
            lit_re = pupil_ref[0] * parts[0] - pupil_ref[1] * parts[1]
            lit_im = pupil_ref[0] * parts[1] + pupil_ref[1] * parts[0]
            boxes.append(jnp.concatenate([lit_re, lit_im], axis=1))
        high, low = split(jnp.concatenate(boxes, axis=0))
        cols_hi, cols_lo = cols_ref[:depth], cols_ref[depth:]
        spread = mm(high, cols_hi) + mm(high, cols_lo) + mm(low, cols_hi)
        for place in range(group):
            one = spread[place * band_rows : (place + 1) * band_rows]
            high, low = split(jnp.concatenate([one[:, :half_w], one[:, half_w:]], axis=0))
            field = mm(rows_ref[...], jnp.concatenate([high, low, high], axis=0))
            field_ref[step * group + place] = field
            bright[step * group + place] = field[:half_h] ** 2 + field[half_h:] ** 2
        return carry

    lax.fori_loop(0, leds // group, some, 0)

    def one_frame(frame, carry):
        total = bright[patterns[0, frame]]
        for lit in range(1, patterns.shape[0]):
            total += bright[patterns[lit, frame]]
        estimate_ref[frame] = total
        return carry

    lax.fori_loop(0, patterns.shape[1], one_frame, 0)
    for load in loads:
        load.wait()


def all_fields(spectrum, pupil, patterns, led_row, led_col, tables, handed, group=8):
    rows, cols, _, _ = tables
    leds = led_row.shape[0]
    _, height, width = spectrum.shape
    half_h, half_w = height // 2, width // 2
    high, low = two_parts(rows)
    return pl.pallas_call(
        functools.partial(field_kernel, group=group),
        out_shape=(
            jax.ShapeDtypeStruct((leds, 2 * half_h, half_w), F32),
            jax.ShapeDtypeStruct((patterns.shape[1], half_h, half_w), F32),
            *(jax.ShapeDtypeStruct(table.shape, table.dtype) for table in handed),
        ),
        in_specs=[pl.BlockSpec(memory_space=SMEM)] * 3
        + vmem_spec(4)
        + [pl.BlockSpec(memory_space=pltpu.HBM)] * 2,
        out_specs=tuple(vmem_spec(4)),
        scratch_shapes=[
            pltpu.VMEM((2, height + 8, width + 128), F32),
            pltpu.VMEM((leds, half_h, half_w), F32),
            pltpu.SemaphoreType.DMA((2,)),
        ],
        compiler_params=pltpu.CompilerParams(vmem_limit_bytes=LIMIT),
        cost_estimate=pl.CostEstimate(
            flops=8_000_000_000, bytes_accessed=16_000_000, transcendentals=0
        ),
        name="fields",
    )(
        led_row, led_col, patterns, spectrum, pupil, np.concatenate(two_parts(cols)),
        np.concatenate([high, high, low], axis=1),
        *(pltpu.with_memory_space_constraint(jnp.asarray(t), pltpu.HBM) for t in handed),
    )


def window_kernel(dq_ref, rows_ref, small_ref, window_ref, *, frames, core):
    slabs, lines, _ = dq_ref.shape
    half_h, half_w = rows_ref.shape[0], window_ref.shape[1]
    halves = half_w // 128
    lines = (lines - 16) // halves
    lr_sum, line = small_ref[:half_h, :128], small_ref[half_h:]
    rows_here = lines // frames
    height = slabs * rows_here
    over_y = 1.0 / (core * (height * (height * height - 1) / 12.0))
    over_x = 1.0 / (height * (core * (core * core - 1) / 12.0))
    lane = lax.broadcasted_iota(jnp.int32, (8, 128), 1)
    notes = [rows_value(dq_ref[slab, halves * lines :]) for slab in range(slabs)]
    slopes = functools.reduce(jnp.add, notes)
    slopes = slopes * jnp.where(lane % 2 == 0, over_y, over_x)
    slab_means = jnp.zeros((8, 128), F32)
    for slab in range(slabs):
        slab_means = jnp.where(lane == slab, notes[slab][:, 6:7], slab_means)
    values = []
    for slab in range(slabs):
        parts = [dq_ref[slab, part * lines : (part + 1) * lines] for part in range(halves)]
        values.append(jnp.concatenate(parts, axis=1))
    if rows_here % 16:
        values = [value.astype(F32) for value in values]
    means = []
    for frame in range(frames):
        cut = slice(frame * rows_here, (frame + 1) * rows_here)
        whole = jnp.concatenate([v[cut] for v in values], axis=0).astype(BF16)
        window = mm(rows_ref[...], jnp.concatenate([whole, whole], axis=0))
        level = jnp.sum(lr_sum * slab_means[frame : frame + 1], axis=1, keepdims=True)
        window = window + level
        tilt_y, tilt_x = 0.0, 0.0
        for side in range(3):
            tilt_y += line[2 * side : 2 * side + 1] * slopes[frame : frame + 1, 2 * side : 2 * side + 1]
            tilt_x += line[2 * side + 1 : 2 * side + 2] * slopes[frame : frame + 1, 2 * side + 1 : 2 * side + 2]
        window = window - lr_sum[:, 127:128] * tilt_y - tilt_x
        mean = jnp.sum(window, axis=0, keepdims=True)
        mean = jnp.sum(mean, axis=1, keepdims=True) * (1.0 / (half_h * half_w))
        means.append(jnp.broadcast_to(mean, (1, 128)))
        window_ref[frame * half_h : (frame + 1) * half_h] = (window - mean).astype(BF16)
    means = jnp.concatenate(means + [jnp.zeros((8 - frames, 128), F32)], axis=0)
    notes = parts_rows(means)
    window_ref[frames * half_h :] = jnp.concatenate([notes] * halves, axis=1)


def tilt_lines(width, margin, core, lc):
    local = np.arange(width) - margin
    lines = []
    for begin, end, shift in ((0, core, 0), (-margin, 0, core), (core, core + margin, -core)):
        on = (local >= begin) & (local < end)
        lines.append(on.astype(np.float64) @ lc)
        lines.append(((local + shift - (core - 1) / 2.0) * on) @ lc)
    return np.stack(lines + lines[:2])


def window_tables(tiles, passes, margin, core):
    lr, lc = passes
    half_h, height = lr.shape
    sums = np.zeros((half_h, lc.shape[1]))
    sums[:, :tiles] = lr.reshape(half_h, tiles, height // tiles).sum(axis=2)
    sums[:, 127] = lr @ (np.arange(height) - (height - 1) / 2.0)
    small = np.concatenate([sums, tilt_lines(lc.shape[0], margin, core, lc)])
    return np.concatenate(two_parts(lr), axis=1), small.astype(np.float32)


def windows(arrived, rows, small, frames, core):
    half_h, half_w = rows.shape[0], small.shape[1]
    return pl.pallas_call(
        functools.partial(window_kernel, frames=frames, core=core),
        out_shape=jax.ShapeDtypeStruct((frames * half_h + 16, half_w), BF16),
        in_specs=vmem_spec(3),
        out_specs=pl.BlockSpec(memory_space=VMEM),
        compiler_params=pltpu.CompilerParams(vmem_limit_bytes=LIMIT),
        name="windows",
    )(arrived, rows, small)


def add_frame(weight, patterns, frame, value):
    for lit in range(patterns.shape[0]):
        weight[patterns[lit, frame]] += value


def take_windows(weight, patterns, windows_here, slots, half_h):
    for window, slot in zip(windows_here, slots):
        frames_here = window.shape[0] // half_h
        owner = jnp.bitwise_xor(lax.axis_index("grp"), slot)
        means = rows_value(window[frames_here * half_h :])
        for place in range(frames_here):
            value = window[place * half_h : (place + 1) * half_h].astype(F32)
            value = -means[place : place + 1, 0:1] - value
            add_frame(weight, patterns, owner * frames_here + place, value)


def fetch_kernel(patterns, estimate_ref, window, field_hbm, field_ref, weight, sem):
    load = pltpu.make_async_copy(field_hbm, field_ref, sem)
    load.start()
    weight[...] = jnp.zeros_like(weight)
    frames, half_h, _ = estimate_ref.shape

    def one_frame(frame, carry):
        add_frame(weight, patterns, frame, estimate_ref[frame])
        return carry

    lax.fori_loop(0, frames, one_frame, 0)
    take_windows(weight, patterns, (window,), (0,), half_h)
    load.wait()


def fetch(field, estimate, window, patterns):
    leds = field.shape[0]
    return pl.pallas_call(
        fetch_kernel,
        out_shape=(
            jax.ShapeDtypeStruct(field.shape, F32),
            jax.ShapeDtypeStruct((leds, *estimate.shape[1:]), F32),
        ),
        in_specs=[pl.BlockSpec(memory_space=SMEM)]
        + vmem_spec(2)
        + [pl.BlockSpec(memory_space=pltpu.HBM)],
        out_specs=tuple(vmem_spec(2)),
        scratch_shapes=[pltpu.SemaphoreType.DMA],
        compiler_params=pltpu.CompilerParams(vmem_limit_bytes=LIMIT),
        cost_estimate=pl.CostEstimate(flops=0, bytes_accessed=16_000_000, transcendentals=0),
        name="fetch",
    )(patterns, estimate, window, pltpu.with_memory_space_constraint(field, pltpu.HBM))


def collect_kernel(patterns, w1, w2, weight_in, weight):
    take_windows(weight, patterns, (w1, w2), (1, 2), weight.shape[1])


def collect(weight, w1, w2, patterns):
    return pl.pallas_call(
        collect_kernel,
        out_shape=jax.ShapeDtypeStruct(weight.shape, F32),
        in_specs=[pl.BlockSpec(memory_space=SMEM)] + vmem_spec(3),
        out_specs=pl.BlockSpec(memory_space=VMEM),
        input_output_aliases={3: 0},
        compiler_params=pltpu.CompilerParams(vmem_limit_bytes=LIMIT),
        name="collect",
    )(patterns, w1, w2, weight)


def across(left, right):
    dims = (((1,), (1,)), ((), ()))
    return lax.dot_general(left, right, dims, preferred_element_type=F32)


def update_kernel(
    led_row, led_col, patterns, field_ref, weight_in, w3,
    spec_ref, pupil_ref, back_ref, big_hbm,
    fresh_hbm, high_ref, low_ref, first_ref, second_ref, weight,
    grads, fresh_ref, big, sides_ref, big_sem, fresh_sems, *, group,
):
    leds, half_h, half_w = weight.shape
    band_rows, band_cols = pupil_ref.shape[1:]
    height, width = spec_ref.shape[1:]
    is_odd = lax.rem(lax.axis_index("tile"), 2) == 1
    big_load = pltpu.make_async_copy(big_hbm, big, big_sem)
    big_load.start()
    grads[...] = jnp.zeros_like(grads)
    take_windows(weight, patterns, (w3,), (3,), half_h)

    left_rows = 2 * band_rows
    pair_rows, pair_cols = half_h // 2, half_w // 2

    def some(step, carry):
        backs = []
        for place in range(group):
            q = weight[step * group + place]
            field = field_ref[step * group + place]
            g_re, g_im = field[:half_h] * q, field[half_h:] * q
            re_a, re_b = g_re[:pair_rows], g_re[pair_rows:]
            im_a, im_b = g_im[:pair_rows], g_im[pair_rows:]
            to_re = jnp.concatenate([re_a + re_b, im_a - im_b], axis=0)
            to_im = jnp.concatenate([im_a + im_b, re_b - re_a], axis=0)
            high, low = split(jnp.concatenate([to_re, to_im], axis=1))
            both = mm(back_ref[:left_rows], jnp.concatenate([high, low], axis=0))
            back = both[:band_rows] + both[band_rows:]
            re_a, re_b = back[:, :pair_cols], back[:, pair_cols : 2 * pair_cols]
            im_a, im_b = back[:, 2 * pair_cols : 3 * pair_cols], back[:, 3 * pair_cols :]
            backs.append(jnp.concatenate([re_a + re_b, im_a - im_b], axis=1))
            backs.append(jnp.concatenate([im_a + im_b, re_b - re_a], axis=1))
        high, low = split(jnp.concatenate(backs, axis=0))
        cols = back_ref[left_rows:]
        both = mm(jnp.concatenate([high, low], axis=1), jnp.concatenate([cols, cols], axis=0))
        boxes = both[:, :band_cols] + both[:, band_cols:]
        for place in range(group):
            led = step * group + place
            begin = 2 * place * band_rows
            back_re = boxes[begin : begin + band_rows]
            back_im = boxes[begin + band_rows : begin + 2 * band_rows]
            parts = (
                pupil_ref[0] * back_re + pupil_ref[1] * back_im,
                pupil_ref[0] * back_im - pupil_ref[1] * back_re,
            )
            area, down, right = box_area(led_row[led], led_col[led], band_rows, band_cols)
            for part in range(2):
                filled = jnp.concatenate([parts[part], jnp.zeros((8, band_cols), F32)], axis=0)
                filled = pltpu.roll(filled, down, 0)
                filled = jnp.concatenate([filled, jnp.zeros((band_rows + 8, 128), F32)], axis=1)
                grads[(part, *area)] += pltpu.roll(filled, right, 1)
        return carry

    lax.fori_loop(0, leds // group, some, 0)
    fresh_re = spec_ref[0] - (4.0 * STEP) * grads[0, :height, :width]
    fresh_im = spec_ref[1] - (4.0 * STEP) * grads[1, :height, :width]
    for part, fresh in enumerate((fresh_re, fresh_im)):
        for number, block in enumerate(lane_blocks(fresh)):
            fresh_ref[part, number, :height] = block
    stores = []
    for number in range(width // 128):
        store = pltpu.make_async_copy(
            fresh_ref.at[:, number, pl.ds(0, height)], fresh_hbm.at[:, :, pl.ds(number * 128, 128)],
            fresh_sems.at[number],
        )
        store.start()
        stores.append(store)
    big_load.wait()

    def spread(parity, table):
        rows = pl.ds(parity, height // 2, stride=2)
        parts = [
            jnp.concatenate([fresh_ref[part, n, rows] for n in range(width // 128)], axis=1)
            for part in range(2)
        ]
        high, low = split(jnp.concatenate(parts, axis=0))
        table_hi, table_lo = big[table : table + height], big[table + height : table + 2 * height]
        left = jnp.concatenate([table_hi, table_lo, table_hi], axis=1)
        return mm(left, jnp.concatenate([high, high, low], axis=0))

    even, odd = spread(0, 0), spread(1, 2 * height)
    upper, lower = even + odd, even - odd
    half = height // 2
    z_re = jnp.concatenate([upper[:half], lower[:half]], axis=0)
    z_im = jnp.concatenate([upper[half:], lower[half:]], axis=0)

    near = [z[:, : width // 2] for z in (z_re, z_im)]
    far = [z[:, width // 2 :] for z in (z_re, z_im)]
    mixed = [a + b for a, b in zip(near, far)] + [a - b for a, b in zip(near, far)]
    high, low = split(jnp.concatenate(mixed, axis=1))
    high_ref[...] = high
    low_ref[...] = low
    count = first_ref.shape[0]
    for parity in range(2):
        table = 4 * height + 4 * count * parity
        cut = slice(parity * width, (parity + 1) * width)
        side_hi = jnp.concatenate([big[table : table + count], big[table + count : table + 2 * count]], axis=1)
        side_lo = jnp.concatenate(
            [big[table + 2 * count : table + 3 * count], big[table + 3 * count : table + 4 * count]], axis=1
        )
        one = across(side_hi, high[:, cut]) + across(side_lo, high[:, cut])
        one = one + across(side_hi, low[:, cut])
        for number, block in enumerate(lane_blocks(one)):
            sides_ref[number, pl.ds(parity, count, stride=2)] = block
    sides = jnp.concatenate([sides_ref[n] for n in range(height // 128)], axis=1)
    to_left, to_right = sides[:count], sides[count : 2 * count]
    first_ref[...] = jnp.where(is_odd, to_left, to_right)
    second_ref[...] = jnp.where(is_odd, to_right, to_left)
    for store in stores:
        store.wait()


def update(
    field, weight, window, spectrum, pupil, patterns, led_row, led_col, tables,
    margin, group=8,
):
    _, _, back_rows, back_cols = tables
    leds = led_row.shape[0]
    _, height, width = spectrum.shape
    half_h, half_w = height // 2, width // 2
    big = []
    for parity in range(2):
        freqs = np.arange(parity, height, 2) - height // 2
        re, im = wave(np.arange(height // 2), freqs, height, height)
        big += two_parts(np.block([[re, -im], [im, re]]))
    for parity in range(2):
        left = np.arange(parity, margin, 2)
        freqs = np.arange(width // 2) - width // 2
        l_re, l_im = wave(left, freqs, width, width)
        r_re, r_im = wave(left + width - margin, freqs, width, width)
        from_re = two_parts(np.concatenate([l_re, l_im, r_re, r_im]))
        from_im = two_parts(np.concatenate([-l_im, l_re, -r_im, r_re]))
        big += [from_re[0], from_im[0], from_re[1], from_im[1]]
    big = np.concatenate(big)
    back = np.concatenate([back_rows, back_cols])
    out_shape = (
        jax.ShapeDtypeStruct(spectrum.shape, F32),
        jax.ShapeDtypeStruct((height, 2 * width), BF16),
        jax.ShapeDtypeStruct((height, 2 * width), BF16),
        jax.ShapeDtypeStruct((2 * margin, height), F32),
        jax.ShapeDtypeStruct((2 * margin, height), F32),
        jax.ShapeDtypeStruct(weight.shape, F32),
    )
    return pl.pallas_call(
        functools.partial(update_kernel, group=group),
        out_shape=out_shape,
        in_specs=[pl.BlockSpec(memory_space=SMEM)] * 3
        + vmem_spec(6)
        + [pl.BlockSpec(memory_space=pltpu.HBM)],
        out_specs=(pl.BlockSpec(memory_space=pltpu.HBM), *vmem_spec(5)),
        input_output_aliases={4: 5},
        scratch_shapes=[
            pltpu.VMEM((2, height + 8, width + 128), F32),
            pltpu.VMEM((2, width // 128, height + 8, 128), F32),
            pltpu.VMEM(big.shape, BF16),
            pltpu.VMEM((height // 128, 4 * margin + 8, 128), F32),
            pltpu.SemaphoreType.DMA,
            pltpu.SemaphoreType.DMA((width // 128,)),
        ],
        compiler_params=pltpu.CompilerParams(vmem_limit_bytes=LIMIT),
        name="update",
    )(
        led_row, led_col, patterns, field, weight, window, spectrum, pupil, back,
        pltpu.with_memory_space_constraint(jnp.asarray(big), pltpu.HBM),
    )[:5]


def object_kernel(high_ref, low_ref, table_ref, out_hbm, edges_ref, out, sems):
    core = out_hbm.shape[1]
    margin = edges_ref.shape[2]
    half = core // 2
    depth = high_ref.shape[1] // 4
    cuts = (slice(0, half // 2 // 16 * 16 + 16), slice(half // 2 // 16 * 16 + 16, half))
    stores = []
    for number, cut in enumerate(cuts):
        for parity in range(2):
            lefts = []
            for begin in (4 * parity * half, (4 * parity + 1) * half):
                rows = slice(begin + cut.start, begin + cut.stop)
                more = slice(rows.start + 2 * half, rows.stop + 2 * half)
                lefts.append(jnp.concatenate([table_ref[rows], table_ref[more], table_ref[rows]], axis=1))
            left = jnp.concatenate(lefts, axis=0)
            products = []
            for part in range(2):
                lanes = slice((2 * parity + part) * depth, (2 * parity + part + 1) * depth)
                z_hi, z_lo = high_ref[:, lanes], low_ref[:, lanes]
                products.append(across(left, jnp.concatenate([z_hi, z_hi, z_lo], axis=1)))
            count = cut.stop - cut.start
            rows = pl.ds(2 * cut.start + parity, count, stride=2)
            real = products[0][:count] - products[1][count:]
            imaginary = products[0][count:] + products[1][:count]
            for part, values in enumerate((real, imaginary)):
                for lanes, block in enumerate(lane_blocks(values)):
                    out[part, lanes, rows] = block
        span = pl.ds(2 * cut.start, 2 * (cut.stop - cut.start))
        for lanes in range(out.shape[1]):
            store = pltpu.make_async_copy(
                out.at[:, lanes, span], out_hbm.at[:, span, pl.ds(lanes * 128, 128)],
                sems.at[number, lanes],
            )
            store.start()
            stores.append(store)
    for part in range(2):
        for side, begin in enumerate((0, core - margin)):
            edge = [out[part, n, begin : begin + margin] for n in range(out.shape[1])]
            edges_ref[part, side] = jnp.concatenate(edge, axis=1)
    for store in stores:
        store.wait()


def object_core(high, low, margin, core):
    height, width = high.shape[0], high.shape[1] // 2
    table = []
    for parity in range(2):
        places = margin + np.arange(parity, core, 2)
        table += two_parts(
            np.concatenate(wave(places, np.arange(width // 2) - width // 2, width, width))
        )
    table = np.concatenate(table)
    return pl.pallas_call(
        object_kernel,
        out_shape=(
            jax.ShapeDtypeStruct((2, core, height), F32),
            jax.ShapeDtypeStruct((2, 2, margin, height), F32),
        ),
        in_specs=vmem_spec(3),
        out_specs=(pl.BlockSpec(memory_space=pltpu.HBM), pl.BlockSpec(memory_space=VMEM)),
        scratch_shapes=[
            pltpu.VMEM((2, height // 128, core + 8, 128), F32),
            pltpu.SemaphoreType.DMA((2, height // 128)),
        ],
        compiler_params=pltpu.CompilerParams(vmem_limit_bytes=LIMIT),
        cost_estimate=pl.CostEstimate(
            flops=3_000_000_000, bytes_accessed=5_000_000, transcendentals=0
        ),
        name="object",
    )(high, low, table)


def blend_kernel(first_ref, second_ref, edges_ref, core_hbm, out_hbm, mixed, sems):
    tile = lax.axis_index("tile")
    is_odd = lax.rem(tile, 2) == 1
    margin, core = edges_ref.shape[2], out_hbm.shape[1]
    k = lax.broadcasted_iota(jnp.int32, (margin, 1), 0).astype(F32)
    span = 2.0 * margin
    from_left = jnp.where(is_odd, first_ref[...], second_ref[...])
    from_right = jnp.where(is_odd, second_ref[...], first_ref[...])
    sides = (
        ((k + margin + 0.5) / span, (margin - k - 0.5) / span, tile > 0, from_left, 0),
        (
            (span - k - 0.5) / span, (k + 0.5) / span, tile < lax.axis_size("tile") - 1, from_right,
            core - margin,
        ),
    )
    stores = []
    for side, (own_w, other_w, has_other, other, begin) in enumerate(sides):
        own_w = jnp.where(has_other, own_w, 1.0)
        other_w = jnp.where(has_other, other_w, 0.0)
        for part in range(2):
            cut = slice(part * margin, (part + 1) * margin)
            mixed[side, part] = edges_ref[part, side] * own_w + other[cut] * other_w
        store = pltpu.make_async_copy(
            mixed.at[side], out_hbm.at[:, pl.ds(begin, margin)], sems.at[side]
        )
        store.start()
        stores.append(store)
    for store in stores:
        store.wait()


def blend(core_part, edges, first, second):
    return pl.pallas_call(
        blend_kernel,
        out_shape=jax.ShapeDtypeStruct(core_part.shape, F32),
        in_specs=vmem_spec(3) + [pl.BlockSpec(memory_space=pltpu.HBM)],
        out_specs=pl.BlockSpec(memory_space=pltpu.HBM),
        input_output_aliases={3: 0},
        scratch_shapes=[pltpu.VMEM(edges.shape, F32), pltpu.SemaphoreType.DMA((2,))],
        compiler_params=pltpu.CompilerParams(vmem_limit_bytes=LIMIT),
        name="blend",
    )(first, second, edges, core_part)


def body(raw, scales, flat, spectrum, pupil, patterns, led_row, led_col):
    height, core = flat.shape
    margin = OV // 2
    width = core + OV
    tiles = lax.axis_size("tile")
    frames_here = raw.shape[0]
    band_rows, band_cols = pupil.shape[1:]
    spectrum_tile = spectrum[0]
    patterns = patterns.T

    swap_a = [(i, i ^ 1) for i in range(tiles)]
    swap_b = [(i, ((i + 1) ^ 1) - 1) for i in range(1, tiles - 1)]

    def neighbours(for_a, for_b):
        return lax.ppermute(for_a, "tile", swap_a), lax.ppermute(for_b, "tile", swap_b)

    tables = stacked_tables(height, width, band_rows, band_cols)
    passes = (low_pass(height, band_rows), low_pass(width, band_cols).T)

    by_rows = gains_by_rows(flat.T, tiles, width)
    dequantized = dequantize(raw, scales, by_rows, tiles, core, margin)
    gains = lax.all_to_all(by_rows, "tile", split_axis=0, concat_axis=0, tiled=True)
    narrow = strips(dequantized, gains, passes[1], frames_here, core, margin)
    arrived = lax.all_to_all(narrow, "tile", split_axis=0, concat_axis=0, tiled=True)
    handed = window_tables(tiles, passes, margin, core)
    field, estimate, rows, small = all_fields(
        spectrum_tile, pupil, patterns, led_row, led_col, tables, handed
    )
    window = windows(arrived, rows, small, frames_here, core)
    field, weight = fetch(field, estimate, window, patterns)

    swap_core = [(i, i ^ 1) for i in range(4)]
    swap_chip = [(i, i ^ 2) for i in range(4)]
    other = functools.partial(lax.ppermute, axis_name="grp")
    window_2 = other(window, perm=swap_chip)
    window_1 = other(window, perm=swap_core)
    window_2, field, weight = lax.optimization_barrier((window_2, field, weight))
    window_3 = other(window_2, perm=swap_core)
    weight = collect(weight, window_1, window_2, patterns)

    fresh, high, low, for_a, for_b = update(
        field, weight, window_3, spectrum_tile, pupil, patterns,
        led_row, led_col, tables, margin,
    )
    side_a, side_b = neighbours(for_a, for_b)
    core_part, edges = object_core(high, low, margin, core)
    stitched = blend(core_part, edges, side_a, side_b)
    return fresh[None], jnp.transpose(stitched, (0, 2, 1))


def solution(mesh):
    return jax.shard_map(
        body,
        mesh=mesh,
        in_specs=(
            P("grp", "tile", None),
            P("grp", "tile", None),
            P(None, "tile"),
            P("tile", None, None, None),
            P(),
            P(),
            P(),
            P(),
        ),
        out_specs=(P("tile", None, None, None), P(None, None, "tile")),
        check_vma=False,
    )
```

```python
import functools
import math

import jax
import jax.numpy as jnp
import ml_dtypes
import numpy as np
from jax import lax
from jax.experimental import pallas as pl
from jax.experimental.pallas import tpu as pltpu
from jax.sharding import PartitionSpec as P

OV = 32
BC = 32
STEP = 0.02
F32 = jnp.float32
BF16 = jnp.bfloat16
VMEM = pltpu.VMEM
SMEM = pltpu.SMEM
LIMIT = 30 << 20


def two_parts(table):
    table = np.asarray(table, np.float64)
    high = table.astype(ml_dtypes.bfloat16)
    low = (table - high.astype(np.float64)).astype(ml_dtypes.bfloat16)
    return high, low


def wave(places, freqs, length, norm):
    turns = np.outer(places, freqs) % length
    angle = turns * (2.0 * math.pi / length)
    return np.cos(angle) / math.sqrt(norm), np.sin(angle) / math.sqrt(norm)


def pairs(length):
    first = np.arange(1, length // 2, 2)
    return np.concatenate([first, length - first])


def low_pass(length, band):
    places = pairs(length)[:, None] - np.arange(length)[None, :]
    total = np.ones(places.shape)
    for freq in range(1, band):
        total += 2.0 * np.cos(2.0 * math.pi * ((freq * places) % length) / length)
    return total / length


def stacked_tables(height, width, band_rows, band_cols):
    row_re, row_im = wave(
        pairs(height), np.arange(band_rows) - band_rows // 2, height, band_rows
    )
    rows = np.block([[row_re, -row_im], [row_im, row_re]])
    col_re, col_im = wave(
        np.arange(band_cols) - band_cols // 2, pairs(width), width, band_cols
    )
    cols = np.block([[col_re, col_im], [-col_im, col_re]])
    half_rows, half_cols = height // 4, width // 4
    high, low = two_parts(np.concatenate([row_re[:half_rows], row_im[:half_rows]]).T)
    back_rows = np.block([[high, high], [low, np.zeros_like(low)]])
    back_cols = np.concatenate(
        two_parts(np.concatenate([col_re[:, :half_cols], col_im[:, :half_cols]], axis=1).T), axis=1
    )
    return rows, cols, back_rows, back_cols


def split(values):
    high = values.astype(BF16)
    return high, (values - high.astype(F32)).astype(BF16)


def mm(left, right):
    return jnp.dot(left, right, preferred_element_type=F32)


def vmem_spec(count):
    return [pl.BlockSpec(memory_space=VMEM)] * count


def lane_blocks(values):
    return [values[:, begin : begin + 128] for begin in range(0, values.shape[1], 128)]


def parts_rows(values):
    high = values.astype(BF16).astype(F32)
    return jnp.concatenate([high, values - high], axis=0).astype(BF16)


def rows_value(rows):
    rows = rows.astype(F32)
    return rows[:8, :128] + rows[8:, :128]


def gains_kernel(flat_ref, out_hbm, out, sems):
    core, height = flat_ref.shape
    tiles, rows_here, width = out_hbm.shape
    stores = []
    for number, begin in enumerate(range(0, width, 128)):
        length = min(128, core - begin)
        gains = flat_ref[begin : begin + length] - 1.0
        if length < 128:
            gains = jnp.concatenate([gains, jnp.zeros((128 - length, height), F32)], axis=0)
        by_rows = jnp.transpose(gains, (1, 0)).reshape(tiles, rows_here, 128)
        out[:, :, begin : begin + 128] = by_rows.astype(BF16)
        part = (slice(None), slice(None), pl.ds(begin, 128))
        store = pltpu.make_async_copy(out.at[part], out_hbm.at[part], sems.at[number])
        store.start()
        stores.append(store)
    for store in stores:
        store.wait()


def gains_by_rows(flat, tiles, width):
    core, height = flat.shape
    shape = (tiles, height // tiles, width)
    return pl.pallas_call(
        gains_kernel,
        out_shape=jax.ShapeDtypeStruct(shape, BF16),
        in_specs=vmem_spec(1),
        out_specs=pl.BlockSpec(memory_space=pltpu.HBM),
        scratch_shapes=[pltpu.VMEM(shape, BF16), pltpu.SemaphoreType.DMA((width // 128,))],
        compiler_params=pltpu.CompilerParams(vmem_limit_bytes=LIMIT),
        name="gains",
    )(flat)


def dequantize_kernel(raw_ref, scales_ref, after, out_ref, *, core, margin):
    lines, strip = raw_ref.shape
    coarse_rows, coarse_cols = scales_ref.shape
    tiles, _, width = out_ref.shape
    ratio = lines // coarse_rows
    row = lax.broadcasted_iota(jnp.int32, (lines, coarse_rows), 0)
    pick = lax.broadcasted_iota(jnp.int32, (lines, coarse_rows), 1)
    spread_rows = (row // ratio == pick).astype(F32).astype(BF16)
    factors = mm(spread_rows, scales_ref[...])
    wide = (coarse_cols // 128 + 1) * 128
    factors = jnp.concatenate([factors, jnp.zeros((lines, wide - coarse_cols), F32)], axis=1)

    blocks = []
    for tile in range(tiles):
        begin = (tile * core - margin) // BC
        blocks.append(pltpu.roll(factors, -begin % wide, 1)[:, :128].astype(BF16))
    block = lax.broadcasted_iota(jnp.int32, (128, width), 0)
    place = lax.broadcasted_iota(jnp.int32, (128, width), 1) + (-margin) % BC
    inside = (place >= block * BC) & (place < (block + 1) * BC)
    scales = mm(jnp.concatenate(blocks, axis=0), inside.astype(F32).astype(BF16))
    for tile in range(tiles):
        start = tile * core - margin
        base = max(start, 0) // 128 * 128
        span = min(width + 128, strip - base)
        codes = raw_ref[:, base : base + span].astype(F32)
        turn = (base - start) % span
        if turn:
            codes = pltpu.roll(codes, turn, 1)
        out_ref[tile] = codes[:, :width] * scales[tile * lines : (tile + 1) * lines]


def dequantize(raw, scales, after, tiles, core, margin):
    frames, rows_here, strip = raw.shape
    return pl.pallas_call(
        functools.partial(dequantize_kernel, core=core, margin=margin),
        out_shape=jax.ShapeDtypeStruct((tiles, frames * rows_here, core + 2 * margin), F32),
        in_specs=vmem_spec(2) + [pl.BlockSpec(memory_space=pl.ANY)],
        out_specs=pl.BlockSpec(memory_space=VMEM),
        compiler_params=pltpu.CompilerParams(vmem_limit_bytes=LIMIT),
        cost_estimate=pl.CostEstimate(
            flops=2_000_000_000, bytes_accessed=4_000_000, transcendentals=0
        ),
        name="dequantize",
    )(raw.reshape(frames * rows_here, strip), scales.reshape(-1, scales.shape[-1]), after)


def strips_kernel(dq_ref, gains_ref, lc_ref, out_hbm, out_ref, sems, *, frames, core, margin):
    tiles, lines, width = dq_ref.shape
    half_w = lc_ref.shape[1]
    rows_here = lines // frames
    line = lax.broadcasted_iota(jnp.int32, (1, width), 1)
    in_core = ((line >= margin) & (line < margin + core)).astype(F32)
    xc = (line.astype(F32) - margin - (core - 1) / 2.0) * in_core
    first_row = (lax.axis_index("tile") * rows_here).astype(F32)
    height = rows_here * tiles
    yc = lax.broadcasted_iota(jnp.int32, (rows_here, 1), 0).astype(F32)
    yc = yc + (first_row - (height - 1) / 2.0)
    lane = lax.broadcasted_iota(jnp.int32, (8, 128), 1)
    narrow_lane = lax.broadcasted_iota(jnp.int32, (1, 128), 1)

    lc_hi, lc_lo = lc_ref[:width], lc_ref[width:]
    own, stores = [], []

    all_yc = jnp.concatenate([yc] * frames, axis=0)

    def by_frame(values, weights):
        sums = []
        for frame in range(frames):
            one = values[frame * rows_here : (frame + 1) * rows_here]
            one = functools.reduce(
                jnp.add, [one[row : row + 8] for row in range(0, rows_here, 8)]
            )
            if weights is not None:
                one = one * weights
            one = functools.reduce(jnp.add, lane_blocks(one))
            one = jnp.sum(one, axis=1, keepdims=True)
            sums.append(jnp.sum(one, axis=0, keepdims=True))
        return jnp.concatenate(sums + [jnp.zeros((8 - frames, 1), F32)], axis=0)

    def windowed(tile):
        gains = pltpu.roll(gains_ref[tile].astype(F32), margin, 1)
        if tile > 0:
            end = gains_ref[tile - 1][:, width - 128 :].astype(F32)
            end = pltpu.roll(end, (2 * margin) + margin, 1)
            end = jnp.where(narrow_lane < margin, end, 0.0)
            gains = jnp.concatenate([gains[:, :128] + end, gains[:, 128:]], axis=1)
        if tile < tiles - 1:
            end = gains_ref[tile + 1][:, :128].astype(F32)
            end = pltpu.roll(end, 128 - margin, 1)
            end = jnp.where(narrow_lane >= 128 - margin, end, 0.0)
            gains = jnp.concatenate(
                [gains[:, : width - 128], gains[:, width - 128 :] + end], axis=1
            )
        gains = jnp.concatenate([gains + 1.0] * frames, axis=0)
        flattened = dq_ref[tile] * gains
        slope_y = by_frame(flattened * all_yc, in_core)
        slope_x = by_frame(flattened, xc)
        own.append(jnp.where(lane == 0, slope_y, jnp.where(lane == 1, slope_x, 0.0)))
        return flattened.astype(BF16)

    def finish(tile, one):
        mean = by_frame(one, None) * (1.0 / (rows_here * half_w))
        centred = []
        for frame in range(frames):
            cut = slice(frame * rows_here, (frame + 1) * rows_here)
            centred.append(one[cut] - mean[frame : frame + 1])
        centred = jnp.concatenate(centred, axis=0)
        for part in range(half_w // 128):
            columns = centred[:, part * 128 : (part + 1) * 128]
            out_ref[tile, part * lines : (part + 1) * lines] = columns.astype(BF16)
        packed = own[tile] + jnp.where(lane == 6, mean, 0.0)
        if tile > 0:
            packed += pltpu.roll(own[tile - 1], 2, 1)
        if tile < tiles - 1:
            packed += pltpu.roll(own[tile + 1], 4, 1)
        out_ref[tile, half_w // 128 * lines :] = parts_rows(packed)

    part_tiles = max(tiles // 2, 1)
    waiting = None
    for begin in range(0, tiles, part_tiles):
        pixels = jnp.concatenate([windowed(t) for t in range(begin, begin + part_tiles)], axis=0)
        if waiting is not None:
            finish(*waiting)
        narrow = mm(pixels, lc_hi) + mm(pixels, lc_lo)
        for number in range(part_tiles):
            one = (begin + number, narrow[number * lines : (number + 1) * lines])
            if number == part_tiles - 1 and begin + part_tiles < tiles:
                waiting = one
            else:
                finish(*one)
        done = begin + part_tiles - (1 if begin + part_tiles < tiles else 0)
        first = max(begin - 1, 0)
        span = pl.ds(first, done - first)
        store = pltpu.make_async_copy(out_ref.at[span], out_hbm.at[span], sems.at[begin // part_tiles])
        store.start()
        stores.append(store)
    for store in stores:
        store.wait()


def strips(dequantized, gains, lc, frames, core, margin):
    tiles, lines, _ = dequantized.shape
    shape = (tiles, lines * (lc.shape[1] // 128) + 16, 128)
    return pl.pallas_call(
        functools.partial(strips_kernel, frames=frames, core=core, margin=margin),
        out_shape=jax.ShapeDtypeStruct(shape, BF16),
        in_specs=vmem_spec(3),
        out_specs=pl.BlockSpec(memory_space=pltpu.HBM),
        scratch_shapes=[pltpu.VMEM(shape, BF16), pltpu.SemaphoreType.DMA((2,))],
        compiler_params=pltpu.CompilerParams(vmem_limit_bytes=LIMIT),
        name="strips",
    )(dequantized, gains, np.concatenate(two_parts(lc)))


def box_area(top, left, band_rows, band_cols):
    row = top // 8 * 8
    col = left // 128 * 128
    area = (
        pl.ds(pl.multiple_of(row, 8), band_rows + 8),
        pl.ds(pl.multiple_of(col, 128), band_cols + 128),
    )
    return area, top - row, left - col


def field_kernel(
    led_row, led_col, patterns, spec_ref, pupil_ref, cols_ref, rows_ref,
    rows_hbm, small_hbm, field_ref, estimate_ref, rows_out, small_out, wide, bright, sems, *, group,
):
    leds, half_h, half_w = bright.shape
    loads = [
        pltpu.make_async_copy(rows_hbm, rows_out, sems.at[0]),
        pltpu.make_async_copy(small_hbm, small_out, sems.at[1]),
    ]
    for load in loads:
        load.start()
    band_rows, band_cols = pupil_ref.shape[1:]
    width = spec_ref.shape[2]
    depth = 2 * band_cols
    wide[...] = jnp.zeros_like(wide)
    wide[:, : spec_ref.shape[1], :width] = spec_ref[...]

    def some(step, carry):
        boxes = []
        for place in range(group):
            led = step * group + place
            area, down, right = box_area(led_row[led], led_col[led], band_rows, band_cols)
            back = lax.rem(2 * band_cols - right, 2 * band_cols)
            up = lax.rem(band_rows + 8 - down, band_rows + 8)
            parts = []
            for part in range(2):
                strip = pltpu.roll(wide[(part, *area)], back, 1)
                parts.append(pltpu.roll(strip[:, :band_cols], up, 0)[:band_rows])
            lit_re = pupil_ref[0] * parts[0] - pupil_ref[1] * parts[1]
            lit_im = pupil_ref[0] * parts[1] + pupil_ref[1] * parts[0]
            boxes.append(jnp.concatenate([lit_re, lit_im], axis=1))
        high, low = split(jnp.concatenate(boxes, axis=0))
        cols_hi, cols_lo = cols_ref[:depth], cols_ref[depth:]
        spread = mm(high, cols_hi) + mm(high, cols_lo) + mm(low, cols_hi)
        for place in range(group):
            one = spread[place * band_rows : (place + 1) * band_rows]
            high, low = split(jnp.concatenate([one[:, :half_w], one[:, half_w:]], axis=0))
            field = mm(rows_ref[...], jnp.concatenate([high, low, high], axis=0))
            field_ref[step * group + place] = field
            bright[step * group + place] = field[:half_h] ** 2 + field[half_h:] ** 2
        return carry

    lax.fori_loop(0, leds // group, some, 0)

    def one_frame(frame, carry):
        total = bright[patterns[0, frame]]
        for lit in range(1, patterns.shape[0]):
            total += bright[patterns[lit, frame]]
        estimate_ref[frame] = total
        return carry

    lax.fori_loop(0, patterns.shape[1], one_frame, 0)
    for load in loads:
        load.wait()


def all_fields(spectrum, pupil, patterns, led_row, led_col, tables, handed, group=8):
    rows, cols, _, _ = tables
    leds = led_row.shape[0]
    _, height, width = spectrum.shape
    half_h, half_w = height // 2, width // 2
    high, low = two_parts(rows)
    return pl.pallas_call(
        functools.partial(field_kernel, group=group),
        out_shape=(
            jax.ShapeDtypeStruct((leds, 2 * half_h, half_w), F32),
            jax.ShapeDtypeStruct((patterns.shape[1], half_h, half_w), F32),
            *(jax.ShapeDtypeStruct(table.shape, table.dtype) for table in handed),
        ),
        in_specs=[pl.BlockSpec(memory_space=SMEM)] * 3
        + vmem_spec(4)
        + [pl.BlockSpec(memory_space=pltpu.HBM)] * 2,
        out_specs=tuple(vmem_spec(4)),
        scratch_shapes=[
            pltpu.VMEM((2, height + 8, width + 128), F32),
            pltpu.VMEM((leds, half_h, half_w), F32),
            pltpu.SemaphoreType.DMA((2,)),
        ],
        compiler_params=pltpu.CompilerParams(vmem_limit_bytes=LIMIT),
        cost_estimate=pl.CostEstimate(
            flops=8_000_000_000, bytes_accessed=16_000_000, transcendentals=0
        ),
        name="fields",
    )(
        led_row, led_col, patterns, spectrum, pupil, np.concatenate(two_parts(cols)),
        np.concatenate([high, high, low], axis=1),
        *(pltpu.with_memory_space_constraint(jnp.asarray(t), pltpu.HBM) for t in handed),
    )


def window_kernel(dq_ref, rows_ref, small_ref, window_ref, *, frames, core):
    slabs, lines, _ = dq_ref.shape
    half_h, half_w = rows_ref.shape[0], window_ref.shape[1]
    halves = half_w // 128
    lines = (lines - 16) // halves
    lr_sum, line = small_ref[:half_h, :128], small_ref[half_h:]
    rows_here = lines // frames
    height = slabs * rows_here
    over_y = 1.0 / (core * (height * (height * height - 1) / 12.0))
    over_x = 1.0 / (height * (core * (core * core - 1) / 12.0))
    lane = lax.broadcasted_iota(jnp.int32, (8, 128), 1)
    notes = [rows_value(dq_ref[slab, halves * lines :]) for slab in range(slabs)]
    slopes = functools.reduce(jnp.add, notes)
    slopes = slopes * jnp.where(lane % 2 == 0, over_y, over_x)
    slab_means = jnp.zeros((8, 128), F32)
    for slab in range(slabs):
        slab_means = jnp.where(lane == slab, notes[slab][:, 6:7], slab_means)
    values = []
    for slab in range(slabs):
        parts = [dq_ref[slab, part * lines : (part + 1) * lines] for part in range(halves)]
        values.append(jnp.concatenate(parts, axis=1))
    if rows_here % 16:
        values = [value.astype(F32) for value in values]
    means = []
    for frame in range(frames):
        cut = slice(frame * rows_here, (frame + 1) * rows_here)
        whole = jnp.concatenate([v[cut] for v in values], axis=0).astype(BF16)
        window = mm(rows_ref[...], jnp.concatenate([whole, whole], axis=0))
        level = jnp.sum(lr_sum * slab_means[frame : frame + 1], axis=1, keepdims=True)
        window = window + level
        tilt_y, tilt_x = 0.0, 0.0
        for side in range(3):
            tilt_y += line[2 * side : 2 * side + 1] * slopes[frame : frame + 1, 2 * side : 2 * side + 1]
            tilt_x += line[2 * side + 1 : 2 * side + 2] * slopes[frame : frame + 1, 2 * side + 1 : 2 * side + 2]
        window = window - lr_sum[:, 127:128] * tilt_y - tilt_x
        mean = jnp.sum(window, axis=0, keepdims=True)
        mean = jnp.sum(mean, axis=1, keepdims=True) * (1.0 / (half_h * half_w))
        means.append(jnp.broadcast_to(mean, (1, 128)))
        window_ref[frame * half_h : (frame + 1) * half_h] = (window - mean).astype(BF16)
    means = jnp.concatenate(means + [jnp.zeros((8 - frames, 128), F32)], axis=0)
    notes = parts_rows(means)
    window_ref[frames * half_h :] = jnp.concatenate([notes] * halves, axis=1)


def tilt_lines(width, margin, core, lc):
    local = np.arange(width) - margin
    lines = []
    for begin, end, shift in ((0, core, 0), (-margin, 0, core), (core, core + margin, -core)):
        on = (local >= begin) & (local < end)
        lines.append(on.astype(np.float64) @ lc)
        lines.append(((local + shift - (core - 1) / 2.0) * on) @ lc)
    return np.stack(lines + lines[:2])


def window_tables(tiles, passes, margin, core):
    lr, lc = passes
    half_h, height = lr.shape
    sums = np.zeros((half_h, lc.shape[1]))
    sums[:, :tiles] = lr.reshape(half_h, tiles, height // tiles).sum(axis=2)
    sums[:, 127] = lr @ (np.arange(height) - (height - 1) / 2.0)
    small = np.concatenate([sums, tilt_lines(lc.shape[0], margin, core, lc)])
    return np.concatenate(two_parts(lr), axis=1), small.astype(np.float32)


def windows(arrived, rows, small, frames, core):
    half_h, half_w = rows.shape[0], small.shape[1]
    return pl.pallas_call(
        functools.partial(window_kernel, frames=frames, core=core),
        out_shape=jax.ShapeDtypeStruct((frames * half_h + 16, half_w), BF16),
        in_specs=vmem_spec(3),
        out_specs=pl.BlockSpec(memory_space=VMEM),
        compiler_params=pltpu.CompilerParams(vmem_limit_bytes=LIMIT),
        name="windows",
    )(arrived, rows, small)


def add_frame(weight, patterns, frame, value):
    for lit in range(patterns.shape[0]):
        weight[patterns[lit, frame]] += value


def take_windows(weight, patterns, windows_here, slots, half_h):
    for window, slot in zip(windows_here, slots):
        frames_here = window.shape[0] // half_h
        owner = jnp.bitwise_xor(lax.axis_index("grp"), slot)
        means = rows_value(window[frames_here * half_h :])
        for place in range(frames_here):
            value = window[place * half_h : (place + 1) * half_h].astype(F32)
            value = -means[place : place + 1, 0:1] - value
            add_frame(weight, patterns, owner * frames_here + place, value)


def fetch_kernel(patterns, estimate_ref, window, field_hbm, field_ref, weight, sem):
    load = pltpu.make_async_copy(field_hbm, field_ref, sem)
    load.start()
    weight[...] = jnp.zeros_like(weight)
    frames, half_h, _ = estimate_ref.shape

    def one_frame(frame, carry):
        add_frame(weight, patterns, frame, estimate_ref[frame])
        return carry

    lax.fori_loop(0, frames, one_frame, 0)
    take_windows(weight, patterns, (window,), (0,), half_h)
    load.wait()


def fetch(field, estimate, window, patterns):
    leds = field.shape[0]
    return pl.pallas_call(
        fetch_kernel,
        out_shape=(
            jax.ShapeDtypeStruct(field.shape, F32),
            jax.ShapeDtypeStruct((leds, *estimate.shape[1:]), F32),
        ),
        in_specs=[pl.BlockSpec(memory_space=SMEM)]
        + vmem_spec(2)
        + [pl.BlockSpec(memory_space=pltpu.HBM)],
        out_specs=tuple(vmem_spec(2)),
        scratch_shapes=[pltpu.SemaphoreType.DMA],
        compiler_params=pltpu.CompilerParams(vmem_limit_bytes=LIMIT),
        cost_estimate=pl.CostEstimate(flops=0, bytes_accessed=16_000_000, transcendentals=0),
        name="fetch",
    )(patterns, estimate, window, pltpu.with_memory_space_constraint(field, pltpu.HBM))


def collect_kernel(patterns, w1, w2, weight_in, weight):
    weight[...] = weight_in[...]
    take_windows(weight, patterns, (w1, w2), (1, 2), weight.shape[1])


def collect(weight, w1, w2, patterns):
    return pl.pallas_call(
        collect_kernel,
        out_shape=jax.ShapeDtypeStruct(weight.shape, F32),
        in_specs=[pl.BlockSpec(memory_space=SMEM)] + vmem_spec(3),
        out_specs=pl.BlockSpec(memory_space=VMEM),
        compiler_params=pltpu.CompilerParams(vmem_limit_bytes=LIMIT),
        name="collect",
    )(patterns, w1, w2, weight)


def across(left, right):
    dims = (((1,), (1,)), ((), ()))
    return lax.dot_general(left, right, dims, preferred_element_type=F32)


def update_kernel(
    led_row, led_col, patterns, field_ref, weight_in, w3,
    spec_ref, pupil_ref, back_ref, big_hbm,
    fresh_hbm, high_ref, low_ref, first_ref, second_ref,
    weight, grads, fresh_ref, big, sides_ref, big_sem, fresh_sems, *, group,
):
    leds, half_h, half_w = weight.shape
    band_rows, band_cols = pupil_ref.shape[1:]
    height, width = spec_ref.shape[1:]
    is_odd = lax.rem(lax.axis_index("tile"), 2) == 1
    big_load = pltpu.make_async_copy(big_hbm, big, big_sem)
    big_load.start()
    grads[...] = jnp.zeros_like(grads)
    weight[...] = weight_in[...]
    take_windows(weight, patterns, (w3,), (3,), half_h)

    left_rows = 2 * band_rows
    pair_rows, pair_cols = half_h // 2, half_w // 2

    def some(step, carry):
        backs = []
        for place in range(group):
            q = weight[step * group + place]
            field = field_ref[step * group + place]
            g_re, g_im = field[:half_h] * q, field[half_h:] * q
            re_a, re_b = g_re[:pair_rows], g_re[pair_rows:]
            im_a, im_b = g_im[:pair_rows], g_im[pair_rows:]
            to_re = jnp.concatenate([re_a + re_b, im_a - im_b], axis=0)
            to_im = jnp.concatenate([im_a + im_b, re_b - re_a], axis=0)
            high, low = split(jnp.concatenate([to_re, to_im], axis=1))
            both = mm(back_ref[:left_rows], jnp.concatenate([high, low], axis=0))
            back = both[:band_rows] + both[band_rows:]
            re_a, re_b = back[:, :pair_cols], back[:, pair_cols : 2 * pair_cols]
            im_a, im_b = back[:, 2 * pair_cols : 3 * pair_cols], back[:, 3 * pair_cols :]
            backs.append(jnp.concatenate([re_a + re_b, im_a - im_b], axis=1))
            backs.append(jnp.concatenate([im_a + im_b, re_b - re_a], axis=1))
        high, low = split(jnp.concatenate(backs, axis=0))
        cols = back_ref[left_rows:]
        both = mm(jnp.concatenate([high, low], axis=1), jnp.concatenate([cols, cols], axis=0))
        boxes = both[:, :band_cols] + both[:, band_cols:]
        for place in range(group):
            led = step * group + place
            begin = 2 * place * band_rows
            back_re = boxes[begin : begin + band_rows]
            back_im = boxes[begin + band_rows : begin + 2 * band_rows]
            parts = (
                pupil_ref[0] * back_re + pupil_ref[1] * back_im,
                pupil_ref[0] * back_im - pupil_ref[1] * back_re,
            )
            area, down, right = box_area(led_row[led], led_col[led], band_rows, band_cols)
            for part in range(2):
                filled = jnp.concatenate([parts[part], jnp.zeros((8, band_cols), F32)], axis=0)
                filled = pltpu.roll(filled, down, 0)
                filled = jnp.concatenate([filled, jnp.zeros((band_rows + 8, 128), F32)], axis=1)
                grads[(part, *area)] += pltpu.roll(filled, right, 1)
        return carry

    lax.fori_loop(0, leds // group, some, 0)
    fresh_re = spec_ref[0] - (4.0 * STEP) * grads[0, :height, :width]
    fresh_im = spec_ref[1] - (4.0 * STEP) * grads[1, :height, :width]
    for part, fresh in enumerate((fresh_re, fresh_im)):
        for number, block in enumerate(lane_blocks(fresh)):
            fresh_ref[part, number, :height] = block
    stores = []
    for number in range(width // 128):
        store = pltpu.make_async_copy(
            fresh_ref.at[:, number, pl.ds(0, height)], fresh_hbm.at[:, :, pl.ds(number * 128, 128)],
            fresh_sems.at[number],
        )
        store.start()
        stores.append(store)
    big_load.wait()

    def spread(parity, table):
        rows = pl.ds(parity, height // 2, stride=2)
        parts = [
            jnp.concatenate([fresh_ref[part, n, rows] for n in range(width // 128)], axis=1)
            for part in range(2)
        ]
        high, low = split(jnp.concatenate(parts, axis=0))
        table_hi, table_lo = big[table : table + height], big[table + height : table + 2 * height]
        left = jnp.concatenate([table_hi, table_lo, table_hi], axis=1)
        return mm(left, jnp.concatenate([high, high, low], axis=0))

    even, odd = spread(0, 0), spread(1, 2 * height)
    upper, lower = even + odd, even - odd
    half = height // 2
    z_re = jnp.concatenate([upper[:half], lower[:half]], axis=0)
    z_im = jnp.concatenate([upper[half:], lower[half:]], axis=0)

    near = [z[:, : width // 2] for z in (z_re, z_im)]
    far = [z[:, width // 2 :] for z in (z_re, z_im)]
    mixed = [a + b for a, b in zip(near, far)] + [a - b for a, b in zip(near, far)]
    high, low = split(jnp.concatenate(mixed, axis=1))
    high_ref[...] = high
    low_ref[...] = low
    count = first_ref.shape[0]
    for parity in range(2):
        table = 4 * height + 4 * count * parity
        cut = slice(parity * width, (parity + 1) * width)
        side_hi = jnp.concatenate([big[table : table + count], big[table + count : table + 2 * count]], axis=1)
        side_lo = jnp.concatenate(
            [big[table + 2 * count : table + 3 * count], big[table + 3 * count : table + 4 * count]], axis=1
        )
        one = across(side_hi, high[:, cut]) + across(side_lo, high[:, cut])
        one = one + across(side_hi, low[:, cut])
        for number, block in enumerate(lane_blocks(one)):
            sides_ref[number, pl.ds(parity, count, stride=2)] = block
    sides = jnp.concatenate([sides_ref[n] for n in range(height // 128)], axis=1)
    to_left, to_right = sides[:count], sides[count : 2 * count]
    first_ref[...] = jnp.where(is_odd, to_left, to_right)
    second_ref[...] = jnp.where(is_odd, to_right, to_left)
    for store in stores:
        store.wait()


def update(
    field, weight, window, spectrum, pupil, patterns, led_row, led_col, tables,
    margin, group=8,
):
    _, _, back_rows, back_cols = tables
    leds = led_row.shape[0]
    _, height, width = spectrum.shape
    half_h, half_w = height // 2, width // 2
    big = []
    for parity in range(2):
        freqs = np.arange(parity, height, 2) - height // 2
        re, im = wave(np.arange(height // 2), freqs, height, height)
        big += two_parts(np.block([[re, -im], [im, re]]))
    for parity in range(2):
        left = np.arange(parity, margin, 2)
        freqs = np.arange(width // 2) - width // 2
        l_re, l_im = wave(left, freqs, width, width)
        r_re, r_im = wave(left + width - margin, freqs, width, width)
        from_re = two_parts(np.concatenate([l_re, l_im, r_re, r_im]))
        from_im = two_parts(np.concatenate([-l_im, l_re, -r_im, r_re]))
        big += [from_re[0], from_im[0], from_re[1], from_im[1]]
    big = np.concatenate(big)
    back = np.concatenate([back_rows, back_cols])
    out_shape = (
        jax.ShapeDtypeStruct(spectrum.shape, F32),
        jax.ShapeDtypeStruct((height, 2 * width), BF16),
        jax.ShapeDtypeStruct((height, 2 * width), BF16),
        jax.ShapeDtypeStruct((2 * margin, height), F32),
        jax.ShapeDtypeStruct((2 * margin, height), F32),
    )
    return pl.pallas_call(
        functools.partial(update_kernel, group=group),
        out_shape=out_shape,
        in_specs=[pl.BlockSpec(memory_space=SMEM)] * 3
        + vmem_spec(6)
        + [pl.BlockSpec(memory_space=pltpu.HBM)],
        out_specs=(pl.BlockSpec(memory_space=pltpu.HBM), *vmem_spec(4)),
        scratch_shapes=[
            pltpu.VMEM(weight.shape, F32),
            pltpu.VMEM((2, height + 8, width + 128), F32),
            pltpu.VMEM((2, width // 128, height + 8, 128), F32),
            pltpu.VMEM(big.shape, BF16),
            pltpu.VMEM((height // 128, 4 * margin + 8, 128), F32),
            pltpu.SemaphoreType.DMA,
            pltpu.SemaphoreType.DMA((width // 128,)),
        ],
        compiler_params=pltpu.CompilerParams(vmem_limit_bytes=LIMIT),
        name="update",
    )(
        led_row, led_col, patterns, field, weight, window, spectrum, pupil, back,
        pltpu.with_memory_space_constraint(jnp.asarray(big), pltpu.HBM),
    )


def object_kernel(high_ref, low_ref, table_ref, out_hbm, edges_ref, out, sems):
    core = out_hbm.shape[1]
    margin = edges_ref.shape[2]
    half = core // 2
    depth = high_ref.shape[1] // 4
    cuts = (slice(0, half // 2 // 16 * 16 + 16), slice(half // 2 // 16 * 16 + 16, half))
    stores = []
    for number, cut in enumerate(cuts):
        for parity in range(2):
            lefts = []
            for begin in (4 * parity * half, (4 * parity + 1) * half):
                rows = slice(begin + cut.start, begin + cut.stop)
                more = slice(rows.start + 2 * half, rows.stop + 2 * half)
                lefts.append(jnp.concatenate([table_ref[rows], table_ref[more], table_ref[rows]], axis=1))
            left = jnp.concatenate(lefts, axis=0)
            products = []
            for part in range(2):
                lanes = slice((2 * parity + part) * depth, (2 * parity + part + 1) * depth)
                z_hi, z_lo = high_ref[:, lanes], low_ref[:, lanes]
                products.append(across(left, jnp.concatenate([z_hi, z_hi, z_lo], axis=1)))
            count = cut.stop - cut.start
            rows = pl.ds(2 * cut.start + parity, count, stride=2)
            real = products[0][:count] - products[1][count:]
            imaginary = products[0][count:] + products[1][:count]
            for part, values in enumerate((real, imaginary)):
                for lanes, block in enumerate(lane_blocks(values)):
                    out[part, lanes, rows] = block
        span = pl.ds(2 * cut.start, 2 * (cut.stop - cut.start))
        for lanes in range(out.shape[1]):
            store = pltpu.make_async_copy(
                out.at[:, lanes, span], out_hbm.at[:, span, pl.ds(lanes * 128, 128)],
                sems.at[number, lanes],
            )
            store.start()
            stores.append(store)
    for part in range(2):
        for side, begin in enumerate((0, core - margin)):
            edge = [out[part, n, begin : begin + margin] for n in range(out.shape[1])]
            edges_ref[part, side] = jnp.concatenate(edge, axis=1)
    for store in stores:
        store.wait()


def object_core(high, low, margin, core):
    height, width = high.shape[0], high.shape[1] // 2
    table = []
    for parity in range(2):
        places = margin + np.arange(parity, core, 2)
        table += two_parts(
            np.concatenate(wave(places, np.arange(width // 2) - width // 2, width, width))
        )
    table = np.concatenate(table)
    return pl.pallas_call(
        object_kernel,
        out_shape=(
            jax.ShapeDtypeStruct((2, core, height), F32),
            jax.ShapeDtypeStruct((2, 2, margin, height), F32),
        ),
        in_specs=vmem_spec(3),
        out_specs=(pl.BlockSpec(memory_space=pltpu.HBM), pl.BlockSpec(memory_space=VMEM)),
        scratch_shapes=[
            pltpu.VMEM((2, height // 128, core + 8, 128), F32),
            pltpu.SemaphoreType.DMA((2, height // 128)),
        ],
        compiler_params=pltpu.CompilerParams(vmem_limit_bytes=LIMIT),
        cost_estimate=pl.CostEstimate(
            flops=3_000_000_000, bytes_accessed=5_000_000, transcendentals=0
        ),
        name="object",
    )(high, low, table)


def blend_kernel(first_ref, second_ref, edges_ref, core_hbm, out_hbm, mixed, sems):
    tile = lax.axis_index("tile")
    is_odd = lax.rem(tile, 2) == 1
    margin, core = edges_ref.shape[2], out_hbm.shape[1]
    k = lax.broadcasted_iota(jnp.int32, (margin, 1), 0).astype(F32)
    span = 2.0 * margin
    from_left = jnp.where(is_odd, first_ref[...], second_ref[...])
    from_right = jnp.where(is_odd, second_ref[...], first_ref[...])
    sides = (
        ((k + margin + 0.5) / span, (margin - k - 0.5) / span, tile > 0, from_left, 0),
        (
            (span - k - 0.5) / span, (k + 0.5) / span, tile < lax.axis_size("tile") - 1, from_right,
            core - margin,
        ),
    )
    stores = []
    for side, (own_w, other_w, has_other, other, begin) in enumerate(sides):
        own_w = jnp.where(has_other, own_w, 1.0)
        other_w = jnp.where(has_other, other_w, 0.0)
        for part in range(2):
            cut = slice(part * margin, (part + 1) * margin)
            mixed[side, part] = edges_ref[part, side] * own_w + other[cut] * other_w
        store = pltpu.make_async_copy(
            mixed.at[side], out_hbm.at[:, pl.ds(begin, margin)], sems.at[side]
        )
        store.start()
        stores.append(store)
    for store in stores:
        store.wait()


def blend(core_part, edges, first, second):
    return pl.pallas_call(
        blend_kernel,
        out_shape=jax.ShapeDtypeStruct(core_part.shape, F32),
        in_specs=vmem_spec(3) + [pl.BlockSpec(memory_space=pltpu.HBM)],
        out_specs=pl.BlockSpec(memory_space=pltpu.HBM),
        input_output_aliases={3: 0},
        scratch_shapes=[pltpu.VMEM(edges.shape, F32), pltpu.SemaphoreType.DMA((2,))],
        compiler_params=pltpu.CompilerParams(vmem_limit_bytes=LIMIT),
        name="blend",
    )(first, second, edges, core_part)


def body(raw, scales, flat, spectrum, pupil, patterns, led_row, led_col):
    height, core = flat.shape
    margin = OV // 2
    width = core + OV
    tiles = lax.axis_size("tile")
    frames_here = raw.shape[0]
    band_rows, band_cols = pupil.shape[1:]
    spectrum_tile = spectrum[0]
    patterns = patterns.T

    swap_a = [(i, i ^ 1) for i in range(tiles)]
    swap_b = [(i, ((i + 1) ^ 1) - 1) for i in range(1, tiles - 1)]

    def neighbours(for_a, for_b):
        return lax.ppermute(for_a, "tile", swap_a), lax.ppermute(for_b, "tile", swap_b)

    tables = stacked_tables(height, width, band_rows, band_cols)
    passes = (low_pass(height, band_rows), low_pass(width, band_cols).T)

    by_rows = gains_by_rows(flat.T, tiles, width)
    dequantized = dequantize(raw, scales, by_rows, tiles, core, margin)
    gains = lax.all_to_all(by_rows, "tile", split_axis=0, concat_axis=0, tiled=True)
    narrow = strips(dequantized, gains, passes[1], frames_here, core, margin)
    arrived = lax.all_to_all(narrow, "tile", split_axis=0, concat_axis=0, tiled=True)
    handed = window_tables(tiles, passes, margin, core)
    field, estimate, rows, small = all_fields(
        spectrum_tile, pupil, patterns, led_row, led_col, tables, handed
    )
    window = windows(arrived, rows, small, frames_here, core)
    field, weight = fetch(field, estimate, window, patterns)

    swap_core = [(i, i ^ 1) for i in range(4)]
    swap_chip = [(i, i ^ 2) for i in range(4)]
    other = functools.partial(lax.ppermute, axis_name="grp")
    window_2 = other(window, perm=swap_chip)
    window_1 = other(window, perm=swap_core)
    window_2, field, weight = lax.optimization_barrier((window_2, field, weight))
    window_3 = other(window_2, perm=swap_core)
    weight = collect(weight, window_1, window_2, patterns)

    fresh, high, low, for_a, for_b = update(
        field, weight, window_3, spectrum_tile, pupil, patterns,
        led_row, led_col, tables, margin,
    )
    side_a, side_b = neighbours(for_a, for_b)
    core_part, edges = object_core(high, low, margin, core)
    stitched = blend(core_part, edges, side_a, side_b)
    return fresh[None], jnp.transpose(stitched, (0, 2, 1))


def solution(mesh):
    return jax.shard_map(
        body,
        mesh=mesh,
        in_specs=(
            P("grp", "tile", None),
            P("grp", "tile", None),
            P(None, "tile"),
            P("tile", None, None, None),
            P(),
            P(),
            P(),
            P(),
        ),
        out_specs=(P("tile", None, None, None), P(None, None, "tile")),
        check_vma=False,
    )
```

```python
import functools
import math

import jax
import jax.numpy as jnp
import ml_dtypes
import numpy as np
from jax import lax
from jax.experimental import pallas as pl
from jax.experimental.pallas import tpu as pltpu
from jax.sharding import PartitionSpec as P

OV = 32
BC = 32
STEP = 0.02
F32 = jnp.float32
BF16 = jnp.bfloat16
VMEM = pltpu.VMEM
SMEM = pltpu.SMEM
LIMIT = 30 << 20


def two_parts(table):
    table = np.asarray(table, np.float64)
    high = table.astype(ml_dtypes.bfloat16)
    low = (table - high.astype(np.float64)).astype(ml_dtypes.bfloat16)
    return high, low


def wave(places, freqs, length, norm):
    turns = np.outer(places, freqs) % length
    angle = turns * (2.0 * math.pi / length)
    return np.cos(angle) / math.sqrt(norm), np.sin(angle) / math.sqrt(norm)


def pairs(length):
    first = np.arange(1, length // 2, 2)
    return np.concatenate([first, length - first])


def low_pass(length, band):
    places = pairs(length)[:, None] - np.arange(length)[None, :]
    total = np.ones(places.shape)
    for freq in range(1, band):
        total += 2.0 * np.cos(2.0 * math.pi * ((freq * places) % length) / length)
    return total / length


def stacked_tables(height, width, band_rows, band_cols):
    row_re, row_im = wave(
        pairs(height), np.arange(band_rows) - band_rows // 2, height, band_rows
    )
    rows = np.block([[row_re, -row_im], [row_im, row_re]])
    col_re, col_im = wave(
        np.arange(band_cols) - band_cols // 2, pairs(width), width, band_cols
    )
    cols = np.block([[col_re, col_im], [-col_im, col_re]])
    half_rows, half_cols = height // 4, width // 4
    high, low = two_parts(np.concatenate([row_re[:half_rows], row_im[:half_rows]]).T)
    back_rows = np.block([[high, high], [low, np.zeros_like(low)]])
    back_cols = np.concatenate(
        two_parts(np.concatenate([col_re[:, :half_cols], col_im[:, :half_cols]], axis=1).T), axis=1
    )
    return rows, cols, back_rows, back_cols


def split(values):
    high = values.astype(BF16)
    return high, (values - high.astype(F32)).astype(BF16)


def mm(left, right):
    return jnp.dot(left, right, preferred_element_type=F32)


def vmem_spec(count):
    return [pl.BlockSpec(memory_space=VMEM)] * count


def lane_blocks(values):
    return [values[:, begin : begin + 128] for begin in range(0, values.shape[1], 128)]


def parts_rows(values):
    high = values.astype(BF16).astype(F32)
    return jnp.concatenate([high, values - high], axis=0).astype(BF16)


def rows_value(rows):
    rows = rows.astype(F32)
    return rows[:8, :128] + rows[8:, :128]


def gains_kernel(flat_ref, out_hbm, out, sems):
    core, height = flat_ref.shape
    tiles, rows_here, width = out_hbm.shape
    stores = []
    for number, begin in enumerate(range(0, width, 128)):
        length = min(128, core - begin)
        gains = flat_ref[begin : begin + length] - 1.0
        if length < 128:
            gains = jnp.concatenate([gains, jnp.zeros((128 - length, height), F32)], axis=0)
        by_rows = jnp.transpose(gains, (1, 0)).reshape(tiles, rows_here, 128)
        out[:, :, begin : begin + 128] = by_rows.astype(BF16)
        part = (slice(None), slice(None), pl.ds(begin, 128))
        store = pltpu.make_async_copy(out.at[part], out_hbm.at[part], sems.at[number])
        store.start()
        stores.append(store)
    for store in stores:
        store.wait()


def gains_by_rows(flat, tiles, width):
    core, height = flat.shape
    shape = (tiles, height // tiles, width)
    return pl.pallas_call(
        gains_kernel,
        out_shape=jax.ShapeDtypeStruct(shape, BF16),
        in_specs=vmem_spec(1),
        out_specs=pl.BlockSpec(memory_space=pltpu.HBM),
        scratch_shapes=[pltpu.VMEM(shape, BF16), pltpu.SemaphoreType.DMA((width // 128,))],
        compiler_params=pltpu.CompilerParams(vmem_limit_bytes=LIMIT),
        name="gains",
    )(flat)


def dequantize_kernel(raw_ref, scales_ref, after, out_ref, *, core, margin):
    lines, strip = raw_ref.shape
    coarse_rows, coarse_cols = scales_ref.shape
    tiles, _, width = out_ref.shape
    ratio = lines // coarse_rows
    row = lax.broadcasted_iota(jnp.int32, (lines, coarse_rows), 0)
    pick = lax.broadcasted_iota(jnp.int32, (lines, coarse_rows), 1)
    spread_rows = (row // ratio == pick).astype(F32).astype(BF16)
    factors = mm(spread_rows, scales_ref[...])
    wide = (coarse_cols // 128 + 1) * 128
    factors = jnp.concatenate([factors, jnp.zeros((lines, wide - coarse_cols), F32)], axis=1)

    blocks = []
    for tile in range(tiles):
        begin = (tile * core - margin) // BC
        blocks.append(pltpu.roll(factors, -begin % wide, 1)[:, :128].astype(BF16))
    block = lax.broadcasted_iota(jnp.int32, (128, width), 0)
    place = lax.broadcasted_iota(jnp.int32, (128, width), 1) + (-margin) % BC
    inside = (place >= block * BC) & (place < (block + 1) * BC)
    scales = mm(jnp.concatenate(blocks, axis=0), inside.astype(F32).astype(BF16))
    for tile in range(tiles):
        start = tile * core - margin
        base = max(start, 0) // 128 * 128
        span = min(width + 128, strip - base)
        codes = raw_ref[:, base : base + span].astype(F32)
        turn = (base - start) % span
        if turn:
            codes = pltpu.roll(codes, turn, 1)
        out_ref[tile] = codes[:, :width] * scales[tile * lines : (tile + 1) * lines]


def dequantize(raw, scales, after, tiles, core, margin):
    frames, rows_here, strip = raw.shape
    return pl.pallas_call(
        functools.partial(dequantize_kernel, core=core, margin=margin),
        out_shape=jax.ShapeDtypeStruct((tiles, frames * rows_here, core + 2 * margin), F32),
        in_specs=vmem_spec(2) + [pl.BlockSpec(memory_space=pl.ANY)],
        out_specs=pl.BlockSpec(memory_space=VMEM),
        compiler_params=pltpu.CompilerParams(vmem_limit_bytes=LIMIT),
        cost_estimate=pl.CostEstimate(
            flops=2_000_000_000, bytes_accessed=4_000_000, transcendentals=0
        ),
        name="dequantize",
    )(raw.reshape(frames * rows_here, strip), scales.reshape(-1, scales.shape[-1]), after)


def strips_kernel(dq_ref, gains_ref, lc_ref, out_hbm, out_ref, sems, *, frames, core, margin):
    tiles, lines, width = dq_ref.shape
    half_w = lc_ref.shape[1]
    rows_here = lines // frames
    line = lax.broadcasted_iota(jnp.int32, (1, width), 1)
    in_core = ((line >= margin) & (line < margin + core)).astype(F32)
    xc = (line.astype(F32) - margin - (core - 1) / 2.0) * in_core
    first_row = (lax.axis_index("tile") * rows_here).astype(F32)
    height = rows_here * tiles
    yc = lax.broadcasted_iota(jnp.int32, (rows_here, 1), 0).astype(F32)
    yc = yc + (first_row - (height - 1) / 2.0)
    lane = lax.broadcasted_iota(jnp.int32, (8, 128), 1)
    narrow_lane = lax.broadcasted_iota(jnp.int32, (1, 128), 1)

    lc_hi, lc_lo = lc_ref[:width], lc_ref[width:]
    own, stores = [], []

    all_yc = jnp.concatenate([yc] * frames, axis=0)

    def by_frame(values, weights):
        sums = []
        for frame in range(frames):
            one = values[frame * rows_here : (frame + 1) * rows_here]
            one = functools.reduce(
                jnp.add, [one[row : row + 8] for row in range(0, rows_here, 8)]
            )
            if weights is not None:
                one = one * weights
            one = functools.reduce(jnp.add, lane_blocks(one))
            one = jnp.sum(one, axis=1, keepdims=True)
            sums.append(jnp.sum(one, axis=0, keepdims=True))
        return jnp.concatenate(sums + [jnp.zeros((8 - frames, 1), F32)], axis=0)

    def windowed(tile):
        gains = pltpu.roll(gains_ref[tile].astype(F32), margin, 1)
        if tile > 0:
            end = gains_ref[tile - 1][:, width - 128 :].astype(F32)
            end = pltpu.roll(end, (2 * margin) + margin, 1)
            end = jnp.where(narrow_lane < margin, end, 0.0)
            gains = jnp.concatenate([gains[:, :128] + end, gains[:, 128:]], axis=1)
        if tile < tiles - 1:
            end = gains_ref[tile + 1][:, :128].astype(F32)
            end = pltpu.roll(end, 128 - margin, 1)
            end = jnp.where(narrow_lane >= 128 - margin, end, 0.0)
            gains = jnp.concatenate(
                [gains[:, : width - 128], gains[:, width - 128 :] + end], axis=1
            )
        gains = jnp.concatenate([gains + 1.0] * frames, axis=0)
        flattened = dq_ref[tile] * gains
        slope_y = by_frame(flattened * all_yc, in_core)
        slope_x = by_frame(flattened, xc)
        own.append(jnp.where(lane == 0, slope_y, jnp.where(lane == 1, slope_x, 0.0)))
        return flattened.astype(BF16)

    def finish(tile, one):
        mean = by_frame(one, None) * (1.0 / (rows_here * half_w))
        centred = []
        for frame in range(frames):
            cut = slice(frame * rows_here, (frame + 1) * rows_here)
            centred.append(one[cut] - mean[frame : frame + 1])
        centred = jnp.concatenate(centred, axis=0)
        for part in range(half_w // 128):
            columns = centred[:, part * 128 : (part + 1) * 128]
            out_ref[tile, part * lines : (part + 1) * lines] = columns.astype(BF16)
        packed = own[tile] + jnp.where(lane == 6, mean, 0.0)
        if tile > 0:
            packed += pltpu.roll(own[tile - 1], 2, 1)
        if tile < tiles - 1:
            packed += pltpu.roll(own[tile + 1], 4, 1)
        out_ref[tile, half_w // 128 * lines :] = parts_rows(packed)

    part_tiles = max(tiles // 2, 1)
    waiting = None
    for begin in range(0, tiles, part_tiles):
        pixels = jnp.concatenate([windowed(t) for t in range(begin, begin + part_tiles)], axis=0)
        if waiting is not None:
            finish(*waiting)
        narrow = mm(pixels, lc_hi) + mm(pixels, lc_lo)
        for number in range(part_tiles):
            one = (begin + number, narrow[number * lines : (number + 1) * lines])
            if number == part_tiles - 1 and begin + part_tiles < tiles:
                waiting = one
            else:
                finish(*one)
        done = begin + part_tiles - (1 if begin + part_tiles < tiles else 0)
        first = max(begin - 1, 0)
        span = pl.ds(first, done - first)
        store = pltpu.make_async_copy(out_ref.at[span], out_hbm.at[span], sems.at[begin // part_tiles])
        store.start()
        stores.append(store)
    for store in stores:
        store.wait()


def strips(dequantized, gains, lc, frames, core, margin):
    tiles, lines, _ = dequantized.shape
    shape = (tiles, lines * (lc.shape[1] // 128) + 16, 128)
    return pl.pallas_call(
        functools.partial(strips_kernel, frames=frames, core=core, margin=margin),
        out_shape=jax.ShapeDtypeStruct(shape, BF16),
        in_specs=vmem_spec(3),
        out_specs=pl.BlockSpec(memory_space=pltpu.HBM),
        scratch_shapes=[pltpu.VMEM(shape, BF16), pltpu.SemaphoreType.DMA((2,))],
        compiler_params=pltpu.CompilerParams(vmem_limit_bytes=LIMIT),
        name="strips",
    )(dequantized, gains, np.concatenate(two_parts(lc)))


def box_area(top, left, band_rows, band_cols):
    row = top // 8 * 8
    col = left // 128 * 128
    area = (
        pl.ds(pl.multiple_of(row, 8), band_rows + 8),
        pl.ds(pl.multiple_of(col, 128), band_cols + 128),
    )
    return area, top - row, left - col


def field_kernel(
    led_row, led_col, patterns, spec_ref, pupil_ref, cols_ref, rows_ref,
    rows_hbm, small_hbm, field_ref, estimate_ref, rows_out, small_out, wide, bright, sems, *, group,
):
    leds, half_h, half_w = bright.shape
    loads = [
        pltpu.make_async_copy(rows_hbm, rows_out, sems.at[0]),
        pltpu.make_async_copy(small_hbm, small_out, sems.at[1]),
    ]
    for load in loads:
        load.start()
    band_rows, band_cols = pupil_ref.shape[1:]
    width = spec_ref.shape[2]
    depth = 2 * band_cols
    wide[...] = jnp.zeros_like(wide)
    wide[:, : spec_ref.shape[1], :width] = spec_ref[...]

    def some(step, carry):
        boxes = []
        for place in range(group):
            led = step * group + place
            area, down, right = box_area(led_row[led], led_col[led], band_rows, band_cols)
            back = lax.rem(2 * band_cols - right, 2 * band_cols)
            up = lax.rem(band_rows + 8 - down, band_rows + 8)
            parts = []
            for part in range(2):
                strip = pltpu.roll(wide[(part, *area)], back, 1)
                parts.append(pltpu.roll(strip[:, :band_cols], up, 0)[:band_rows])
            lit_re = pupil_ref[0] * parts[0] - pupil_ref[1] * parts[1]
            lit_im = pupil_ref[0] * parts[1] + pupil_ref[1] * parts[0]
            boxes.append(jnp.concatenate([lit_re, lit_im], axis=1))
        high, low = split(jnp.concatenate(boxes, axis=0))
        cols_hi, cols_lo = cols_ref[:depth], cols_ref[depth:]
        spread = mm(high, cols_hi) + mm(high, cols_lo) + mm(low, cols_hi)
        for place in range(group):
            one = spread[place * band_rows : (place + 1) * band_rows]
            high, low = split(jnp.concatenate([one[:, :half_w], one[:, half_w:]], axis=0))
            field = mm(rows_ref[...], jnp.concatenate([high, low, high], axis=0))
            field_ref[step * group + place] = field
            bright[step * group + place] = field[:half_h] ** 2 + field[half_h:] ** 2
        return carry

    lax.fori_loop(0, leds // group, some, 0)

    def one_frame(frame, carry):
        total = bright[patterns[0, frame]]
        for lit in range(1, patterns.shape[0]):
            total += bright[patterns[lit, frame]]
        estimate_ref[frame] = total
        return carry

    lax.fori_loop(0, patterns.shape[1], one_frame, 0)
    for load in loads:
        load.wait()


def all_fields(spectrum, pupil, patterns, led_row, led_col, tables, handed, group=8):
    rows, cols, _, _ = tables
    leds = led_row.shape[0]
    _, height, width = spectrum.shape
    half_h, half_w = height // 2, width // 2
    high, low = two_parts(rows)
    return pl.pallas_call(
        functools.partial(field_kernel, group=group),
        out_shape=(
            jax.ShapeDtypeStruct((leds, 2 * half_h, half_w), F32),
            jax.ShapeDtypeStruct((patterns.shape[1], half_h, half_w), F32),
            *(jax.ShapeDtypeStruct(table.shape, table.dtype) for table in handed),
        ),
        in_specs=[pl.BlockSpec(memory_space=SMEM)] * 3
        + vmem_spec(4)
        + [pl.BlockSpec(memory_space=pltpu.HBM)] * 2,
        out_specs=tuple(vmem_spec(4)),
        scratch_shapes=[
            pltpu.VMEM((2, height + 8, width + 128), F32),
            pltpu.VMEM((leds, half_h, half_w), F32),
            pltpu.SemaphoreType.DMA((2,)),
        ],
        compiler_params=pltpu.CompilerParams(vmem_limit_bytes=LIMIT),
        cost_estimate=pl.CostEstimate(
            flops=8_000_000_000, bytes_accessed=16_000_000, transcendentals=0
        ),
        name="fields",
    )(
        led_row, led_col, patterns, spectrum, pupil, np.concatenate(two_parts(cols)),
        np.concatenate([high, high, low], axis=1),
        *(pltpu.with_memory_space_constraint(jnp.asarray(t), pltpu.HBM) for t in handed),
    )


def window_kernel(dq_ref, rows_ref, small_ref, *window_refs, frames, core):
    slabs, lines, _ = dq_ref.shape
    half_h, half_w = rows_ref.shape[0], window_refs[0].shape[1]
    count = frames // len(window_refs)
    halves = half_w // 128
    lines = (lines - 16) // halves
    lr_sum, line = small_ref[:half_h, :128], small_ref[half_h:]
    rows_here = lines // frames
    height = slabs * rows_here
    over_y = 1.0 / (core * (height * (height * height - 1) / 12.0))
    over_x = 1.0 / (height * (core * (core * core - 1) / 12.0))
    lane = lax.broadcasted_iota(jnp.int32, (8, 128), 1)
    notes = [rows_value(dq_ref[slab, halves * lines :]) for slab in range(slabs)]
    slopes = functools.reduce(jnp.add, notes)
    slopes = slopes * jnp.where(lane % 2 == 0, over_y, over_x)
    slab_means = jnp.zeros((8, 128), F32)
    for slab in range(slabs):
        slab_means = jnp.where(lane == slab, notes[slab][:, 6:7], slab_means)
    values = []
    for slab in range(slabs):
        parts = [dq_ref[slab, part * lines : (part + 1) * lines] for part in range(halves)]
        values.append(jnp.concatenate(parts, axis=1))
    if rows_here % 16:
        values = [value.astype(F32) for value in values]
    means = []
    for frame in range(frames):
        cut = slice(frame * rows_here, (frame + 1) * rows_here)
        whole = jnp.concatenate([v[cut] for v in values], axis=0).astype(BF16)
        window = mm(rows_ref[...], jnp.concatenate([whole, whole], axis=0))
        level = jnp.sum(lr_sum * slab_means[frame : frame + 1], axis=1, keepdims=True)
        window = window + level
        tilt_y, tilt_x = 0.0, 0.0
        for side in range(3):
            tilt_y += line[2 * side : 2 * side + 1] * slopes[frame : frame + 1, 2 * side : 2 * side + 1]
            tilt_x += line[2 * side + 1 : 2 * side + 2] * slopes[frame : frame + 1, 2 * side + 1 : 2 * side + 2]
        window = window - lr_sum[:, 127:128] * tilt_y - tilt_x
        mean = jnp.sum(window, axis=0, keepdims=True)
        mean = jnp.sum(mean, axis=1, keepdims=True) * (1.0 / (half_h * half_w))
        means.append(jnp.broadcast_to(mean, (1, 128)))
        begin = frame % count * half_h
        window_refs[frame // count][begin : begin + half_h] = (window - mean).astype(BF16)
    means = jnp.concatenate(means + [jnp.zeros((8 - frames, 128), F32)], axis=0)
    notes = jnp.concatenate([parts_rows(means)] * halves, axis=1)
    for window_ref in window_refs:
        window_ref[count * half_h :] = notes


def tilt_lines(width, margin, core, lc):
    local = np.arange(width) - margin
    lines = []
    for begin, end, shift in ((0, core, 0), (-margin, 0, core), (core, core + margin, -core)):
        on = (local >= begin) & (local < end)
        lines.append(on.astype(np.float64) @ lc)
        lines.append(((local + shift - (core - 1) / 2.0) * on) @ lc)
    return np.stack(lines + lines[:2])


def window_tables(tiles, passes, margin, core):
    lr, lc = passes
    half_h, height = lr.shape
    sums = np.zeros((half_h, lc.shape[1]))
    sums[:, :tiles] = lr.reshape(half_h, tiles, height // tiles).sum(axis=2)
    sums[:, 127] = lr @ (np.arange(height) - (height - 1) / 2.0)
    small = np.concatenate([sums, tilt_lines(lc.shape[0], margin, core, lc)])
    return np.concatenate(two_parts(lr), axis=1), small.astype(np.float32)


def windows(arrived, rows, small, frames, core):
    half_h, half_w = rows.shape[0], small.shape[1]
    return pl.pallas_call(
        functools.partial(window_kernel, frames=frames, core=core),
        out_shape=(jax.ShapeDtypeStruct((frames // 2 * half_h + 16, half_w), BF16),) * 2,
        in_specs=vmem_spec(3),
        out_specs=tuple(vmem_spec(2)),
        compiler_params=pltpu.CompilerParams(vmem_limit_bytes=LIMIT),
        name="windows",
    )(arrived, rows, small)


def add_frame(weight, patterns, frame, value):
    for lit in range(patterns.shape[0]):
        weight[patterns[lit, frame]] += value


def take_windows(weight, patterns, windows_here, places, half_h):
    for window, (slot, part) in zip(windows_here, places):
        count = window.shape[0] // half_h
        owner = jnp.bitwise_xor(lax.axis_index("grp"), slot)
        means = rows_value(window[count * half_h :])
        for place in range(count):
            value = window[place * half_h : (place + 1) * half_h].astype(F32)
            own = part * count + place
            value = -means[own : own + 1, 0:1] - value
            add_frame(weight, patterns, owner * (2 * count) + own, value)


def fetch_kernel(patterns, estimate_ref, part_a, part_b, field_hbm, field_ref, weight, sem):
    quarter = field_ref.shape[0] // 4
    loads = []
    for number in range(4):
        part = pl.ds(number * quarter, quarter)
        load = pltpu.make_async_copy(field_hbm.at[part], field_ref.at[part], sem.at[number])
        load.start()
        loads.append(load)
    weight[...] = jnp.zeros_like(weight)
    frames, half_h, _ = estimate_ref.shape

    def one_frame(frame, carry):
        add_frame(weight, patterns, frame, estimate_ref[frame])
        return carry

    lax.fori_loop(0, frames, one_frame, 0)
    take_windows(weight, patterns, (part_a, part_b), ((0, 0), (0, 1)), half_h)
    for load in loads:
        load.wait()


def fetch(field, estimate, window, patterns):
    leds = field.shape[0]
    return pl.pallas_call(
        fetch_kernel,
        out_shape=(
            jax.ShapeDtypeStruct(field.shape, F32),
            jax.ShapeDtypeStruct((leds, *estimate.shape[1:]), F32),
        ),
        in_specs=[pl.BlockSpec(memory_space=SMEM)]
        + vmem_spec(3)
        + [pl.BlockSpec(memory_space=pltpu.HBM)],
        out_specs=tuple(vmem_spec(2)),
        scratch_shapes=[pltpu.SemaphoreType.DMA((4,))],
        compiler_params=pltpu.CompilerParams(vmem_limit_bytes=LIMIT),
        cost_estimate=pl.CostEstimate(flops=0, bytes_accessed=16_000_000, transcendentals=0),
        name="fetch",
    )(patterns, estimate, *window, pltpu.with_memory_space_constraint(field, pltpu.HBM))


def collect_kernel(patterns, w1a, w1b, w2a, w2b, weight_in, weight):
    weight[...] = weight_in[...]
    places = ((1, 0), (1, 1), (2, 0), (2, 1))
    take_windows(weight, patterns, (w1a, w1b, w2a, w2b), places, weight.shape[1])


def collect(weight, here, patterns):
    return pl.pallas_call(
        collect_kernel,
        out_shape=jax.ShapeDtypeStruct(weight.shape, F32),
        in_specs=[pl.BlockSpec(memory_space=SMEM)] + vmem_spec(5),
        out_specs=pl.BlockSpec(memory_space=VMEM),
        compiler_params=pltpu.CompilerParams(vmem_limit_bytes=LIMIT),
        name="collect",
    )(patterns, *here, weight)


def across(left, right):
    dims = (((1,), (1,)), ((), ()))
    return lax.dot_general(left, right, dims, preferred_element_type=F32)


def update_kernel(
    led_row, led_col, patterns, field_ref, weight_in, w3a, w3b,
    spec_ref, pupil_ref, back_ref, big_hbm,
    fresh_hbm, high_ref, low_ref, first_ref, second_ref,
    weight, grads, fresh_ref, big, sides_ref, big_sem, fresh_sems, *, group,
):
    leds, half_h, half_w = weight.shape
    band_rows, band_cols = pupil_ref.shape[1:]
    height, width = spec_ref.shape[1:]
    is_odd = lax.rem(lax.axis_index("tile"), 2) == 1
    big_load = pltpu.make_async_copy(big_hbm, big, big_sem)
    big_load.start()
    grads[...] = jnp.zeros_like(grads)
    weight[...] = weight_in[...]
    take_windows(weight, patterns, (w3a, w3b), ((3, 0), (3, 1)), half_h)

    left_rows = 2 * band_rows
    pair_rows, pair_cols = half_h // 2, half_w // 2

    def some(step, carry):
        backs = []
        for place in range(group):
            q = weight[step * group + place]
            field = field_ref[step * group + place]
            g_re, g_im = field[:half_h] * q, field[half_h:] * q
            re_a, re_b = g_re[:pair_rows], g_re[pair_rows:]
            im_a, im_b = g_im[:pair_rows], g_im[pair_rows:]
            to_re = jnp.concatenate([re_a + re_b, im_a - im_b], axis=0)
            to_im = jnp.concatenate([im_a + im_b, re_b - re_a], axis=0)
            high, low = split(jnp.concatenate([to_re, to_im], axis=1))
            both = mm(back_ref[:left_rows], jnp.concatenate([high, low], axis=0))
            back = both[:band_rows] + both[band_rows:]
            re_a, re_b = back[:, :pair_cols], back[:, pair_cols : 2 * pair_cols]
            im_a, im_b = back[:, 2 * pair_cols : 3 * pair_cols], back[:, 3 * pair_cols :]
            backs.append(jnp.concatenate([re_a + re_b, im_a - im_b], axis=1))
            backs.append(jnp.concatenate([im_a + im_b, re_b - re_a], axis=1))
        high, low = split(jnp.concatenate(backs, axis=0))
        cols = back_ref[left_rows:]
        both = mm(jnp.concatenate([high, low], axis=1), jnp.concatenate([cols, cols], axis=0))
        boxes = both[:, :band_cols] + both[:, band_cols:]
        for place in range(group):
            led = step * group + place
            begin = 2 * place * band_rows
            back_re = boxes[begin : begin + band_rows]
            back_im = boxes[begin + band_rows : begin + 2 * band_rows]
            parts = (
                pupil_ref[0] * back_re + pupil_ref[1] * back_im,
                pupil_ref[0] * back_im - pupil_ref[1] * back_re,
            )
            area, down, right = box_area(led_row[led], led_col[led], band_rows, band_cols)
            for part in range(2):
                filled = jnp.concatenate([parts[part], jnp.zeros((8, band_cols), F32)], axis=0)
                filled = pltpu.roll(filled, down, 0)
                filled = jnp.concatenate([filled, jnp.zeros((band_rows + 8, 128), F32)], axis=1)
                grads[(part, *area)] += pltpu.roll(filled, right, 1)
        return carry

    lax.fori_loop(0, leds // group, some, 0)
    fresh_re = spec_ref[0] - (4.0 * STEP) * grads[0, :height, :width]
    fresh_im = spec_ref[1] - (4.0 * STEP) * grads[1, :height, :width]
    for part, fresh in enumerate((fresh_re, fresh_im)):
        for number, block in enumerate(lane_blocks(fresh)):
            fresh_ref[part, number, :height] = block
    stores = []
    for number in range(width // 128):
        store = pltpu.make_async_copy(
            fresh_ref.at[:, number, pl.ds(0, height)], fresh_hbm.at[:, :, pl.ds(number * 128, 128)],
            fresh_sems.at[number],
        )
        store.start()
        stores.append(store)
    big_load.wait()

    def spread(parity, table):
        rows = pl.ds(parity, height // 2, stride=2)
        parts = [
            jnp.concatenate([fresh_ref[part, n, rows] for n in range(width // 128)], axis=1)
            for part in range(2)
        ]
        high, low = split(jnp.concatenate(parts, axis=0))
        table_hi, table_lo = big[table : table + height], big[table + height : table + 2 * height]
        left = jnp.concatenate([table_hi, table_lo, table_hi], axis=1)
        return mm(left, jnp.concatenate([high, high, low], axis=0))

    even, odd = spread(0, 0), spread(1, 2 * height)
    upper, lower = even + odd, even - odd
    half = height // 2
    z_re = jnp.concatenate([upper[:half], lower[:half]], axis=0)
    z_im = jnp.concatenate([upper[half:], lower[half:]], axis=0)

    near = [z[:, : width // 2] for z in (z_re, z_im)]
    far = [z[:, width // 2 :] for z in (z_re, z_im)]
    mixed = [a + b for a, b in zip(near, far)] + [a - b for a, b in zip(near, far)]
    high, low = split(jnp.concatenate(mixed, axis=1))
    high_ref[...] = high
    low_ref[...] = low
    count = first_ref.shape[0]
    for parity in range(2):
        table = 4 * height + 4 * count * parity
        cut = slice(parity * width, (parity + 1) * width)
        side_hi = jnp.concatenate([big[table : table + count], big[table + count : table + 2 * count]], axis=1)
        side_lo = jnp.concatenate(
            [big[table + 2 * count : table + 3 * count], big[table + 3 * count : table + 4 * count]], axis=1
        )
        one = across(side_hi, high[:, cut]) + across(side_lo, high[:, cut])
        one = one + across(side_hi, low[:, cut])
        for number, block in enumerate(lane_blocks(one)):
            sides_ref[number, pl.ds(parity, count, stride=2)] = block
    sides = jnp.concatenate([sides_ref[n] for n in range(height // 128)], axis=1)
    to_left, to_right = sides[:count], sides[count : 2 * count]
    first_ref[...] = jnp.where(is_odd, to_left, to_right)
    second_ref[...] = jnp.where(is_odd, to_right, to_left)
    for store in stores:
        store.wait()


def update(
    field, weight, window, spectrum, pupil, patterns, led_row, led_col, tables,
    margin, group=8,
):
    _, _, back_rows, back_cols = tables
    leds = led_row.shape[0]
    _, height, width = spectrum.shape
    half_h, half_w = height // 2, width // 2
    big = []
    for parity in range(2):
        freqs = np.arange(parity, height, 2) - height // 2
        re, im = wave(np.arange(height // 2), freqs, height, height)
        big += two_parts(np.block([[re, -im], [im, re]]))
    for parity in range(2):
        left = np.arange(parity, margin, 2)
        freqs = np.arange(width // 2) - width // 2
        l_re, l_im = wave(left, freqs, width, width)
        r_re, r_im = wave(left + width - margin, freqs, width, width)
        from_re = two_parts(np.concatenate([l_re, l_im, r_re, r_im]))
        from_im = two_parts(np.concatenate([-l_im, l_re, -r_im, r_re]))
        big += [from_re[0], from_im[0], from_re[1], from_im[1]]
    big = np.concatenate(big)
    back = np.concatenate([back_rows, back_cols])
    out_shape = (
        jax.ShapeDtypeStruct(spectrum.shape, F32),
        jax.ShapeDtypeStruct((height, 2 * width), BF16),
        jax.ShapeDtypeStruct((height, 2 * width), BF16),
        jax.ShapeDtypeStruct((2 * margin, height), F32),
        jax.ShapeDtypeStruct((2 * margin, height), F32),
    )
    return pl.pallas_call(
        functools.partial(update_kernel, group=group),
        out_shape=out_shape,
        in_specs=[pl.BlockSpec(memory_space=SMEM)] * 3
        + vmem_spec(7)
        + [pl.BlockSpec(memory_space=pltpu.HBM)],
        out_specs=(pl.BlockSpec(memory_space=pltpu.HBM), *vmem_spec(4)),
        scratch_shapes=[
            pltpu.VMEM(weight.shape, F32),
            pltpu.VMEM((2, height + 8, width + 128), F32),
            pltpu.VMEM((2, width // 128, height + 8, 128), F32),
            pltpu.VMEM(big.shape, BF16),
            pltpu.VMEM((height // 128, 4 * margin + 8, 128), F32),
            pltpu.SemaphoreType.DMA,
            pltpu.SemaphoreType.DMA((width // 128,)),
        ],
        compiler_params=pltpu.CompilerParams(vmem_limit_bytes=LIMIT),
        name="update",
    )(
        led_row, led_col, patterns, field, weight, *window, spectrum, pupil, back,
        pltpu.with_memory_space_constraint(jnp.asarray(big), pltpu.HBM),
    )


def object_kernel(high_ref, low_ref, table_ref, out_hbm, edges_ref, out, sems):
    core = out_hbm.shape[1]
    margin = edges_ref.shape[2]
    half = core // 2
    depth = high_ref.shape[1] // 4
    cuts = (slice(0, half // 2 // 16 * 16 + 16), slice(half // 2 // 16 * 16 + 16, half))
    stores = []
    for number, cut in enumerate(cuts):
        for parity in range(2):
            lefts = []
            for begin in (4 * parity * half, (4 * parity + 1) * half):
                rows = slice(begin + cut.start, begin + cut.stop)
                more = slice(rows.start + 2 * half, rows.stop + 2 * half)
                lefts.append(jnp.concatenate([table_ref[rows], table_ref[more], table_ref[rows]], axis=1))
            left = jnp.concatenate(lefts, axis=0)
            products = []
            for part in range(2):
                lanes = slice((2 * parity + part) * depth, (2 * parity + part + 1) * depth)
                z_hi, z_lo = high_ref[:, lanes], low_ref[:, lanes]
                products.append(across(left, jnp.concatenate([z_hi, z_hi, z_lo], axis=1)))
            count = cut.stop - cut.start
            rows = pl.ds(2 * cut.start + parity, count, stride=2)
            real = products[0][:count] - products[1][count:]
            imaginary = products[0][count:] + products[1][:count]
            for part, values in enumerate((real, imaginary)):
                for lanes, block in enumerate(lane_blocks(values)):
                    out[part, lanes, rows] = block
        span = pl.ds(2 * cut.start, 2 * (cut.stop - cut.start))
        for lanes in range(out.shape[1]):
            store = pltpu.make_async_copy(
                out.at[:, lanes, span], out_hbm.at[:, span, pl.ds(lanes * 128, 128)],
                sems.at[number, lanes],
            )
            store.start()
            stores.append(store)
    for part in range(2):
        for side, begin in enumerate((0, core - margin)):
            edge = [out[part, n, begin : begin + margin] for n in range(out.shape[1])]
            edges_ref[part, side] = jnp.concatenate(edge, axis=1)
    for store in stores:
        store.wait()


def object_core(high, low, margin, core):
    height, width = high.shape[0], high.shape[1] // 2
    table = []
    for parity in range(2):
        places = margin + np.arange(parity, core, 2)
        table += two_parts(
            np.concatenate(wave(places, np.arange(width // 2) - width // 2, width, width))
        )
    table = np.concatenate(table)
    return pl.pallas_call(
        object_kernel,
        out_shape=(
            jax.ShapeDtypeStruct((2, core, height), F32),
            jax.ShapeDtypeStruct((2, 2, margin, height), F32),
        ),
        in_specs=vmem_spec(3),
        out_specs=(pl.BlockSpec(memory_space=pltpu.HBM), pl.BlockSpec(memory_space=VMEM)),
        scratch_shapes=[
            pltpu.VMEM((2, height // 128, core + 8, 128), F32),
            pltpu.SemaphoreType.DMA((2, height // 128)),
        ],
        compiler_params=pltpu.CompilerParams(vmem_limit_bytes=LIMIT),
        cost_estimate=pl.CostEstimate(
            flops=3_000_000_000, bytes_accessed=5_000_000, transcendentals=0
        ),
        name="object",
    )(high, low, table)


def blend_kernel(first_ref, second_ref, edges_ref, core_hbm, out_hbm, mixed, sems):
    tile = lax.axis_index("tile")
    is_odd = lax.rem(tile, 2) == 1
    margin, core = edges_ref.shape[2], out_hbm.shape[1]
    k = lax.broadcasted_iota(jnp.int32, (margin, 1), 0).astype(F32)
    span = 2.0 * margin
    from_left = jnp.where(is_odd, first_ref[...], second_ref[...])
    from_right = jnp.where(is_odd, second_ref[...], first_ref[...])
    sides = (
        ((k + margin + 0.5) / span, (margin - k - 0.5) / span, tile > 0, from_left, 0),
        (
            (span - k - 0.5) / span, (k + 0.5) / span, tile < lax.axis_size("tile") - 1, from_right,
            core - margin,
        ),
    )
    stores = []
    for side, (own_w, other_w, has_other, other, begin) in enumerate(sides):
        own_w = jnp.where(has_other, own_w, 1.0)
        other_w = jnp.where(has_other, other_w, 0.0)
        for part in range(2):
            cut = slice(part * margin, (part + 1) * margin)
            mixed[side, part] = edges_ref[part, side] * own_w + other[cut] * other_w
        store = pltpu.make_async_copy(
            mixed.at[side], out_hbm.at[:, pl.ds(begin, margin)], sems.at[side]
        )
        store.start()
        stores.append(store)
    for store in stores:
        store.wait()


def blend(core_part, edges, first, second):
    return pl.pallas_call(
        blend_kernel,
        out_shape=jax.ShapeDtypeStruct(core_part.shape, F32),
        in_specs=vmem_spec(3) + [pl.BlockSpec(memory_space=pltpu.HBM)],
        out_specs=pl.BlockSpec(memory_space=pltpu.HBM),
        input_output_aliases={3: 0},
        scratch_shapes=[pltpu.VMEM(edges.shape, F32), pltpu.SemaphoreType.DMA((2,))],
        compiler_params=pltpu.CompilerParams(vmem_limit_bytes=LIMIT),
        name="blend",
    )(first, second, edges, core_part)


def body(raw, scales, flat, spectrum, pupil, patterns, led_row, led_col):
    height, core = flat.shape
    margin = OV // 2
    width = core + OV
    tiles = lax.axis_size("tile")
    frames_here = raw.shape[0]
    band_rows, band_cols = pupil.shape[1:]
    spectrum_tile = spectrum[0]
    patterns = patterns.T

    swap_a = [(i, i ^ 1) for i in range(tiles)]
    swap_b = [(i, ((i + 1) ^ 1) - 1) for i in range(1, tiles - 1)]

    def neighbours(for_a, for_b):
        return lax.ppermute(for_a, "tile", swap_a), lax.ppermute(for_b, "tile", swap_b)

    tables = stacked_tables(height, width, band_rows, band_cols)
    passes = (low_pass(height, band_rows), low_pass(width, band_cols).T)

    by_rows = gains_by_rows(flat.T, tiles, width)
    dequantized = dequantize(raw, scales, by_rows, tiles, core, margin)
    gains = lax.all_to_all(by_rows, "tile", split_axis=0, concat_axis=0, tiled=True)
    narrow = strips(dequantized, gains, passes[1], frames_here, core, margin)
    arrived = lax.all_to_all(narrow, "tile", split_axis=0, concat_axis=0, tiled=True)
    handed = window_tables(tiles, passes, margin, core)
    field, estimate, rows, small = all_fields(
        spectrum_tile, pupil, patterns, led_row, led_col, tables, handed
    )
    window = windows(arrived, rows, small, frames_here, core)
    field, weight = fetch(field, estimate, window, patterns)

    swap_core = [(i, i ^ 1) for i in range(4)]
    swap_chip = [(i, i ^ 2) for i in range(4)]
    other = functools.partial(lax.ppermute, axis_name="grp")
    early, late = (other(part, perm=swap_chip) for part in window)
    window_1 = [other(part, perm=swap_core) for part in window]
    late, field, weight = lax.optimization_barrier((late, field, weight))
    window_3 = [other(part, perm=swap_core) for part in (early, late)]
    weight = collect(weight, (*window_1, early, late), patterns)

    fresh, high, low, for_a, for_b = update(
        field, weight, window_3, spectrum_tile, pupil, patterns,
        led_row, led_col, tables, margin,
    )
    side_a, side_b = neighbours(for_a, for_b)
    core_part, edges = object_core(high, low, margin, core)
    stitched = blend(core_part, edges, side_a, side_b)
    return fresh[None], jnp.transpose(stitched, (0, 2, 1))


def solution(mesh):
    return jax.shard_map(
        body,
        mesh=mesh,
        in_specs=(
            P("grp", "tile", None),
            P("grp", "tile", None),
            P(None, "tile"),
            P("tile", None, None, None),
            P(),
            P(),
            P(),
            P(),
        ),
        out_specs=(P("tile", None, None, None), P(None, None, "tile")),
        check_vma=False,
    )
```
